128 devices in a mesh: dp: 2 (over x_lo), tm: 16 (over z, x_hi, core), elec: 4 (over y).
Axes of the slice: x: 4 (x_hi: 2, x_lo: 2; x = x_hi * 2 + x_lo), y: 4, z: 4, core: 2. Of those that a mesh axis runs over, the one named last changes fastest.
Arguments:
- inputs: bfloat16 [2, 16, 6144, 512], P('dp', 'elec', 'tm'), may hold values from -12 to 12
- cotangent: bfloat16 [2, 16, 6144, 512], P('dp', 'elec', 'tm'), may hold values from -24 to 24
- w_query: bfloat16 [512, 512], replicated, may hold values from -0.375 to 0.375
- w_key: bfloat16 [512, 512], replicated, may hold values from -0.375 to 0.375
- w_value: bfloat16 [512, 512], replicated, may hold values from -0.25 to 0.25
- w_out: bfloat16 [512, 512], replicated, may hold values from -0.25 to 0.25
Outputs:
- grad_inputs: bfloat16 [2, 16, 6144, 512], P('dp', 'elec', 'tm')
- grad_w_query: float32 [512, 512], replicated
- grad_w_key: float32 [512, 512], replicated
- grad_w_value: float32 [512, 512], replicated
- grad_w_out: float32 [512, 512], replicated
The draws below stay inside these ranges and needn't reach their ends.
All inputs are finite; a program needn't handle non-finite values.
Results may differ from the reference program's by a relative error of at most 0.012.
The reference program's roundings to bfloat16 on the way (of `grad_attn`, `probs_low`, `attended`, `grad_scores` and `grad_q`) count: a program that leaves them out, or rounds other values in their place, can miss the bound.
Values may be sent and summed in bfloat16 or wider, within the bound.
A program may use at most 192 MiB of HBM per device.

```python
import math
import jax
import jax.numpy as jnp
from jax import lax

D = 512
HEADS = 8
WIN = 128
HEAD_DIM = 64
B = 2
E = 16
P_SIZE = 6144
TOKENS = 196608


def draw_inputs(key, part):
    key = jax.random.fold_in(key, 11)
    base_key, scale_key = jax.random.split(key, 2)
    base = jnp.clip(jax.random.normal(base_key, (B, E, P_SIZE, D), jnp.float32), -4.0, 4.0)
    row_scale = jnp.exp(jax.random.uniform(scale_key, (B, E, P_SIZE, 1), jnp.float32, math.log(0.7), math.log(1.4)))
    return (base * row_scale).astype(jnp.bfloat16)


def levels(stream_key, dims, cuts, least, high):
    gain, own = 1.0, jax.random.fold_in(stream_key, 6)
    for dim, blocks in cuts:
        steps = jnp.exp(jax.random.uniform(jax.random.fold_in(own, dim), (blocks,), jnp.float32, least / len(cuts), high / len(cuts)))
        gain = gain * jnp.repeat(steps, dims[dim] // blocks).reshape([-1 if axis == dim else 1 for axis in range(len(dims))])
    return gain


def centred(key, dims, deviation, bound, shards=(), kind=jnp.bfloat16):
    values = jax.random.normal(key, dims, jnp.float32) * deviation
    if len(shards) > 0:
        values = levels(key, dims, shards, -0.22, 0.18) * values
    return jnp.clip(values, min=-bound, max=bound).astype(kind)


def setup_inputs(seed: int = 0) -> dict:
    key_of = jax.random.split(jax.random.key(seed), 7)
    return {
        "inputs": draw_inputs(jax.random.fold_in(key_of[6], 71), 0),
        "cotangent": centred(key_of[1], (B, E, P_SIZE, D), 4.0, 24.0, ((0, 2), (1, 4), (2, 16))),
        "w_query": centred(key_of[2], (D, D), (D // 2) ** -0.5, 0.375),
        "w_key": centred(key_of[3], (D, D), (D // 2) ** -0.5, 0.375),
        "w_value": centred(key_of[4], (D, D), D ** -0.5, 0.25),
        "w_out": centred(key_of[5], (D, D), D ** -0.5, 0.25),
    }


def to_heads(tensor):
    return tensor.reshape(tensor.shape[:-1] + (HEADS // 2, HEAD_DIM))

def from_heads(tensor):
    return tensor.reshape(tensor.shape[:-2] + (tensor.shape[-2] * tensor.shape[-1],))

def spatial_block(operands):
    score_scale = 1.0 / math.sqrt(HEAD_DIM)
    query_f32 = operands[0].astype(jnp.float32)
    key_f32 = operands[1].astype(jnp.float32)
    value_f32 = operands[2].astype(jnp.float32)
    attn_f32 = operands[3].astype(jnp.float32)
    scores = jnp.einsum('bephd,bfphd->bhefp', query_f32, key_f32) * score_scale
    row_peak = lax.optimization_barrier(jnp.max(scores, axis=3, keepdims=True))
    exp_scores = jnp.exp(scores - row_peak)
    probs = exp_scores / lax.optimization_barrier(jnp.sum(exp_scores, axis=3, keepdims=True))
    probs_low = probs.astype(jnp.bfloat16).astype(jnp.float32)
    attended = jnp.einsum('bhefp,bfphd->bephd', probs_low, value_f32).astype(jnp.bfloat16)
    grad_probs = jnp.einsum('bephd,bfphd->bhefp', attn_f32, value_f32)
    row_delta = lax.optimization_barrier(jnp.sum(probs * grad_probs, axis=3, keepdims=True))
    grad_scores = (probs * (grad_probs - row_delta)).astype(jnp.bfloat16).astype(jnp.float32)
    grad_query = (jnp.einsum('bhefp,bfphd->bephd', grad_scores, key_f32) * score_scale).astype(jnp.bfloat16)
    grad_key = jnp.einsum('bhefp,bephd->bfphd', grad_scores, query_f32) * score_scale
    grad_value = jnp.einsum('bhefp,bephd->bfphd', probs_low, attn_f32)
    return (attended, grad_query, grad_key, grad_value)

def spatial_part(queries, keys, values, grad_attn):
    count = P_SIZE // WIN

    def to_blocks(tensor):
        shaped = tensor.reshape(B, E, count, WIN, HEADS // 2, HEAD_DIM)
        return jnp.moveaxis(shaped, 2, 0)

    def back(tensor):
        return jnp.moveaxis(tensor, 0, 2).reshape(B, E, P_SIZE, HEADS // 2, HEAD_DIM)
    results = lax.map(spatial_block, (to_blocks(queries), to_blocks(keys), to_blocks(values), to_blocks(grad_attn)))
    return tuple((back(result) for result in results))

def temporal_part(queries, keys, values, grad_attn):
    count = P_SIZE // WIN
    score_scale = 1.0 / math.sqrt(HEAD_DIM)
    key_pad = jnp.concatenate([jnp.zeros_like(keys[:, :, :WIN]), keys], axis=2)
    value_pad = jnp.concatenate([jnp.zeros_like(values[:, :, :WIN]), values], axis=2)

    def one_block(index):
        first = index * WIN
        query_f32 = lax.dynamic_slice_in_dim(queries, first, WIN, 2).astype(jnp.float32)
        attn_f32 = lax.dynamic_slice_in_dim(grad_attn, first, WIN, 2).astype(jnp.float32)
        key_f32 = lax.dynamic_slice_in_dim(key_pad, first, 2 * WIN, 2).astype(jnp.float32)
        value_f32 = lax.dynamic_slice_in_dim(value_pad, first, 2 * WIN, 2).astype(jnp.float32)
        query_pos = first + jnp.arange(WIN, dtype=jnp.int32)
        key_pos = first - WIN + jnp.arange(2 * WIN, dtype=jnp.int32)
        in_window = (key_pos[None, :] <= query_pos[:, None]) & (key_pos[None, :] > query_pos[:, None] - WIN) & (key_pos[None, :] >= 0)
        scores = jnp.einsum('beuhd,bethd->behut', query_f32, key_f32) * score_scale
        row_peak = lax.optimization_barrier(jnp.max(jnp.where(in_window, scores, -jnp.inf), axis=-1, keepdims=True))
        exp_scores = jnp.where(in_window, jnp.exp(scores - row_peak), 0.0)
        probs = exp_scores / lax.optimization_barrier(jnp.sum(exp_scores, axis=-1, keepdims=True))
        probs_low = probs.astype(jnp.bfloat16).astype(jnp.float32)
        attended = jnp.einsum('behut,bethd->beuhd', probs_low, value_f32).astype(jnp.bfloat16)
        grad_probs = jnp.einsum('beuhd,bethd->behut', attn_f32, value_f32)
        row_delta = lax.optimization_barrier(jnp.sum(probs * grad_probs, axis=-1, keepdims=True))
        grad_scores = (probs * (grad_probs - row_delta)).astype(jnp.bfloat16).astype(jnp.float32)
        grad_query = (jnp.einsum('behut,bethd->beuhd', grad_scores, key_f32) * score_scale).astype(jnp.bfloat16)
        grad_key = jnp.einsum('behut,beuhd->bethd', grad_scores, query_f32) * score_scale
        grad_value = jnp.einsum('behut,beuhd->bethd', probs_low, attn_f32)
        return (attended, grad_query, grad_key, grad_value)
    attended, grad_query, key_blocks, value_blocks = lax.map(one_block, jnp.arange(count, dtype=jnp.int32))

    def back(tensor):
        return jnp.moveaxis(tensor, 0, 2).reshape(B, E, P_SIZE, HEADS // 2, HEAD_DIM)

    def combine(blocks):
        earlier = blocks[:, :, :, :WIN]
        current = blocks[:, :, :, WIN:]
        shifted = jnp.concatenate([earlier[1:], jnp.zeros_like(earlier[:1])], axis=0)
        return back(current + shifted)
    return (back(attended), back(grad_query), combine(key_blocks), combine(value_blocks))

def reference(inputs, cotangent, w_query, w_key, w_value, w_out):
    cut = D // 2
    flat_inputs = inputs.reshape(-1, D)
    flat_cot = cotangent.reshape(-1, D)

    def project(weight):
        return jnp.dot(flat_inputs, weight, preferred_element_type=jnp.float32).astype(jnp.bfloat16).reshape(B, E, P_SIZE, D)
    queries = project(w_query)
    keys = project(w_key)
    values = project(w_value)
    grad_attn = jnp.dot(flat_cot, w_out.T, preferred_element_type=jnp.float32).astype(jnp.bfloat16).reshape(B, E, P_SIZE, D)
    sp_att, sp_gq, sp_gk, sp_gv = spatial_part(to_heads(queries[..., :cut]), to_heads(keys[..., :cut]), to_heads(values[..., :cut]), to_heads(grad_attn[..., :cut]))
    tm_att, tm_gq, tm_gk, tm_gv = temporal_part(to_heads(queries[..., cut:]), to_heads(keys[..., cut:]), to_heads(values[..., cut:]), to_heads(grad_attn[..., cut:]))
    attended = jnp.concatenate([from_heads(sp_att), from_heads(tm_att)], axis=-1).reshape(-1, D)
    grad_q = jnp.concatenate([from_heads(sp_gq), from_heads(tm_gq)], axis=-1).reshape(-1, D)
    grad_k = jnp.concatenate([from_heads(sp_gk), from_heads(tm_gk)], axis=-1).astype(jnp.bfloat16).reshape(-1, D)
    grad_v = jnp.concatenate([from_heads(sp_gv), from_heads(tm_gv)], axis=-1).astype(jnp.bfloat16).reshape(-1, D)
    grad_norm = 1.0 / math.sqrt(TOKENS)
    grad_w_out = jnp.dot(attended.T, flat_cot, preferred_element_type=jnp.float32) * grad_norm
    grad_w_query = jnp.dot(flat_inputs.T, grad_q, preferred_element_type=jnp.float32) * grad_norm
    grad_w_key = jnp.dot(flat_inputs.T, grad_k, preferred_element_type=jnp.float32) * grad_norm
    grad_w_value = jnp.dot(flat_inputs.T, grad_v, preferred_element_type=jnp.float32) * grad_norm
    total = jnp.dot(grad_q, w_query.T, preferred_element_type=jnp.float32)
    total = total + jnp.dot(grad_k, w_key.T, preferred_element_type=jnp.float32)
    total = total + jnp.dot(grad_v, w_value.T, preferred_element_type=jnp.float32)
    grad_inputs = total.astype(jnp.bfloat16).reshape(B, E, P_SIZE, D)
    return (grad_inputs, grad_w_query, grad_w_key, grad_w_value, grad_w_out)
```

```python
import functools
import math

import jax
import jax.numpy as jnp
from jax import lax
from jax.experimental import pallas as pl
from jax.experimental.pallas import tpu as pltpu
from jax.sharding import PartitionSpec as P

BF16 = jnp.bfloat16
F32 = jnp.float32
WIN = 128
HALF = 256
HEAD = 64
HEADS = 4
NEG = -1e30
SCALE = 0.125
VMEM_LIMIT = 56 * 1024 * 1024
MESH = pl.DeviceIdType.MESH

NN = (((1,), (0,)), ((), ()))
NT = (((1,), (1,)), ((), ()))
TN = (((0,), (0,)), ((), ()))


def mm(left, right, dims):
    return lax.dot_general(left, right, dims, preferred_element_type=F32)


def stack_heads(rows):
    head = lax.broadcasted_iota(jnp.int32, (1, HALF), 1) // HEAD
    return jnp.concatenate(
        [rows * (head == h).astype(F32).astype(BF16) for h in range(HEADS)], axis=0
    )


def pick_heads(rows):
    count = rows.shape[0] // HEADS
    head = lax.broadcasted_iota(jnp.int32, (count, HALF), 1) // HEAD
    out = rows[:count]
    for h in range(1, HEADS):
        out = jnp.where(head == h, rows[h * count : (h + 1) * count], out)
    return out


def soft(scores, grad_probs):
    peak = jnp.max(scores, axis=0, keepdims=True)
    ex = jnp.exp(scores - peak)
    probs = ex / jnp.sum(ex, axis=0, keepdims=True)
    delta = jnp.sum(probs * grad_probs, axis=0, keepdims=True)
    return probs, probs * (grad_probs - delta)


def temporal_block(q, ga, k, v, bias):
    qs, gs = stack_heads(q), stack_heads(ga)
    st = mm(k, qs, NT)
    gt = mm(v, gs, NT)
    shape = (WIN, HEADS * WIN)
    older = lax.broadcasted_iota(jnp.int32, shape, 0) > lax.rem(
        lax.broadcasted_iota(jnp.int32, shape, 1), WIN
    )
    probs, grad = soft(
        jnp.where(older, st[:WIN] + bias, st[WIN:]), jnp.where(older, gt[:WIN], gt[WIN:])
    )

    def spread(t):
        return jnp.concatenate(
            [jnp.where(older, t, 0.0).astype(BF16), jnp.where(older, 0.0, t).astype(BF16)], axis=0
        )

    pt, dt = spread(probs), spread(grad)
    att = pick_heads(mm(pt, v, TN))
    dq = pick_heads(mm(dt, k, TN)) * SCALE
    return att, dq, mm(dt, qs, NN), mm(pt, gs, NN)


def spatial_block(q, ga, k, v):
    qs, gs = stack_heads(q), stack_heads(ga)
    shape = (WIN, HEADS * WIN)
    same = lax.rem(lax.broadcasted_iota(jnp.int32, shape, 0), 8) == lax.rem(
        lax.broadcasted_iota(jnp.int32, shape, 1), 8
    )
    probs, grad = soft(jnp.where(same, mm(k, qs, NT), NEG), mm(v, gs, NT))
    pt, dt = probs.astype(BF16), grad.astype(BF16)
    att = pick_heads(mm(pt, v, TN))
    dq = pick_heads(mm(dt, k, TN)) * SCALE
    return att, dq, mm(dt, qs, NN), mm(pt, gs, NN)


def join_weights(w_refs, first, w_all):
    for i, w in enumerate(w_refs):
        w_all[:, i * HALF : (i + 1) * HALF] = w[:, first : first + HALF]


def temporal_kernel(
    x, halo, cot, wq, wk, wv, wo, att_o, dq_o, dk_o, dv_o, back_o, w_all, q_s, k_s, v_s, g_s, dk_s, dv_s
):
    elecs, patches, width = x.shape
    join_weights((wq, wk, wv), HALF, w_all)
    bias0 = jnp.where(lax.axis_index("tm") == 0, NEG, 0.0).astype(F32)

    def electrode(e, carry):
        xe = x[e]
        q_s[...] = (mm(xe, w_all[:, :HALF], NN) * SCALE).astype(BF16)
        ext = jnp.concatenate([halo[e], xe], axis=0)
        k_s[...] = mm(ext, w_all[:, HALF : 2 * HALF], NN).astype(BF16)
        v_s[...] = mm(ext, w_all[:, 2 * HALF :], NN).astype(BF16)
        g_s[...] = mm(cot[e], wo[HALF:, :], NT).astype(BF16)
        dk_s[...] = jnp.zeros_like(dk_s)
        dv_s[...] = jnp.zeros_like(dv_s)
        for c in range(patches // WIN):
            rows = slice(c * WIN, (c + 1) * WIN)
            keys = slice(c * WIN, (c + 2) * WIN)
            att, dq, dk, dv = temporal_block(
                q_s[rows], g_s[rows], k_s[keys], v_s[keys], bias0 if c == 0 else 0.0
            )
            att_o[e, rows] = att.astype(BF16)
            dq_o[e, rows] = dq.astype(BF16)
            dk_s[keys] += dk
            dv_s[keys] += dv
        back_o[0, e] = dk_s[:WIN].astype(BF16)
        back_o[1, e] = dv_s[:WIN].astype(BF16)
        dk_o[e] = dk_s[WIN:]
        dv_o[e] = dv_s[WIN:]
        return carry

    lax.fori_loop(0, elecs, electrode, 0)


def weight_rows(acc_in, acc_out, w_o):
    for i in range(3):
        w_o[i * 512 : (i + 1) * 512] = acc_in[:, i * HALF : (i + 1) * HALF].astype(BF16)
    w_o[1536:1792] = acc_out[:, :HALF].astype(BF16)
    w_o[1792:2048] = acc_out[:, HALF:].astype(BF16)


def temporal_end_kernel(
    x, cot, att, dq, dk, dv, back, wq, wk, wv, dx_o, w_o, w_all, acc_in, acc_out
):
    elecs, patches, width = x.shape
    join_weights((wq, wk, wv), HALF, w_all)
    acc_in[...] = jnp.zeros_like(acc_in)
    acc_out[...] = jnp.zeros_like(acc_out)

    def electrode(e, carry):
        def full(own, side):
            tail = own[e, patches - WIN :] + back[side, e].astype(F32)
            return jnp.concatenate(
                [own[e, : patches - WIN].astype(BF16), tail.astype(BF16)], axis=0
            )

        grads = jnp.concatenate([dq[e], full(dk, 0), full(dv, 1)], axis=1)
        dx_o[e] = mm(grads, w_all[...], NT)
        acc_in[...] += mm(x[e], grads, TN)
        acc_out[...] += mm(att[e], cot[e], TN)
        return carry

    lax.fori_loop(0, elecs, electrode, 0)
    weight_rows(acc_in, acc_out, w_o)


def spatial_kernel(*refs):
    xs, cots = refs[0:4], refs[4:8]
    wq, wk, wv, wo = refs[8:12]
    dxs, w_o = refs[12:16], refs[16]
    w_all, q_s, k_s, v_s, g_s, acc_in, acc_out = refs[17:]
    elecs, patches, width = xs[0].shape
    rows = elecs * patches
    join_weights((wq, wk, wv), 0, w_all)

    def split(t):
        return t.reshape(elecs, patches, HALF)

    for i in range(4):
        part = slice(i * elecs, (i + 1) * elecs)
        xi = xs[i][...].reshape(rows, width)
        q_s[part] = split(mm(xi, w_all[:, :HALF], NN) * SCALE)
        k_s[part] = split(mm(xi, w_all[:, HALF : 2 * HALF], NN))
        v_s[part] = split(mm(xi, w_all[:, 2 * HALF :], NN))
        g_s[part] = split(mm(cots[i][...].reshape(rows, width), wo[:HALF, :], NT))

    def block(g, carry):
        at = pl.ds(pl.multiple_of(g * 8, 8), 8)

        def load(ref):
            return ref[:, at, :].reshape(WIN, HALF).astype(BF16)

        def store(ref, value):
            ref[:, at, :] = value.reshape(4 * elecs, 8, HALF)

        att, dq, dk, dv = spatial_block(load(q_s), load(g_s), load(k_s), load(v_s))
        store(g_s, att)
        store(q_s, dq)
        store(k_s, dk)
        store(v_s, dv)
        return carry

    lax.fori_loop(0, patches // 8, block, 0)

    for i in range(4):
        part = slice(i * elecs, (i + 1) * elecs)
        xi = xs[i][...].reshape(rows, width)
        grads = jnp.concatenate(
            [ref[part].astype(BF16).reshape(rows, HALF) for ref in (q_s, k_s, v_s)], axis=1
        )
        dxs[i][...] = mm(grads, w_all[...], NT).astype(BF16).reshape(elecs, patches, width)
        add_in = mm(xi, grads, TN)
        add_out = mm(
            g_s[part].astype(BF16).reshape(rows, HALF), cots[i][...].reshape(rows, width), TN
        )
        if i == 0:
            acc_in[...] = add_in
            acc_out[...] = add_out
        else:
            acc_in[...] += add_in
            acc_out[...] += add_out
    weight_rows(acc_in, acc_out, w_o)


def final_kernel(dx, p0, p1, p2, p3, out):
    me = lax.axis_index("elec")
    patches = p0.shape[1]
    for d, piece in enumerate((p0, p1, p2, p3)):
        at = pl.ds(pl.multiple_of(lax.rem(me + d, 4) * patches, 16), patches)
        out[:, at, :] = (dx[:, at, :] + piece[...].astype(F32)).astype(BF16)


def coordinates():
    dp, tm, y = lax.axis_index("dp"), lax.axis_index("tm"), lax.axis_index("elec")
    z, rest = lax.div(tm, 4), lax.rem(tm, 4)
    x = lax.div(rest, 2) * 2 + dp
    return x, y, z, lax.rem(rest, 2)


def device_at(x, y, z, core):
    return {"dp": lax.rem(x, 2), "tm": z * 4 + lax.div(x, 2) * 2 + core, "elec": y}


def sum_kernel(wt, ws, out, recv_c, part_c, recv_a, part_a, recv_b, part_b, recv_e, send_sem, recv_sem):
    x, y, z, core = coordinates()
    other_core = device_at(x, y, z, 1 - core)

    def peer(axis, d):
        if axis == "x":
            return device_at(lax.rem(x + d, 4), y, z, core)
        if axis == "y":
            return device_at(x, lax.rem(y + d, 4), z, core)
        return device_at(x, y, lax.rem(z + d, 4), core)

    where = {"x": x, "y": y, "z": z}
    barrier = pltpu.get_barrier_semaphore()
    pl.semaphore_signal(barrier, inc=1, device_id=other_core, device_id_type=MESH)
    for axis in "xyz":
        for d in range(1, 4):
            pl.semaphore_signal(barrier, inc=1, device_id=peer(axis, d), device_id_type=MESH)
    pl.semaphore_wait(barrier, 10)

    orders = ("xzy", "zxy")
    sources = (wt, ws)
    started = []

    def start(p, n, src, dst, device):
        copy = pltpu.make_async_remote_copy(
            src_ref=src,
            dst_ref=dst,
            send_sem=send_sem.at[p, n],
            recv_sem=recv_sem.at[p, n],
            device_id=device,
            device_id_type=MESH,
        )
        copy.start()
        started.append(copy)
        return copy

    def block(first, size):
        return pl.ds(pl.multiple_of(first, 16), size)

    waiting = []
    for p in range(2):
        waiting.append([start(p, 0, sources[p].at[block((1 - core) * 1024, 1024)], recv_c.at[p], other_core)])
    base = [core * 1024, core * 1024]
    source, size = None, 1024
    stages = ((recv_a, part_c), (recv_b, part_a), (recv_e, part_b))
    for stage in range(3):
        size = size // 4
        landing, held = stages[stage]
        for p in range(2):
            for copy in waiting[p]:
                copy.wait_recv()
            if stage == 0:
                total = sources[p][block(core * 1024, 1024)].astype(F32) + recv_c[p].astype(F32)
            else:
                arrived, before = stages[stage - 1]
                spot = where[orders[p][stage - 1]]
                total = before[p, block(spot * size * 4, size * 4)].astype(F32)
                for d in range(3):
                    total = total + arrived[p, d].astype(F32)
            held[p] = total.astype(BF16)
            axis = orders[p][stage]
            waiting[p] = []
            for d in range(1, 4):
                to = lax.rem(where[axis] + d, 4)
                waiting[p].append(
                    start(
                        p,
                        1 + stage * 3 + d - 1,
                        held.at[p, block(to * size, size)],
                        landing.at[p, d - 1],
                        peer(axis, d),
                    )
                )
            base[p] = base[p] + where[axis] * size
    for p in range(2):
        for copy in waiting[p]:
            copy.wait_recv()
        total = part_b[p, block(where["y"] * 16, 16)].astype(F32)
        for d in range(3):
            total = total + recv_e[p, d].astype(F32)
        out[p, block(base[p], 16)] = total.astype(BF16)
        waiting[p] = []
    for stage in (2, 1, 0):
        for p in range(2):
            for copy in waiting[p]:
                copy.wait_recv()
            axis = orders[p][stage]
            rows = block(base[p], size)
            waiting[p] = [
                start(p, 10 + stage * 3 + d - 1, out.at[p, rows], out.at[p, rows], peer(axis, d))
                for d in range(1, 4)
            ]
            base[p] = base[p] - where[axis] * size
        size = size * 4
    for p in range(2):
        for copy in waiting[p]:
            copy.wait_recv()
        rows = block(core * 1024, 1024)
        waiting[p] = [start(p, 19, out.at[p, rows], out.at[p, rows], other_core)]
    for p in range(2):
        for copy in waiting[p]:
            copy.wait_recv()
    for copy in started:
        copy.wait_send()


def call(kernel, outs, scratch, flops, **more):
    params = {"vmem_limit_bytes": VMEM_LIMIT, **more}

    def run(*args):
        return pl.pallas_call(
            kernel,
            out_shape=outs,
            in_specs=[pl.BlockSpec(memory_space=pltpu.VMEM)] * len(args),
            out_specs=jax.tree.map(lambda _: pl.BlockSpec(memory_space=pltpu.VMEM), outs),
            scratch_shapes=scratch,
            compiler_params=pltpu.CompilerParams(**params),
            cost_estimate=pl.CostEstimate(
                flops=flops, bytes_accessed=8 * 1024 * 1024, transcendentals=1024 * 1024
            ),
        )(*args)

    return run


def sds(shape, dtype):
    return jax.ShapeDtypeStruct(shape, dtype)


def rotate(block, axis, distance):
    count = lax.axis_size(axis)
    return lax.ppermute(block, axis, [(i, (i + distance) % count) for i in range(count)])


def shifted(block, axis, distance):
    devices = range(lax.axis_size(axis))
    return lax.ppermute(
        block, axis, [(i - distance, i) for i in devices if i - distance in devices]
    )


def shards(inputs, cotangent, w_query, w_key, w_value, w_out):
    _, elecs, patches, width = inputs.shape
    x, cot = inputs[0], cotangent[0]
    quarter = patches // 4
    me = lax.axis_index("elec")
    halo = shifted(x[:, patches - WIN :], "tm", 1)

    def piece(t, d):
        return lax.dynamic_slice_in_dim(t, lax.rem(me + d, 4) * quarter, quarter, 1)

    xs = [piece(x, 0)] + [rotate(piece(x, d), "elec", d) for d in (2, 1, 3)]
    cots = [piece(cot, 0)] + [rotate(piece(cot, d), "elec", d) for d in (2, 1, 3)]

    vm = pltpu.VMEM
    att, dq, dk, dv, back = call(
        temporal_kernel,
        (
            sds((elecs, patches, HALF), BF16),
            sds((elecs, patches, HALF), BF16),
            sds((elecs, patches, HALF), F32),
            sds((elecs, patches, HALF), F32),
            sds((2, elecs, WIN, HALF), BF16),
        ),
        [
            vm((width, 3 * HALF), BF16),
            vm((patches, HALF), BF16),
            vm((patches + WIN, HALF), BF16),
            vm((patches + WIN, HALF), BF16),
            vm((patches, HALF), BF16),
            vm((patches + WIN, HALF), F32),
            vm((patches + WIN, HALF), F32),
        ],
        10**10,
    )(x, halo, cot, w_query, w_key, w_value, w_out)
    back = shifted(back, "tm", -1)
    dx_time, wt = call(
        temporal_end_kernel,
        (sds((elecs, patches, width), F32), sds((2048, HALF), BF16)),
        [vm((width, 3 * HALF), BF16), vm((width, 3 * HALF), F32), vm((HALF, width), F32)],
        5 * 10**9,
    )(x, cot, att, dq, dk, dv, back, w_query, w_key, w_value)
    *dxs, ws = call(
        spatial_kernel,
        tuple([sds((elecs, quarter, width), BF16)] * 4) + (sds((2048, HALF), BF16),),
        [vm((width, 3 * HALF), BF16)]
        + [vm((4 * elecs, quarter, HALF), F32)] * 4
        + [vm((width, 3 * HALF), F32), vm((HALF, width), F32)],
        10**10,
    )(*xs, *cots, w_query, w_key, w_value, w_out)
    by_back = {0: dxs[0], 2: dxs[1], 1: dxs[2], 3: dxs[3]}
    pieces = [by_back[0]] + [rotate(by_back[d], "elec", -d) for d in (1, 2, 3)]
    grad_inputs = call(final_kernel, sds((elecs, patches, width), BF16), [], 10**7)(
        dx_time, *pieces
    )
    dma = pltpu.SemaphoreType.DMA
    sums = call(
        sum_kernel,
        sds((2, 2048, HALF), BF16),
        [
            vm((2, 1024, HALF), BF16),
            vm((2, 1024, HALF), BF16),
            vm((2, 3, 256, HALF), BF16),
            vm((2, 256, HALF), BF16),
            vm((2, 3, 64, HALF), BF16),
            vm((2, 64, HALF), BF16),
            vm((2, 3, 16, HALF), BF16),
            dma((2, 20)),
            dma((2, 20)),
        ],
        10**9,
        collective_id=0,
        has_side_effects=True,
    )(wt, ws)
    sums = sums.astype(F32) * (1.0 / math.sqrt(196608))
    time, space = sums[0], sums[1]
    grads = [
        jnp.concatenate([space[i : i + 512], time[i : i + 512]], axis=1) for i in (0, 512, 1024)
    ]
    grad_out = jnp.concatenate(
        [jnp.concatenate([t[1536:1792], t[1792:2048]], axis=1) for t in (space, time)], axis=0
    )
    return (grad_inputs[None], grads[0], grads[1], grads[2], grad_out)


def solution(mesh):
    return jax.shard_map(
        shards,
        mesh=mesh,
        in_specs=(P("dp", "elec", "tm", None), P("dp", "elec", "tm", None), P(), P(), P(), P()),
        out_specs=(P("dp", "elec", "tm", None), P(), P(), P(), P()),
        check_vma=False,
    )
```

```python
import math

import jax
import jax.numpy as jnp
from jax import lax
from jax.experimental import pallas as pl
from jax.experimental.pallas import tpu as pltpu
from jax.sharding import PartitionSpec as P

BF16 = jnp.bfloat16
F32 = jnp.float32
WIN = 128
HALF = 256
HEAD = 64
HEADS = 4
NEG = -1e30
SCALE = 0.125
VMEM_LIMIT = 56 * 1024 * 1024
MESH = pl.DeviceIdType.MESH

NN = (((1,), (0,)), ((), ()))
NT = (((1,), (1,)), ((), ()))
TN = (((0,), (0,)), ((), ()))


def mm(left, right, dims):
    return lax.dot_general(left, right, dims, preferred_element_type=F32)


def stack_heads(rows):
    head = lax.broadcasted_iota(jnp.int32, (1, HALF), 1) // HEAD
    return jnp.concatenate(
        [rows * (head == h).astype(F32).astype(BF16) for h in range(HEADS)], axis=0
    )


def pick_heads(rows):
    count = rows.shape[0] // HEADS
    head = lax.broadcasted_iota(jnp.int32, (count, HALF), 1) // HEAD
    out = rows[:count]
    for h in range(1, HEADS):
        out = jnp.where(head == h, rows[h * count : (h + 1) * count], out)
    return out


def soft(scores, grad_probs):
    peak = jnp.max(scores, axis=0, keepdims=True)
    ex = jnp.exp(scores - peak)
    probs = ex / jnp.sum(ex, axis=0, keepdims=True)
    delta = jnp.sum(probs * grad_probs, axis=0, keepdims=True)
    return probs, probs * (grad_probs - delta)


def temporal_block(q, ga, k, v, bias):
    qs, gs = stack_heads(q), stack_heads(ga)
    st = mm(k, qs, NT)
    gt = mm(v, gs, NT)
    shape = (WIN, HEADS * WIN)
    older = lax.broadcasted_iota(jnp.int32, shape, 0) > lax.rem(
        lax.broadcasted_iota(jnp.int32, shape, 1), WIN
    )
    probs, grad = soft(
        jnp.where(older, st[:WIN] + bias, st[WIN:]), jnp.where(older, gt[:WIN], gt[WIN:])
    )

    def spread(t):
        return jnp.concatenate(
            [jnp.where(older, t, 0.0).astype(BF16), jnp.where(older, 0.0, t).astype(BF16)], axis=0
        )

    pt, dt = spread(probs), spread(grad)
    att = pick_heads(mm(pt, v, TN))
    dq = pick_heads(mm(dt, k, TN)) * SCALE
    return att, dq, mm(dt, qs, NN), mm(pt, gs, NN)


def spatial_block(q, ga, k, v):
    qs, gs = stack_heads(q), stack_heads(ga)
    shape = (WIN, HEADS * WIN)
    same = lax.rem(lax.broadcasted_iota(jnp.int32, shape, 0), 8) == lax.rem(
        lax.broadcasted_iota(jnp.int32, shape, 1), 8
    )
    probs, grad = soft(jnp.where(same, mm(k, qs, NT), NEG), mm(v, gs, NT))
    pt, dt = probs.astype(BF16), grad.astype(BF16)
    att = pick_heads(mm(pt, v, TN))
    dq = pick_heads(mm(dt, k, TN)) * SCALE
    return att, dq, mm(dt, qs, NN), mm(pt, gs, NN)


def coordinates():
    dp, tm, y = lax.axis_index("dp"), lax.axis_index("tm"), lax.axis_index("elec")
    z, rest = lax.div(tm, 4), lax.rem(tm, 4)
    x = lax.div(rest, 2) * 2 + dp
    return x, y, z, lax.rem(rest, 2)


def device_at(x, y, z, core):
    return {"dp": lax.rem(x, 2), "tm": z * 4 + lax.div(x, 2) * 2 + core, "elec": y}


CHUNKS = 3
STEPS = 20


def weight_rows(acc_in, acc_out, dst):
    for j in range(2):
        for i in range(3):
            first = i * HALF + j * 128
            dst[j, i * 512 : (i + 1) * 512] = acc_in[:, first : first + 128].astype(BF16)
        for i in range(2):
            first = i * HALF + j * 128
            dst[j, 1536 + i * HALF : 1536 + (i + 1) * HALF] = acc_out[:, first : first + 128].astype(BF16)


def layer_kernel(x_h, cot_h, wq_h, wk_h, wv_h, wo_h, out, *rest):
    w_outs = rest[:4]
    (
        xv, cv, halo, w_t, w_s, wo, q_t, k_t, v_t, g_t, dk_t, dv_t, att_t, dq_t, back_out, back_in, dx_t,
        xr, cr, q_s, k_s, v_s, g_s, dxs, dxr, acc_in_t, acc_out_t, acc_in_s, acc_out_s,
        ar_src, recv_c, part_c, recv_a, part_a, recv_b, part_b, recv_e, ar_out,
        load_sem, halo_send, halo_recv, go_send, go_recv, ret_send, ret_recv, ar_send, ar_recv,
    ) = rest[4:]
    elecs, patches, width = xv.shape
    quarter = patches // 4
    chunk = quarter // CHUNKS
    x, y, z, core = coordinates()
    tm = lax.axis_index("tm")
    right = {"tm": lax.rem(tm + 1, 16)}
    left = {"tm": lax.rem(tm + 15, 16)}
    other_core = device_at(x, y, z, 1 - core)
    where = {"x": x, "y": y, "z": z}

    def peer(axis, d):
        if axis == "x":
            return device_at(lax.rem(x + d, 4), y, z, core)
        if axis == "y":
            return {"elec": lax.rem(y + d, 4)}
        return device_at(x, y, lax.rem(z + d, 4), core)

    barrier = pltpu.get_barrier_semaphore()
    for device in [right, left, other_core] + [peer(axis, d) for axis in "xyz" for d in range(1, 4)]:
        pl.semaphore_signal(barrier, inc=1, device_id=device, device_id_type=MESH)
    pl.semaphore_wait(barrier, 12)

    sent = []

    def send(src, dst, send_sem, recv_sem, device):
        copy = pltpu.make_async_remote_copy(
            src_ref=src, dst_ref=dst, send_sem=send_sem, recv_sem=recv_sem, device_id=device, device_id_type=MESH
        )
        copy.start()
        sent.append(copy)
        return copy

    def rows_at(first, size):
        return pl.ds(pl.multiple_of(first, 16), size)

    halo_copy = send(x_h.at[:, patches - WIN :], halo, halo_send.at[0], halo_recv.at[0], right)
    loads = []

    def load(src, dst):
        copy = pltpu.make_async_copy(src, dst, load_sem.at[len(loads)])
        copy.start()
        loads.append(copy)

    load(x_h, xv)
    load(cot_h, cv)
    load(wo_h, wo)
    for i, w in enumerate((wq_h, wk_h, wv_h)):
        load(w.at[:, HALF:], w_t.at[:, i * HALF : (i + 1) * HALF])
    go = {}
    for c in range(CHUNKS):
        for d in (2, 1, 3):
            at = rows_at(lax.rem(y + d, 4) * quarter + c * chunk, chunk)
            slot = slice(d * elecs, (d + 1) * elecs)
            go[c, d] = [
                send(src.at[:, at], dst.at[c, slot], go_send.at[c, d - 1, k], go_recv.at[c, d - 1, k], peer("y", d))
                for k, (src, dst) in enumerate(((x_h, xr), (cot_h, cr)))
            ]
    for i, w in enumerate((wq_h, wk_h, wv_h)):
        load(w.at[:, :HALF], w_s.at[:, i * HALF : (i + 1) * HALF])
    for c in range(CHUNKS):
        at = rows_at(y * quarter + c * chunk, chunk)
        load(x_h.at[:, at], xr.at[c, :elecs])
        load(cot_h.at[:, at], cr.at[c, :elecs])
    for copy in loads:
        copy.wait()

    bias0 = jnp.where(tm == 0, NEG, 0.0).astype(F32)

    def project_time(e, carry):
        q_t[e] = (mm(xv[e], w_t[:, :HALF], NN) * SCALE).astype(BF16)
        k_t[e, WIN:] = mm(xv[e], w_t[:, HALF : 2 * HALF], NN).astype(BF16)
        v_t[e, WIN:] = mm(xv[e], w_t[:, 2 * HALF :], NN).astype(BF16)
        g_t[e] = mm(cv[e], wo[HALF:, :], NT).astype(BF16)
        return carry

    lax.fori_loop(0, elecs, project_time, 0)

    def time_block(e, c, bias):
        rows, keys = slice(c * WIN, (c + 1) * WIN), slice(c * WIN, (c + 2) * WIN)
        att, dq, dk, dv = temporal_block(q_t[e, rows], g_t[e, rows], k_t[e, keys], v_t[e, keys], bias)
        att_t[e, rows] = att.astype(BF16)
        dq_t[e, rows] = dq.astype(BF16)
        return dk, dv

    def later_blocks(e, carry):
        ones = time_block(e, 1, 0.0)
        twos = time_block(e, 2, 0.0)
        for ref, one, two in zip((dk_t, dv_t), ones, twos):
            ref[e, :WIN] = one[:WIN]
            ref[e, WIN : 2 * WIN] = one[WIN:] + two[:WIN]
            ref[e, 2 * WIN :] = two[WIN:]
        return carry

    lax.fori_loop(0, elecs, later_blocks, 0)
    halo_copy.wait_recv()

    def first_blocks(i, carry):
        for e in (2 * i, 2 * i + 1):
            k_t[e, :WIN] = mm(halo[e], w_t[:, HALF : 2 * HALF], NN).astype(BF16)
            v_t[e, :WIN] = mm(halo[e], w_t[:, 2 * HALF :], NN).astype(BF16)
            for side, (ref, grad) in enumerate(zip((dk_t, dv_t), time_block(e, 0, bias0))):
                back_out[side, e] = grad[:WIN].astype(BF16)
                ref[e, :WIN] += grad[WIN:]
        return carry

    lax.fori_loop(0, elecs // 2, first_blocks, 0)
    back_copy = send(back_out, back_in, halo_send.at[1], halo_recv.at[1], left)

    rows = 4 * elecs * chunk

    def spatial_project(c):
        for d in range(1, 4):
            for copy in go[c, d]:
                copy.wait_recv()
        xi = xr[c].reshape(rows, width)
        shape = (4 * elecs, chunk, HALF)
        q_s[...] = (mm(xi, w_s[:, :HALF], NN) * SCALE).reshape(shape)
        k_s[...] = mm(xi, w_s[:, HALF : 2 * HALF], NN).reshape(shape)
        v_s[...] = mm(xi, w_s[:, 2 * HALF :], NN).reshape(shape)
        g_s[...] = mm(cr[c].reshape(rows, width), wo[:HALF, :], NT).reshape(shape)

    def spatial_attend():
        def block(i, carry):
            for j in range(2):
                at = pl.ds(pl.multiple_of(i * 16 + j * 8, 8), 8)
                q, g, k, v = [ref[:, at, :].reshape(WIN, HALF).astype(BF16) for ref in (q_s, g_s, k_s, v_s)]
                for ref, value in zip((g_s, q_s, k_s, v_s), spatial_block(q, g, k, v)):
                    ref[:, at, :] = value.reshape(4 * elecs, 8, HALF)
            return carry

        lax.fori_loop(0, chunk // 16, block, 0)

    def spatial_end(c):
        xi = xr[c].reshape(rows, width)
        grads = jnp.concatenate([ref[...].astype(BF16).reshape(rows, HALF) for ref in (q_s, k_s, v_s)], axis=1)
        dxs[c] = mm(grads, w_s[...], NT).astype(BF16).reshape(4 * elecs, chunk, width)
        add_in = mm(xi, grads, TN)
        add_out = mm(g_s[...].astype(BF16).reshape(rows, HALF), cr[c].reshape(rows, width), TN)
        if c == 0:
            acc_in_s[...] = add_in
            acc_out_s[...] = add_out
        else:
            acc_in_s[...] += add_in
            acc_out_s[...] += add_out

    returned = {}

    def send_back(c):
        for d in (2, 1, 3):
            slot = slice(d * elecs, (d + 1) * elecs)
            returned[c, d] = send(
                dxs.at[c, slot], dxr.at[c, d - 1], ret_send.at[c, d - 1], ret_recv.at[c, d - 1], peer("y", 4 - d)
            )

    def place(c):
        for d in range(4):
            at = rows_at(lax.rem(y + d, 4) * quarter + c * chunk, chunk)
            if d == 0:
                piece = dxs[c, :elecs]
            else:
                returned[c, d].wait_recv()
                piece = dxr[c, d - 1]
            out[:, at, :] = (dx_t[:, at, :] + piece.astype(F32)).astype(BF16)

    def summing(n):
        orders = ("xzy", "zxy")

        def start(p, step, src, dst, device):
            return send(src, dst, ar_send.at[n, p, step], ar_recv.at[n, p, step], device)

        src = ar_src.at[n]
        waiting = [
            [start(p, 0, src.at[p, rows_at((1 - core) * 1024, 1024)], recv_c.at[n, p], other_core)] for p in range(2)
        ]
        yield
        base = [core * 1024, core * 1024]
        size = 1024
        stages = ((recv_a, part_c), (recv_b, part_a), (recv_e, part_b))
        for stage in range(3):
            size = size // 4
            landing, held = stages[stage]
            for p in range(2):
                for copy in waiting[p]:
                    copy.wait_recv()
                if stage == 0:
                    total = src[p, rows_at(core * 1024, 1024)].astype(F32) + recv_c[n, p].astype(F32)
                else:
                    arrived, before = stages[stage - 1]
                    spot = where[orders[p][stage - 1]]
                    total = before[n, p, rows_at(spot * size * 4, size * 4)].astype(F32)
                    for d in range(3):
                        total = total + arrived[n, p, d].astype(F32)
                held[n, p] = total.astype(BF16)
                axis = orders[p][stage]
                waiting[p] = [
                    start(
                        p,
                        stage * 3 + d,
                        held.at[n, p, rows_at(lax.rem(where[axis] + d, 4) * size, size)],
                        landing.at[n, p, d - 1],
                        peer(axis, d),
                    )
                    for d in range(1, 4)
                ]
                base[p] = base[p] + where[axis] * size
            yield
        for stage in (2, 1, 0):
            for p in range(2):
                for copy in waiting[p]:
                    copy.wait_recv()
                if stage == 2:
                    total = part_b[n, p, rows_at(where["y"] * 16, 16)].astype(F32)
                    for d in range(3):
                        total = total + recv_e[n, p, d].astype(F32)
                    ar_out[n, p, rows_at(base[p], 16)] = total.astype(BF16)
                axis = orders[p][stage]
                spot = ar_out.at[n, p, rows_at(base[p], size)]
                waiting[p] = [start(p, 9 + stage * 3 + d, spot, spot, peer(axis, d)) for d in range(1, 4)]
                base[p] = base[p] - where[axis] * size
            size = size * 4
            yield
        for p in range(2):
            for copy in waiting[p]:
                copy.wait_recv()
            spot = ar_out.at[n, p, rows_at(core * 1024, 1024)]
            waiting[p] = [start(p, 19, spot, spot, other_core)]
        yield
        for p in range(2):
            for copy in waiting[p]:
                copy.wait_recv()
            first = (1 - n) * HALF + p * 128
            for i in range(3):
                w_outs[i][:, first : first + 128] = ar_out[n, p, i * 512 : (i + 1) * 512]
            for i in range(2):
                low, left_col = (1 - n) * HALF, i * HALF + p * 128
                w_outs[3][low : low + HALF, left_col : left_col + 128] = ar_out[
                    n, p, 1536 + i * HALF : 1536 + (i + 1) * HALF
                ]
        yield

    spatial_project(0)
    spatial_attend()
    spatial_end(0)

    back_copy.wait_recv()
    acc_in_t[...] = jnp.zeros_like(acc_in_t)
    acc_out_t[...] = jnp.zeros_like(acc_out_t)

    def end_time(e, carry):
        def full(own, side):
            tail = own[e, patches - WIN :] + back_in[side, e].astype(F32)
            return jnp.concatenate([own[e, : patches - WIN].astype(BF16), tail.astype(BF16)], axis=0)

        grads = jnp.concatenate([dq_t[e], full(dk_t, 0), full(dv_t, 1)], axis=1)
        dx_t[e] = mm(grads, w_t[...], NT)
        acc_in_t[...] += mm(xv[e], grads, TN)
        acc_out_t[...] += mm(att_t[e], cv[e], TN)
        return carry

    lax.fori_loop(0, elecs, end_time, 0)
    weight_rows(acc_in_t, acc_out_t, ar_src.at[0])
    time_sum, space_sum = summing(0), summing(1)
    next(time_sum)
    spatial_project(1)
    next(time_sum)
    spatial_attend()
    next(time_sum)
    spatial_end(1)
    next(time_sum)
    spatial_project(2)
    send_back(0)
    send_back(1)
    next(time_sum)
    spatial_attend()
    next(time_sum)
    spatial_end(2)
    weight_rows(acc_in_s, acc_out_s, ar_src.at[1])
    next(space_sum)
    send_back(2)
    next(time_sum)
    next(space_sum)
    next(time_sum)
    next(space_sum)
    place(0)
    next(time_sum)
    next(space_sum)
    place(1)
    next(space_sum)
    place(2)
    for _ in space_sum:
        pass
    for copy in sent:
        copy.wait_send()


def sds(shape, dtype):
    return jax.ShapeDtypeStruct(shape, dtype)


def shards(inputs, cotangent, w_query, w_key, w_value, w_out):
    _, elecs, patches, width = inputs.shape
    chunk = patches // 4 // CHUNKS
    vm, dma = pltpu.VMEM, pltpu.SemaphoreType.DMA
    tokens = (elecs, patches)
    ext = (elecs, patches + WIN)
    everyone = (4 * elecs, chunk)
    scratch = (
        [vm(tokens + (width,), BF16)] * 2
        + [vm((elecs, WIN, width), BF16)]
        + [vm((width, 3 * HALF), BF16)] * 2
        + [vm((width, width), BF16)]
        + [vm(tokens + (HALF,), BF16), vm(ext + (HALF,), BF16), vm(ext + (HALF,), BF16), vm(tokens + (HALF,), BF16)]
        + [vm(tokens + (HALF,), F32)] * 2
        + [vm(tokens + (HALF,), BF16)] * 2
        + [vm((2, elecs, WIN, HALF), BF16)] * 2
        + [vm(tokens + (width,), F32)]
        + [vm((CHUNKS,) + everyone + (width,), BF16)] * 2
        + [vm(everyone + (HALF,), F32)] * 4
        + [vm((CHUNKS,) + everyone + (width,), BF16), vm((CHUNKS, 3, elecs, chunk, width), BF16)]
        + [vm((width, 3 * HALF), F32), vm((HALF, width), F32)] * 2
        + [vm((2, 2, 2048, 128), BF16)]
        + [vm((2, 2, 1024, 128), BF16)] * 2
        + [vm((2, 2, 3, 256, 128), BF16), vm((2, 2, 256, 128), BF16)]
        + [vm((2, 2, 3, 64, 128), BF16), vm((2, 2, 64, 128), BF16)]
        + [vm((2, 2, 3, 16, 128), BF16)]
        + [vm((2, 2, 2048, 128), BF16)]
        + [dma((6 + 3 + 2 * CHUNKS,)), dma((2,)), dma((2,))]
        + [dma((CHUNKS, 3, 2))] * 2
        + [dma((CHUNKS, 3))] * 2
        + [dma((2, 2, STEPS))] * 2
    )
    grad_inputs, *grads = pl.pallas_call(
        layer_kernel,
        out_shape=(sds(tokens + (width,), BF16),) + (sds((width, width), BF16),) * 4,
        in_specs=[pl.BlockSpec(memory_space=pl.ANY)] * 6,
        out_specs=(pl.BlockSpec(memory_space=pltpu.VMEM),) * 5,
        scratch_shapes=scratch,
        compiler_params=pltpu.CompilerParams(
            collective_id=0, has_side_effects=True, vmem_limit_bytes=VMEM_LIMIT
        ),
        cost_estimate=pl.CostEstimate(flops=2 * 10**10, bytes_accessed=10**7, transcendentals=2 * 10**6),
    )(inputs[0], cotangent[0], w_query, w_key, w_value, w_out)
    norm = 1.0 / math.sqrt(196608)
    return (grad_inputs[None],) + tuple(grad.astype(F32) * norm for grad in grads)


def solution(mesh):
    return jax.shard_map(
        shards,
        mesh=mesh,
        in_specs=(P("dp", "elec", "tm", None), P("dp", "elec", "tm", None), P(), P(), P(), P()),
        out_specs=(P("dp", "elec", "tm", None), P(), P(), P(), P()),
        check_vma=False,
    )
```

```python
import math

import jax
import jax.numpy as jnp
from jax import lax
from jax.experimental import pallas as pl
from jax.experimental.pallas import tpu as pltpu
from jax.sharding import PartitionSpec as P

BF16 = jnp.bfloat16
F32 = jnp.float32
WIN = 128
HALF = 256
HEAD = 64
HEADS = 4
NEG = -1e30
SCALE = 0.125
VMEM_LIMIT = 56 * 1024 * 1024
MESH = pl.DeviceIdType.MESH

NN = (((1,), (0,)), ((), ()))
NT = (((1,), (1,)), ((), ()))
TN = (((0,), (0,)), ((), ()))


def mm(left, right, dims):
    return lax.dot_general(left, right, dims, preferred_element_type=F32)


def stack_heads(rows):
    head = lax.broadcasted_iota(jnp.int32, (1, HALF), 1) // HEAD
    return jnp.concatenate(
        [rows * (head == h).astype(F32).astype(BF16) for h in range(HEADS)], axis=0
    )


def pick_heads(rows):
    count = rows.shape[0] // HEADS
    head = lax.broadcasted_iota(jnp.int32, (count, HALF), 1) // HEAD
    out = rows[:count]
    for h in range(1, HEADS):
        out = jnp.where(head == h, rows[h * count : (h + 1) * count], out)
    return out


def soft(scores, grad_probs):
    peak = jnp.max(scores, axis=0, keepdims=True)
    ex = jnp.exp(scores - peak)
    probs = ex / jnp.sum(ex, axis=0, keepdims=True)
    delta = jnp.sum(probs * grad_probs, axis=0, keepdims=True)
    return probs, probs * (grad_probs - delta)


def temporal_block(q, ga, k, v, bias):
    qs, gs = stack_heads(q), stack_heads(ga)
    st = mm(k, qs, NT)
    gt = mm(v, gs, NT)
    shape = (WIN, HEADS * WIN)
    older = lax.broadcasted_iota(jnp.int32, shape, 0) > lax.rem(
        lax.broadcasted_iota(jnp.int32, shape, 1), WIN
    )
    probs, grad = soft(
        jnp.where(older, st[:WIN] + bias, st[WIN:]), jnp.where(older, gt[:WIN], gt[WIN:])
    )

    def spread(t):
        return jnp.concatenate(
            [jnp.where(older, t, 0.0).astype(BF16), jnp.where(older, 0.0, t).astype(BF16)], axis=0
        )

    pt, dt = spread(probs), spread(grad)
    att = pick_heads(mm(pt, v, TN))
    dq = pick_heads(mm(dt, k, TN)) * SCALE
    return att, dq, mm(dt, qs, NN), mm(pt, gs, NN)


def spatial_block(q, ga, k, v):
    qs, gs = stack_heads(q), stack_heads(ga)
    shape = (WIN, HEADS * WIN)
    same = lax.rem(lax.broadcasted_iota(jnp.int32, shape, 0), 8) == lax.rem(
        lax.broadcasted_iota(jnp.int32, shape, 1), 8
    )
    probs, grad = soft(jnp.where(same, mm(k, qs, NT), NEG), mm(v, gs, NT))
    pt, dt = probs.astype(BF16), grad.astype(BF16)
    att = pick_heads(mm(pt, v, TN))
    dq = pick_heads(mm(dt, k, TN)) * SCALE
    return att, dq, mm(dt, qs, NN), mm(pt, gs, NN)


def coordinates():
    dp, tm, y = lax.axis_index("dp"), lax.axis_index("tm"), lax.axis_index("elec")
    z, rest = lax.div(tm, 4), lax.rem(tm, 4)
    x = lax.div(rest, 2) * 2 + dp
    return x, y, z, lax.rem(rest, 2)


def device_at(x, y, z, core):
    return {"dp": lax.rem(x, 2), "tm": z * 4 + lax.div(x, 2) * 2 + core, "elec": y}


CHUNKS = (48, 32, 16)
STARTS = (0, 48, 80)


def weight_rows(acc_in, acc_out, dst):
    for j in range(2):
        for i in range(3):
            first = i * HALF + j * 128
            dst[j, i * 512 : (i + 1) * 512] = acc_in[:, first : first + 128].astype(BF16)
        for i in range(2):
            first = i * HALF + j * 128
            dst[j, 1536 + i * HALF : 1536 + (i + 1) * HALF] = acc_out[:, first : first + 128].astype(BF16)


def layer_kernel(x_h, cot_h, wq_h, wk_h, wv_h, wo_h, out, *rest):
    w_outs = rest[:4]
    (
        xv, cv, halo, w_t, w_s, wo, q_t, k_t, v_t, g_t, dk_t, dv_t, att_t, dq_t, back_out, back_in, dx_t,
        xr, cr, q_s, k_s, v_s, g_s, dxs, dxr, acc_in_t, acc_out_t, acc_in_s, acc_out_s,
        ar_src, recv_a, part, recv_b, ar_out,
        load_sem, halo_send, halo_recv, go_send, go_recv, ret_send, ret_recv, ar_send, ar_recv,
    ) = rest[4:]
    elecs, patches, width = xv.shape
    quarter = patches // 4
    x, y, z, core = coordinates()
    tm = lax.axis_index("tm")
    right = {"tm": lax.rem(tm + 1, 16)}
    left = {"tm": lax.rem(tm + 15, 16)}
    where = {"x": x, "y": y, "z": z, "core": core}

    def peer(**by):
        at = {n: lax.rem(where[n] + by.get(n, 0), 2 if n == "core" else 4) for n in where}
        return device_at(at["x"], at["y"], at["z"], at["core"])

    orders = ((("x", "core"), ("z", "y")), (("z", "core"), ("x", "y")))

    def others(axes):
        low = 2 if axes[1] == "core" else 4
        return [(i, {axes[0]: i // low, axes[1]: i % low}) for i in range(1, 4 * low)]

    near = {tuple(sorted(by.items())) for axes in (orders[0] + orders[1]) for _, by in others(axes)}
    near = sorted({tuple((n, v) for n, v in by if v) for by in near})
    barrier = pltpu.get_barrier_semaphore()
    for device in [right, left] + [peer(**dict(by)) for by in near]:
        pl.semaphore_signal(barrier, inc=1, device_id=device, device_id_type=MESH)
    pl.semaphore_wait(barrier, 2 + len(near))

    pending = []

    def push(src, dst, sems, device):
        pltpu.make_async_remote_copy(
            src_ref=src, dst_ref=dst, send_sem=sems[0], recv_sem=sems[1], device_id=device, device_id_type=MESH
        ).start()

    def group(ref, sems):
        whole = pltpu.make_async_remote_copy(
            src_ref=ref, dst_ref=ref, send_sem=sems[0], recv_sem=sems[1], device_id=right, device_id_type=MESH
        )
        pending.append(whole)
        return whole

    def rows_at(first, size):
        return pl.ds(pl.multiple_of(first, 16), size)

    loads = []

    def load(src, dst):
        copy = pltpu.make_async_copy(src, dst, load_sem.at[len(loads)])
        copy.start()
        loads.append(copy)

    load(x_h, xv)
    load(cot_h, cv)
    load(wo_h, wo)
    for i, w in enumerate((wq_h, wk_h, wv_h)):
        load(w.at[:, HALF:], w_t.at[:, i * HALF : (i + 1) * HALF])
    for i, w in enumerate((wq_h, wk_h, wv_h)):
        load(w.at[:, :HALF], w_s.at[:, i * HALF : (i + 1) * HALF])
    at = rows_at(y * quarter, quarter)
    load(x_h.at[:, at], xr.at[:elecs])
    load(cot_h.at[:, at], cr.at[:elecs])
    loads[0].wait()
    loads[1].wait()
    halo_sems = halo_send.at[0], halo_recv.at[0]
    push(xv.at[:, patches - WIN :], halo, halo_sems, right)
    halo_copy = group(halo, halo_sems)
    go = {}

    def send_raw(c):
        here = slice(STARTS[c], STARTS[c] + CHUNKS[c])
        for k, (src, dst) in enumerate(((xv, xr), (cv, cr))):
            sems = go_send.at[c, k], go_recv.at[c, k]
            for d in (2, 1, 3):
                at = rows_at(lax.rem(y + d, 4) * quarter + STARTS[c], CHUNKS[c])
                push(src.at[:, at], dst.at[d * elecs : (d + 1) * elecs, here], sems, peer(y=d))
            go[c, k] = group(dst.at[elecs:, here], sems)

    send_raw(0)
    for copy in loads[2:]:
        copy.wait()

    bias0 = jnp.where(tm == 0, NEG, 0.0).astype(F32)

    def project_time(e, carry):
        q_t[e] = (mm(xv[e], w_t[:, :HALF], NN) * SCALE).astype(BF16)
        k_t[e, WIN:] = mm(xv[e], w_t[:, HALF : 2 * HALF], NN).astype(BF16)
        v_t[e, WIN:] = mm(xv[e], w_t[:, 2 * HALF :], NN).astype(BF16)
        g_t[e] = mm(cv[e], wo[HALF:, :], NT).astype(BF16)
        return carry

    lax.fori_loop(0, elecs, project_time, 0)

    def time_block(e, c, bias):
        rows, keys = slice(c * WIN, (c + 1) * WIN), slice(c * WIN, (c + 2) * WIN)
        att, dq, dk, dv = temporal_block(q_t[e, rows], g_t[e, rows], k_t[e, keys], v_t[e, keys], bias)
        att_t[e, rows] = att.astype(BF16)
        dq_t[e, rows] = dq.astype(BF16)
        return dk, dv

    def later_blocks(e, first_done):
        ones = time_block(e, 1, 0.0)
        twos = time_block(e, 2, 0.0)
        for ref, one, two in zip((dk_t, dv_t), ones, twos):
            if first_done:
                ref[e, :WIN] += one[:WIN]
            else:
                ref[e, :WIN] = one[:WIN]
            ref[e, WIN : 2 * WIN] = one[WIN:] + two[:WIN]
            ref[e, 2 * WIN :] = two[WIN:]

    def first_block(e, first_done):
        k_t[e, :WIN] = mm(halo[e], w_t[:, HALF : 2 * HALF], NN).astype(BF16)
        v_t[e, :WIN] = mm(halo[e], w_t[:, 2 * HALF :], NN).astype(BF16)
        for side, (ref, grad) in enumerate(zip((dk_t, dv_t), time_block(e, 0, bias0))):
            back_out[side, e] = grad[:WIN].astype(BF16)
            if first_done:
                ref[e, :WIN] = grad[WIN:]
            else:
                ref[e, :WIN] += grad[WIN:]

    def first_pair(i, carry):
        first_block(2 + 2 * i, True)
        first_block(3 + 2 * i, True)
        return carry

    def later_one(e, carry):
        later_blocks(e, True)
        return carry

    later_blocks(0, False)
    later_blocks(1, False)
    halo_copy.wait_recv()
    first_block(0, False)
    first_block(1, False)
    lax.fori_loop(0, elecs // 2 - 1, first_pair, 0)
    back_sems = halo_send.at[1], halo_recv.at[1]
    push(back_out, back_in, back_sems, left)
    back_copy = group(back_in, back_sems)
    lax.fori_loop(2, elecs, later_one, 0)
    send_raw(1)

    def span(c):
        return slice(STARTS[c], STARTS[c] + CHUNKS[c]), 4 * elecs * CHUNKS[c]

    def spatial_project(c):
        for k in range(2):
            go[c, k].wait_recv()
        here, rows = span(c)
        xi = xr[:, here].reshape(rows, width)
        shape = (4 * elecs, CHUNKS[c], HALF)
        q_s[:, : CHUNKS[c]] = (mm(xi, w_s[:, :HALF], NN) * SCALE).reshape(shape)
        k_s[:, : CHUNKS[c]] = mm(xi, w_s[:, HALF : 2 * HALF], NN).reshape(shape)
        v_s[:, : CHUNKS[c]] = mm(xi, w_s[:, 2 * HALF :], NN).reshape(shape)
        g_s[:, : CHUNKS[c]] = mm(cr[:, here].reshape(rows, width), wo[:HALF, :], NT).reshape(shape)

    def spatial_attend(c):
        def block(i, carry):
            for j in range(2):
                at = pl.ds(pl.multiple_of(i * 16 + j * 8, 8), 8)
                q, g, k, v = [ref[:, at, :].reshape(WIN, HALF).astype(BF16) for ref in (q_s, g_s, k_s, v_s)]
                for ref, value in zip((g_s, q_s, k_s, v_s), spatial_block(q, g, k, v)):
                    ref[:, at, :] = value.reshape(4 * elecs, 8, HALF)
            return carry

        lax.fori_loop(0, CHUNKS[c] // 16, block, 0)

    def spatial_end(c):
        here, rows = span(c)
        xi = xr[:, here].reshape(rows, width)
        grads = jnp.concatenate(
            [ref[:, : CHUNKS[c]].astype(BF16).reshape(rows, HALF) for ref in (q_s, k_s, v_s)], axis=1
        )
        dxs[:, here] = mm(grads, w_s[...], NT).astype(BF16).reshape(4 * elecs, CHUNKS[c], width)
        add_in = mm(xi, grads, TN)
        att = g_s[:, : CHUNKS[c]].astype(BF16).reshape(rows, HALF)
        add_out = mm(att, cr[:, here].reshape(rows, width), TN)
        if c == 0:
            acc_in_s[...] = add_in
            acc_out_s[...] = add_out
        else:
            acc_in_s[...] += add_in
            acc_out_s[...] += add_out

    returned = {}

    def send_back(c):
        here, _ = span(c)
        sems = ret_send.at[c], ret_recv.at[c]
        for d in (2, 1, 3):
            push(dxs.at[d * elecs : (d + 1) * elecs, here], dxr.at[d - 1, :, here], sems, peer(y=4 - d))
        returned[c] = group(dxr.at[:, :, here], sems)

    def place(c):
        here, _ = span(c)
        returned[c].wait_recv()
        for d in range(4):
            at = rows_at(lax.rem(y + d, 4) * quarter + STARTS[c], CHUNKS[c])
            if d == 0:
                piece = dxs[:elecs, here]
            else:
                piece = dxr[d - 1, :, here]
            out[:, at, :] = (dx_t[:, at, :] + piece.astype(F32)).astype(BF16)

    def summing(n):
        def exchange(p, step, axes, copies, whole):
            sems = ar_send.at[n, p, step], ar_recv.at[n, p, step]
            for i, by in others(axes):
                push(*copies(i, by), sems, peer(**by))
            return group(whole, sems)

        def own(axes, **by):
            at = [lax.rem(where[a] + by.get(a, 0), 2 if a == "core" else 4) for a in axes]
            return at[0] * (2 if axes[1] == "core" else 4) + at[1]

        waiting = [None, None]
        for p in range(2):
            axes = orders[p][0]
            waiting[p] = exchange(
                p,
                0,
                axes,
                lambda i, by: (ar_src.at[n, p, rows_at(own(axes, **by) * 256, 256)], recv_a.at[n, p, i - 1]),
                recv_a.at[n, p],
            )
        yield
        for p in range(2):
            waiting[p].wait_recv()
            total = ar_src[n, p, rows_at(own(orders[p][0]) * 256, 256)].astype(F32)
            for i in range(7):
                total = total + recv_a[n, p, i].astype(F32)
            part[n, p] = total.astype(BF16)
            axes = orders[p][1]
            waiting[p] = exchange(
                p,
                1,
                axes,
                lambda i, by: (part.at[n, p, rows_at(own(axes, **by) * 16, 16)], recv_b.at[n, p, i - 1]),
                recv_b.at[n, p],
            )
        yield
        for p in range(2):
            waiting[p].wait_recv()
            axes = orders[p][1]
            total = part[n, p, rows_at(own(axes) * 16, 16)].astype(F32)
            for i in range(15):
                total = total + recv_b[n, p, i].astype(F32)
            at = rows_at(own(orders[p][0]) * 256 + own(axes) * 16, 16)
            ar_out[n, p, at] = total.astype(BF16)
            spot = ar_out.at[n, p, at]
            waiting[p] = exchange(p, 2, axes, lambda i, by: (spot, spot), ar_out.at[n, p, :240])
        yield
        for p in range(2):
            waiting[p].wait_recv()
            axes = orders[p][0]
            spot = ar_out.at[n, p, rows_at(own(axes) * 256, 256)]
            waiting[p] = exchange(p, 3, axes, lambda i, by: (spot, spot), ar_out.at[n, p, :1792])
        yield
        for p in range(2):
            waiting[p].wait_recv()
            first = (1 - n) * HALF + p * 128
            for i in range(3):
                w_outs[i][:, first : first + 128] = ar_out[n, p, i * 512 : (i + 1) * 512]
            for i in range(2):
                low, column = (1 - n) * HALF, i * HALF + p * 128
                w_outs[3][low : low + HALF, column : column + 128] = ar_out[
                    n, p, 1536 + i * HALF : 1536 + (i + 1) * HALF
                ]
        yield

    back_copy.wait_recv()
    acc_in_t[...] = jnp.zeros_like(acc_in_t)
    acc_out_t[...] = jnp.zeros_like(acc_out_t)

    def end_time(e, carry):
        def full(own, side):
            tail = own[e, patches - WIN :] + back_in[side, e].astype(F32)
            return jnp.concatenate([own[e, : patches - WIN].astype(BF16), tail.astype(BF16)], axis=0)

        grads = jnp.concatenate([dq_t[e], full(dk_t, 0), full(dv_t, 1)], axis=1)
        dx_t[e] = mm(grads, w_t[...], NT)
        acc_in_t[...] += mm(xv[e], grads, TN)
        acc_out_t[...] += mm(att_t[e], cv[e], TN)
        return carry

    lax.fori_loop(0, elecs, end_time, 0)
    weight_rows(acc_in_t, acc_out_t, ar_src.at[0])
    time_sum, space_sum = summing(0), summing(1)
    next(time_sum)
    send_raw(2)
    spatial_project(0)
    spatial_attend(0)
    next(time_sum)
    spatial_end(0)
    spatial_project(1)
    spatial_attend(1)
    spatial_end(1)
    spatial_project(2)
    next(time_sum)
    send_back(0)
    spatial_attend(2)
    spatial_end(2)
    weight_rows(acc_in_s, acc_out_s, ar_src.at[1])
    next(space_sum)
    next(time_sum)
    send_back(2)
    next(space_sum)
    place(0)
    next(space_sum)
    send_back(1)
    next(time_sum)
    place(2)
    next(space_sum)
    place(1)
    next(space_sum)
    for whole in pending:
        whole.wait_send()


def end_kernel(dx, g0, g1, g2, g3, out, o0, o1, o2, o3):
    out[...] = dx[...]
    for grad, o in zip((g0, g1, g2, g3), (o0, o1, o2, o3)):
        o[...] = grad[...].astype(F32) * (1.0 / math.sqrt(196608))


def sds(shape, dtype):
    return jax.ShapeDtypeStruct(shape, dtype)


def shards(inputs, cotangent, w_query, w_key, w_value, w_out):
    _, elecs, patches, width = inputs.shape
    quarter = patches // 4
    vm, dma = pltpu.VMEM, pltpu.SemaphoreType.DMA
    tokens = (elecs, patches)
    ext = (elecs, patches + WIN)
    everyone = (4 * elecs, quarter)
    scratch = (
        [vm(tokens + (width,), BF16)] * 2
        + [vm((elecs, WIN, width), BF16)]
        + [vm((width, 3 * HALF), BF16)] * 2
        + [vm((width, width), BF16)]
        + [vm(tokens + (HALF,), BF16), vm(ext + (HALF,), BF16), vm(ext + (HALF,), BF16), vm(tokens + (HALF,), BF16)]
        + [vm(tokens + (HALF,), F32)] * 2
        + [vm(tokens + (HALF,), BF16)] * 2
        + [vm((2, elecs, WIN, HALF), BF16)] * 2
        + [vm(tokens + (width,), F32)]
        + [vm(everyone + (width,), BF16)] * 2
        + [vm((4 * elecs, CHUNKS[0], HALF), F32)] * 4
        + [vm(everyone + (width,), BF16), vm((3, elecs, quarter, width), BF16)]
        + [vm((width, 3 * HALF), F32), vm((HALF, width), F32)] * 2
        + [vm((2, 2, 2048, 128), BF16)]
        + [vm((2, 2, 7, 256, 128), BF16), vm((2, 2, 256, 128), BF16), vm((2, 2, 15, 16, 128), BF16)]
        + [vm((2, 2, 2048, 128), BF16)]
        + [dma((11,)), dma((2,)), dma((2,))]
        + [dma((3, 2))] * 2
        + [dma((3,))] * 2
        + [dma((2, 2, 4))] * 2
    )
    grad_inputs, *grads = pl.pallas_call(
        layer_kernel,
        out_shape=(sds(tokens + (width,), BF16),) + (sds((width, width), BF16),) * 4,
        in_specs=[pl.BlockSpec(memory_space=pl.ANY)] * 6,
        out_specs=(pl.BlockSpec(memory_space=pltpu.VMEM),) * 5,
        scratch_shapes=scratch,
        compiler_params=pltpu.CompilerParams(
            collective_id=0, has_side_effects=True, vmem_limit_bytes=VMEM_LIMIT
        ),
        cost_estimate=pl.CostEstimate(flops=2 * 10**10, bytes_accessed=10**7, transcendentals=2 * 10**6),
    )(inputs[0], cotangent[0], w_query, w_key, w_value, w_out)
    grad_inputs, *grads = pl.pallas_call(
        end_kernel,
        out_shape=(sds(tokens + (width,), BF16),) + (sds((width, width), F32),) * 4,
        in_specs=[pl.BlockSpec(memory_space=pltpu.VMEM)] * 5,
        out_specs=(pl.BlockSpec(memory_space=pltpu.VMEM),) * 5,
        compiler_params=pltpu.CompilerParams(vmem_limit_bytes=VMEM_LIMIT),
    )(grad_inputs, *grads)
    return (grad_inputs[None],) + tuple(grads)


def solution(mesh):
    return jax.shard_map(
        shards,
        mesh=mesh,
        in_specs=(P("dp", "elec", "tm", None), P("dp", "elec", "tm", None), P(), P(), P(), P()),
        out_specs=(P("dp", "elec", "tm", None), P(), P(), P(), P()),
        check_vma=False,
    )
```

```python
import math

import jax
import jax.numpy as jnp
from jax import lax
from jax.experimental import pallas as pl
from jax.experimental.pallas import tpu as pltpu
from jax.sharding import PartitionSpec as P

BF16 = jnp.bfloat16
F32 = jnp.float32
WIN = 128
HALF = 256
HEAD = 64
HEADS = 4
NEG = -1e30
SCALE = 0.125
VMEM_LIMIT = 56 * 1024 * 1024
MESH = pl.DeviceIdType.MESH

NN = (((1,), (0,)), ((), ()))
NT = (((1,), (1,)), ((), ()))
TN = (((0,), (0,)), ((), ()))


def mm(left, right, dims):
    return lax.dot_general(left, right, dims, preferred_element_type=F32)


def stack_heads(rows):
    column = lax.broadcasted_iota(jnp.int32, (1, HALF), 1)
    keeps = [(column >= h * HEAD) & (column < (h + 1) * HEAD) for h in range(HEADS)]
    return jnp.concatenate([rows * keep.astype(F32).astype(BF16) for keep in keeps], axis=0)


def pick_heads(rows):
    r = rows.shape[0] // HEADS
    even = lax.broadcasted_iota(jnp.int32, (r, 128), 1) < HEAD
    return jnp.concatenate(
        [
            jnp.where(even, rows[:r, :128], rows[r : 2 * r, :128]),
            jnp.where(even, rows[2 * r : 3 * r, 128:], rows[3 * r :, 128:]),
        ],
        axis=1,
    )


def soft(scores, grad_probs):
    ex = jnp.exp(scores - jnp.max(scores, axis=0, keepdims=True))
    probs = ex * (1.0 / jnp.sum(ex, axis=0, keepdims=True))
    delta = jnp.sum(probs * grad_probs, axis=0, keepdims=True)
    return probs.astype(BF16), (probs * (grad_probs - delta)).astype(BF16)


def make_masks(older, older_low, newer_low, apart):
    row = lax.broadcasted_iota(jnp.int32, (WIN, WIN), 0)
    column = lax.broadcasted_iota(jnp.int32, (WIN, WIN), 1)
    old = (row > column).astype(F32)
    far = jnp.where(lax.rem(row, 8) == lax.rem(column, 8), 0.0, NEG).astype(F32)
    for h in range(HEADS):
        at = slice(h * WIN, (h + 1) * WIN)
        older[:, at] = old
        older_low[:, at] = old.astype(BF16)
        newer_low[:, at] = (1.0 - old).astype(BF16)
        apart[:, at] = far


def temporal_block(q, ga, k, v, bias, older, older_low, newer_low):
    qs, gs = stack_heads(q), stack_heads(ga)
    st = mm(k, qs, NT)
    gt = mm(v, gs, NT)
    old = older[...] > 0.5
    early = st[:WIN] if bias is None else st[:WIN] + bias
    probs, grad = soft(jnp.where(old, early, st[WIN:]), jnp.where(old, gt[:WIN], gt[WIN:]))
    pt = jnp.concatenate([probs * older_low[...], probs * newer_low[...]], axis=0)
    dt = jnp.concatenate([grad * older_low[...], grad * newer_low[...]], axis=0)
    att = pick_heads(mm(pt, v, TN))
    dq = pick_heads(mm(dt, k, TN)) * SCALE
    return att, dq, mm(dt, qs, NN), mm(pt, gs, NN)


def spatial_block(q, ga, k, v, apart):
    qs, gs = stack_heads(q), stack_heads(ga)
    pt, dt = soft(mm(k, qs, NT) + apart[...], mm(v, gs, NT))
    att = pick_heads(mm(pt, v, TN))
    dq = pick_heads(mm(dt, k, TN)) * SCALE
    return att, dq, mm(dt, qs, NN), mm(pt, gs, NN)


def coordinates():
    dp, tm, y = lax.axis_index("dp"), lax.axis_index("tm"), lax.axis_index("elec")
    z, rest = lax.div(tm, 4), lax.rem(tm, 4)
    x = lax.div(rest, 2) * 2 + dp
    return x, y, z, lax.rem(rest, 2)


def device_at(x, y, z, core):
    return {"dp": lax.rem(x, 2), "tm": z * 4 + lax.div(x, 2) * 2 + core, "elec": y}


CHUNKS = (48, 32, 16)
STARTS = (0, 48, 80)


def weight_rows(acc_in, acc_out, dst):
    for j in range(2):
        for i in range(3):
            first = i * HALF + j * 128
            dst[j, i * 512 : (i + 1) * 512] = acc_in[:, first : first + 128].astype(BF16)
        for i in range(2):
            first = i * HALF + j * 128
            dst[j, 1536 + i * HALF : 1536 + (i + 1) * HALF] = acc_out[:, first : first + 128].astype(BF16)


def layer_kernel(x_h, cot_h, wq_h, wk_h, wv_h, wo_h, out, *rest):
    w_outs = rest[:4]
    (
        xv, cv, halo, w_t, w_s, wo, q_t, k_t, v_t, g_t, dk_t, dv_t, att_t, dq_t, back_out, back_in, dx_t,
        xr, cr, q_s, k_s, v_s, g_s, dxs, dxr, acc_in_t, acc_out_t, acc_in_s, acc_out_s,
        ar_src, recv_a, part, recv_b, ar_out, older, older_low, newer_low, apart,
        load_sem, halo_send, halo_recv, go_send, go_recv, ret_send, ret_recv, ar_send, ar_recv,
    ) = rest[4:]
    elecs, patches, width = xv.shape
    quarter = patches // 4
    x, y, z, core = coordinates()
    tm = lax.axis_index("tm")
    right = {"tm": lax.rem(tm + 1, 16)}
    left = {"tm": lax.rem(tm + 15, 16)}
    where = {"x": x, "y": y, "z": z, "core": core}

    def peer(**by):
        at = {n: lax.rem(where[n] + by.get(n, 0), 2 if n == "core" else 4) for n in where}
        return device_at(at["x"], at["y"], at["z"], at["core"])

    orders = ((("x", "core"), ("z", "y")), (("z", "core"), ("x", "y")))

    def others(axes):
        low = 2 if axes[1] == "core" else 4
        return [(i, {axes[0]: i // low, axes[1]: i % low}) for i in range(1, 4 * low)]

    near = {tuple(sorted(by.items())) for axes in (orders[0] + orders[1]) for _, by in others(axes)}
    near = sorted({tuple((n, v) for n, v in by if v) for by in near})
    barrier = pltpu.get_barrier_semaphore()
    for device in [right, left] + [peer(**dict(by)) for by in near]:
        pl.semaphore_signal(barrier, inc=1, device_id=device, device_id_type=MESH)
    pl.semaphore_wait(barrier, 2 + len(near))

    pending = []

    def push(src, dst, sems, device):
        pltpu.make_async_remote_copy(
            src_ref=src, dst_ref=dst, send_sem=sems[0], recv_sem=sems[1], device_id=device, device_id_type=MESH
        ).start()

    def group(ref, sems):
        whole = pltpu.make_async_remote_copy(
            src_ref=ref, dst_ref=ref, send_sem=sems[0], recv_sem=sems[1], device_id=right, device_id_type=MESH
        )
        pending.append(whole)
        return whole

    def rows_at(first, size):
        return pl.ds(pl.multiple_of(first, 16), size)

    loads = []

    def load(src, dst):
        copy = pltpu.make_async_copy(src, dst, load_sem.at[len(loads)])
        copy.start()
        loads.append(copy)

    load(x_h, xv)
    load(cot_h, cv)
    load(wo_h, wo)
    for i, w in enumerate((wq_h, wk_h, wv_h)):
        load(w.at[:, HALF:], w_t.at[:, i * HALF : (i + 1) * HALF])
    for i, w in enumerate((wq_h, wk_h, wv_h)):
        load(w.at[:, :HALF], w_s.at[:, i * HALF : (i + 1) * HALF])
    at = rows_at(y * quarter, quarter)
    load(x_h.at[:, at], xr.at[:elecs])
    load(cot_h.at[:, at], cr.at[:elecs])
    loads[0].wait()
    loads[1].wait()
    halo_sems = halo_send.at[0], halo_recv.at[0]
    push(xv.at[:, patches - WIN :], halo, halo_sems, right)
    halo_copy = group(halo, halo_sems)
    go = {}

    def send_raw(c):
        here = slice(STARTS[c], STARTS[c] + CHUNKS[c])
        for k, (src, dst) in enumerate(((xv, xr), (cv, cr))):
            sems = go_send.at[c, k], go_recv.at[c, k]
            for d in (2, 1, 3):
                at = rows_at(lax.rem(y + d, 4) * quarter + STARTS[c], CHUNKS[c])
                push(src.at[:, at], dst.at[d * elecs : (d + 1) * elecs, here], sems, peer(y=d))
            go[c, k] = group(dst.at[elecs:, here], sems)

    send_raw(0)
    masks = older, older_low, newer_low
    make_masks(*masks, apart)
    for copy in loads[2:]:
        copy.wait()

    bias0 = jnp.where(tm == 0, NEG, 0.0).astype(F32)

    def project_time(e, carry):
        q_t[e] = (mm(xv[e], w_t[:, :HALF], NN) * SCALE).astype(BF16)
        k_t[e, WIN:] = mm(xv[e], w_t[:, HALF : 2 * HALF], NN).astype(BF16)
        v_t[e, WIN:] = mm(xv[e], w_t[:, 2 * HALF :], NN).astype(BF16)
        g_t[e] = mm(cv[e], wo[HALF:, :], NT).astype(BF16)
        return carry

    lax.fori_loop(0, elecs, project_time, 0)

    def time_block(e, c, bias):
        rows, keys = slice(c * WIN, (c + 1) * WIN), slice(c * WIN, (c + 2) * WIN)
        att, dq, dk, dv = temporal_block(q_t[e, rows], g_t[e, rows], k_t[e, keys], v_t[e, keys], bias, *masks)
        att_t[e, rows] = att.astype(BF16)
        dq_t[e, rows] = dq.astype(BF16)
        return dk, dv

    def later_blocks(e, first_done):
        ones = time_block(e, 1, None)
        twos = time_block(e, 2, None)
        for ref, one, two in zip((dk_t, dv_t), ones, twos):
            if first_done:
                ref[e, :WIN] += one[:WIN]
            else:
                ref[e, :WIN] = one[:WIN]
            ref[e, WIN : 2 * WIN] = one[WIN:] + two[:WIN]
            ref[e, 2 * WIN :] = two[WIN:]

    def first_block(e, first_done):
        k_t[e, :WIN] = mm(halo[e], w_t[:, HALF : 2 * HALF], NN).astype(BF16)
        v_t[e, :WIN] = mm(halo[e], w_t[:, 2 * HALF :], NN).astype(BF16)
        for side, (ref, grad) in enumerate(zip((dk_t, dv_t), time_block(e, 0, bias0))):
            back_out[side, e] = grad[:WIN].astype(BF16)
            if first_done:
                ref[e, :WIN] = grad[WIN:]
            else:
                ref[e, :WIN] += grad[WIN:]

    def first_pair(i, carry):
        first_block(2 + 2 * i, True)
        first_block(3 + 2 * i, True)
        return carry

    def later_one(e, carry):
        later_blocks(e, True)
        return carry

    later_blocks(0, False)
    later_blocks(1, False)
    halo_copy.wait_recv()
    first_block(0, False)
    first_block(1, False)
    lax.fori_loop(0, elecs // 2 - 1, first_pair, 0)
    back_sems = halo_send.at[1], halo_recv.at[1]
    push(back_out, back_in, back_sems, left)
    back_copy = group(back_in, back_sems)
    lax.fori_loop(2, elecs, later_one, 0)
    send_raw(1)

    def span(c):
        return slice(STARTS[c], STARTS[c] + CHUNKS[c]), 4 * elecs * CHUNKS[c]

    def spatial_project(c):
        for k in range(2):
            go[c, k].wait_recv()
        here, rows = span(c)
        xi = xr[:, here].reshape(rows, width)
        shape = (4 * elecs, CHUNKS[c], HALF)
        q_s[:, : CHUNKS[c]] = (mm(xi, w_s[:, :HALF], NN) * SCALE).reshape(shape)
        k_s[:, : CHUNKS[c]] = mm(xi, w_s[:, HALF : 2 * HALF], NN).reshape(shape)
        v_s[:, : CHUNKS[c]] = mm(xi, w_s[:, 2 * HALF :], NN).reshape(shape)
        g_s[:, : CHUNKS[c]] = mm(cr[:, here].reshape(rows, width), wo[:HALF, :], NT).reshape(shape)

    def spatial_attend(c):
        def block(i, carry):
            for j in range(2):
                at = pl.ds(pl.multiple_of(i * 16 + j * 8, 8), 8)
                q, g, k, v = [ref[:, at, :].reshape(WIN, HALF).astype(BF16) for ref in (q_s, g_s, k_s, v_s)]
                for ref, value in zip((g_s, q_s, k_s, v_s), spatial_block(q, g, k, v, apart)):
                    ref[:, at, :] = value.reshape(4 * elecs, 8, HALF)
            return carry

        lax.fori_loop(0, CHUNKS[c] // 16, block, 0)

    def spatial_end(c):
        here, rows = span(c)
        xi = xr[:, here].reshape(rows, width)
        grads = jnp.concatenate(
            [ref[:, : CHUNKS[c]].astype(BF16).reshape(rows, HALF) for ref in (q_s, k_s, v_s)], axis=1
        )
        dxs[:, here] = mm(grads, w_s[...], NT).astype(BF16).reshape(4 * elecs, CHUNKS[c], width)
        add_in = mm(xi, grads, TN)
        att = g_s[:, : CHUNKS[c]].astype(BF16).reshape(rows, HALF)
        add_out = mm(att, cr[:, here].reshape(rows, width), TN)
        if c == 0:
            acc_in_s[...] = add_in
            acc_out_s[...] = add_out
        else:
            acc_in_s[...] += add_in
            acc_out_s[...] += add_out

    returned = {}

    def send_back(c):
        here, _ = span(c)
        sems = ret_send.at[c], ret_recv.at[c]
        for d in (2, 1, 3):
            push(dxs.at[d * elecs : (d + 1) * elecs, here], dxr.at[d - 1, :, here], sems, peer(y=4 - d))
        returned[c] = group(dxr.at[:, :, here], sems)

    def place(c):
        here, _ = span(c)
        returned[c].wait_recv()
        for d in range(4):
            at = rows_at(lax.rem(y + d, 4) * quarter + STARTS[c], CHUNKS[c])
            if d == 0:
                piece = dxs[:elecs, here]
            else:
                piece = dxr[d - 1, :, here]
            out[:, at, :] = (dx_t[:, at, :] + piece.astype(F32)).astype(BF16)

    def summing(n):
        def exchange(p, step, axes, copies, whole):
            sems = ar_send.at[n, p, step], ar_recv.at[n, p, step]
            for i, by in others(axes):
                push(*copies(i, by), sems, peer(**by))
            return group(whole, sems)

        def own(axes, **by):
            at = [lax.rem(where[a] + by.get(a, 0), 2 if a == "core" else 4) for a in axes]
            return at[0] * (2 if axes[1] == "core" else 4) + at[1]

        waiting = [None, None]
        for p in range(2):
            axes = orders[p][0]
            waiting[p] = exchange(
                p,
                0,
                axes,
                lambda i, by: (ar_src.at[n, p, rows_at(own(axes, **by) * 256, 256)], recv_a.at[n, p, i - 1]),
                recv_a.at[n, p],
            )
        yield
        for p in range(2):
            waiting[p].wait_recv()
            total = ar_src[n, p, rows_at(own(orders[p][0]) * 256, 256)].astype(F32)
            for i in range(7):
                total = total + recv_a[n, p, i].astype(F32)
            part[n, p] = total.astype(BF16)
            axes = orders[p][1]
            waiting[p] = exchange(
                p,
                1,
                axes,
                lambda i, by: (part.at[n, p, rows_at(own(axes, **by) * 16, 16)], recv_b.at[n, p, i - 1]),
                recv_b.at[n, p],
            )
        yield
        for p in range(2):
            waiting[p].wait_recv()
            axes = orders[p][1]
            total = part[n, p, rows_at(own(axes) * 16, 16)].astype(F32)
            for i in range(15):
                total = total + recv_b[n, p, i].astype(F32)
            at = rows_at(own(orders[p][0]) * 256 + own(axes) * 16, 16)
            ar_out[n, p, at] = total.astype(BF16)
            spot = ar_out.at[n, p, at]
            waiting[p] = exchange(p, 2, axes, lambda i, by: (spot, spot), ar_out.at[n, p, :240])
        yield
        for p in range(2):
            waiting[p].wait_recv()
            axes = orders[p][0]
            spot = ar_out.at[n, p, rows_at(own(axes) * 256, 256)]
            waiting[p] = exchange(p, 3, axes, lambda i, by: (spot, spot), ar_out.at[n, p, :1792])
        yield
        for p in range(2):
            waiting[p].wait_recv()
            first = (1 - n) * HALF + p * 128
            for i in range(3):
                w_outs[i][:, first : first + 128] = ar_out[n, p, i * 512 : (i + 1) * 512]
            for i in range(2):
                low, column = (1 - n) * HALF, i * HALF + p * 128
                w_outs[3][low : low + HALF, column : column + 128] = ar_out[
                    n, p, 1536 + i * HALF : 1536 + (i + 1) * HALF
                ]
        yield

    back_copy.wait_recv()
    acc_in_t[...] = jnp.zeros_like(acc_in_t)
    acc_out_t[...] = jnp.zeros_like(acc_out_t)

    def end_time(e, carry):
        def full(own, side):
            tail = own[e, patches - WIN :] + back_in[side, e].astype(F32)
            return jnp.concatenate([own[e, : patches - WIN].astype(BF16), tail.astype(BF16)], axis=0)

        grads = jnp.concatenate([dq_t[e], full(dk_t, 0), full(dv_t, 1)], axis=1)
        dx_t[e] = mm(grads, w_t[...], NT)
        acc_in_t[...] += mm(xv[e], grads, TN)
        acc_out_t[...] += mm(att_t[e], cv[e], TN)
        return carry

    lax.fori_loop(0, elecs, end_time, 0)
    weight_rows(acc_in_t, acc_out_t, ar_src.at[0])
    time_sum, space_sum = summing(0), summing(1)
    next(time_sum)
    send_raw(2)
    spatial_project(0)
    spatial_attend(0)
    next(time_sum)
    spatial_end(0)
    spatial_project(1)
    spatial_attend(1)
    spatial_end(1)
    spatial_project(2)
    next(time_sum)
    send_back(0)
    spatial_attend(2)
    spatial_end(2)
    weight_rows(acc_in_s, acc_out_s, ar_src.at[1])
    next(space_sum)
    next(time_sum)
    send_back(2)
    next(space_sum)
    place(0)
    next(space_sum)
    send_back(1)
    next(time_sum)
    place(2)
    next(space_sum)
    place(1)
    next(space_sum)
    for whole in pending:
        whole.wait_send()


def end_kernel(dx, g0, g1, g2, g3, out, o0, o1, o2, o3):
    out[...] = dx[...]
    for grad, o in zip((g0, g1, g2, g3), (o0, o1, o2, o3)):
        o[...] = grad[...].astype(F32) * (1.0 / math.sqrt(196608))


def sds(shape, dtype):
    return jax.ShapeDtypeStruct(shape, dtype)


def shards(inputs, cotangent, w_query, w_key, w_value, w_out):
    _, elecs, patches, width = inputs.shape
    quarter = patches // 4
    vm, dma = pltpu.VMEM, pltpu.SemaphoreType.DMA
    tokens = (elecs, patches)
    ext = (elecs, patches + WIN)
    everyone = (4 * elecs, quarter)
    scratch = (
        [vm(tokens + (width,), BF16)] * 2
        + [vm((elecs, WIN, width), BF16)]
        + [vm((width, 3 * HALF), BF16)] * 2
        + [vm((width, width), BF16)]
        + [vm(tokens + (HALF,), BF16), vm(ext + (HALF,), BF16), vm(ext + (HALF,), BF16), vm(tokens + (HALF,), BF16)]
        + [vm(tokens + (HALF,), F32)] * 2
        + [vm(tokens + (HALF,), BF16)] * 2
        + [vm((2, elecs, WIN, HALF), BF16)] * 2
        + [vm(tokens + (width,), F32)]
        + [vm(everyone + (width,), BF16)] * 2
        + [vm((4 * elecs, CHUNKS[0], HALF), F32)] * 4
        + [vm(everyone + (width,), BF16), vm((3, elecs, quarter, width), BF16)]
        + [vm((width, 3 * HALF), F32), vm((HALF, width), F32)] * 2
        + [vm((2, 2, 2048, 128), BF16)]
        + [vm((2, 2, 7, 256, 128), BF16), vm((2, 2, 256, 128), BF16), vm((2, 2, 15, 16, 128), BF16)]
        + [vm((2, 2, 2048, 128), BF16)]
        + [vm((WIN, HEADS * WIN), t) for t in (F32, BF16, BF16, F32)]
        + [dma((11,)), dma((2,)), dma((2,))]
        + [dma((3, 2))] * 2
        + [dma((3,))] * 2
        + [dma((2, 2, 4))] * 2
    )
    grad_inputs, *grads = pl.pallas_call(
        layer_kernel,
        out_shape=(sds(tokens + (width,), BF16),) + (sds((width, width), BF16),) * 4,
        in_specs=[pl.BlockSpec(memory_space=pl.ANY)] * 6,
        out_specs=(pl.BlockSpec(memory_space=pltpu.VMEM),) * 5,
        scratch_shapes=scratch,
        compiler_params=pltpu.CompilerParams(
            collective_id=0, has_side_effects=True, vmem_limit_bytes=VMEM_LIMIT
        ),
        cost_estimate=pl.CostEstimate(flops=2 * 10**10, bytes_accessed=10**7, transcendentals=2 * 10**6),
    )(inputs[0], cotangent[0], w_query, w_key, w_value, w_out)
    token_spec = pl.BlockSpec((1, patches, width), lambda i: (i, 0, 0))
    weight_spec = pl.BlockSpec((width // 4, width), lambda i: (i, 0))
    grad_inputs, *grads = pl.pallas_call(
        end_kernel,
        grid=(4,),
        out_shape=(sds(tokens + (width,), BF16),) + (sds((width, width), F32),) * 4,
        in_specs=[token_spec] + [weight_spec] * 4,
        out_specs=(token_spec,) + (weight_spec,) * 4,
        compiler_params=pltpu.CompilerParams(vmem_limit_bytes=VMEM_LIMIT),
    )(grad_inputs, *grads)
    return (grad_inputs[None],) + tuple(grads)


def solution(mesh):
    return jax.shard_map(
        shards,
        mesh=mesh,
        in_specs=(P("dp", "elec", "tm", None), P("dp", "elec", "tm", None), P(), P(), P(), P()),
        out_specs=(P("dp", "elec", "tm", None), P(), P(), P(), P()),
        check_vma=False,
    )
```

```python
import math

import jax
import jax.numpy as jnp
from jax import lax
from jax.experimental import pallas as pl
from jax.experimental.pallas import tpu as pltpu
from jax.sharding import PartitionSpec as P

BF16 = jnp.bfloat16
F32 = jnp.float32
WIN = 128
HALF = 256
HEAD = 64
HEADS = 4
NEG = -1e30
SCALE = 0.125
VMEM_LIMIT = 56 * 1024 * 1024
MESH = pl.DeviceIdType.MESH

NN = (((1,), (0,)), ((), ()))
NT = (((1,), (1,)), ((), ()))
TN = (((0,), (0,)), ((), ()))


def mm(left, right, dims):
    return lax.dot_general(left, right, dims, preferred_element_type=F32)


def stack_heads(rows):
    column = lax.broadcasted_iota(jnp.int32, (1, HALF), 1)
    keeps = [(column >= h * HEAD) & (column < (h + 1) * HEAD) for h in range(HEADS)]
    return jnp.concatenate([rows * keep.astype(F32).astype(BF16) for keep in keeps], axis=0)


def pick_heads(rows):
    r = rows.shape[0] // HEADS
    even = lax.broadcasted_iota(jnp.int32, (r, 128), 1) < HEAD
    return jnp.concatenate(
        [
            jnp.where(even, rows[:r, :128], rows[r : 2 * r, :128]),
            jnp.where(even, rows[2 * r : 3 * r, 128:], rows[3 * r :, 128:]),
        ],
        axis=1,
    )


def soft(scores, grad_probs):
    ex = jnp.exp(scores - jnp.max(scores, axis=0, keepdims=True))
    probs = ex * (1.0 / jnp.sum(ex, axis=0, keepdims=True))
    delta = jnp.sum(probs * grad_probs, axis=0, keepdims=True)
    return probs.astype(BF16), (probs * (grad_probs - delta)).astype(BF16)


def make_masks(older, older_low, newer_low, apart):
    row = lax.broadcasted_iota(jnp.int32, (WIN, WIN), 0)
    column = lax.broadcasted_iota(jnp.int32, (WIN, WIN), 1)
    old = (row > column).astype(F32)
    far = jnp.where(lax.rem(row, 8) == lax.rem(column, 8), 0.0, NEG).astype(F32)
    for h in range(HEADS):
        at = slice(h * WIN, (h + 1) * WIN)
        older[:, at] = old
        older_low[:, at] = old.astype(BF16)
        newer_low[:, at] = (1.0 - old).astype(BF16)
        apart[:, at] = far


def temporal_block(q, ga, k, v, bias, older, older_low, newer_low):
    qs, gs = stack_heads(q), stack_heads(ga)
    st = mm(k, qs, NT)
    gt = mm(v, gs, NT)
    old = older[...] > 0.5
    early = st[:WIN] if bias is None else st[:WIN] + bias
    probs, grad = soft(jnp.where(old, early, st[WIN:]), jnp.where(old, gt[:WIN], gt[WIN:]))
    pt = jnp.concatenate([probs * older_low[...], probs * newer_low[...]], axis=0)
    dt = jnp.concatenate([grad * older_low[...], grad * newer_low[...]], axis=0)
    att = pick_heads(mm(pt, v, TN))
    dq = pick_heads(mm(dt, k, TN)) * SCALE
    return att, dq, mm(dt, qs, NN), mm(pt, gs, NN)


def spatial_block(q, ga, k, v, apart):
    qs, gs = stack_heads(q), stack_heads(ga)
    pt, dt = soft(mm(k, qs, NT) + apart[...], mm(v, gs, NT))
    att = pick_heads(mm(pt, v, TN))
    dq = pick_heads(mm(dt, k, TN)) * SCALE
    return att, dq, mm(dt, qs, NN), mm(pt, gs, NN)


def coordinates():
    dp, tm, y = lax.axis_index("dp"), lax.axis_index("tm"), lax.axis_index("elec")
    z, rest = lax.div(tm, 4), lax.rem(tm, 4)
    x = lax.div(rest, 2) * 2 + dp
    return x, y, z, lax.rem(rest, 2)


def device_at(x, y, z, core):
    return {"dp": lax.rem(x, 2), "tm": z * 4 + lax.div(x, 2) * 2 + core, "elec": y}


CHUNKS = (48, 32, 16)
STARTS = (0, 48, 80)


def weight_rows(acc_in, acc_out, dst):
    for j in range(2):
        for i in range(3):
            first = i * HALF + j * 128
            dst[j, i * 512 : (i + 1) * 512] = acc_in[:, first : first + 128].astype(BF16)
        for i in range(2):
            first = i * HALF + j * 128
            dst[j, 1536 + i * HALF : 1536 + (i + 1) * HALF] = acc_out[:, first : first + 128].astype(BF16)


def layer_kernel(x_h, cot_h, wq_h, wk_h, wv_h, wo_h, out, *rest):
    w_outs = rest[:4]
    (
        xv, cv, halo, w_t, w_s, wo, q_t, k_t, v_t, g_t, dk_t, dv_t, att_t, dq_t, back_out, back_in, dx_t,
        xr, cr, q_s, k_s, v_s, g_s, dxs, dxr, acc_in_t, acc_out_t, acc_in_s, acc_out_s,
        ar_src, recv_c, part_c, recv_a, part, recv_b, ar_out, older, older_low, newer_low, apart,
        load_sem, halo_send, halo_recv, go_send, go_recv, ret_send, ret_recv, ar_send, ar_recv,
    ) = rest[4:]
    elecs, patches, width = xv.shape
    quarter = patches // 4
    x, y, z, core = coordinates()
    tm = lax.axis_index("tm")
    right = {"tm": lax.rem(tm + 1, 16)}
    left = {"tm": lax.rem(tm + 15, 16)}
    where = {"x": x, "y": y, "z": z, "core": core}

    def peer(**by):
        at = {n: lax.rem(where[n] + by.get(n, 0), 2 if n == "core" else 4) for n in where}
        return device_at(at["x"], at["y"], at["z"], at["core"])

    orders = (("x", "z"), ("z", "x"))

    def on_axis(a):
        return [(d, {a: d}) for d in range(1, 4)]

    def on_plane(b):
        return [(i, {b: i // 4, "y": i % 4}) for i in range(1, 16)]

    loads = []

    def load(src, dst):
        copy = pltpu.make_async_copy(src, dst, load_sem.at[len(loads)])
        copy.start()
        loads.append(copy)

    load(x_h, xv)
    load(cot_h, cv)
    load(wo_h, wo)
    for i, w in enumerate((wq_h, wk_h, wv_h)):
        load(w.at[:, HALF:], w_t.at[:, i * HALF : (i + 1) * HALF])
    for i, w in enumerate((wq_h, wk_h, wv_h)):
        load(w.at[:, :HALF], w_s.at[:, i * HALF : (i + 1) * HALF])
    at = pl.ds(pl.multiple_of(y * quarter, 16), quarter)
    load(x_h.at[:, at], xr.at[:elecs])
    load(cot_h.at[:, at], cr.at[:elecs])

    near = {tuple((n, v) for n, v in by.items() if v) for b in "xz" for _, by in on_plane(b)}
    near = [(("core", 1),)] + sorted(near)
    barrier = pltpu.get_barrier_semaphore()
    for device in [right, left] + [peer(**dict(by)) for by in near]:
        pl.semaphore_signal(barrier, inc=1, device_id=device, device_id_type=MESH)
    pl.semaphore_wait(barrier, 2 + len(near))

    pending = []

    def push(src, dst, sems, device):
        pltpu.make_async_remote_copy(
            src_ref=src, dst_ref=dst, send_sem=sems[0], recv_sem=sems[1], device_id=device, device_id_type=MESH
        ).start()

    def group(ref, sems):
        whole = pltpu.make_async_remote_copy(
            src_ref=ref, dst_ref=ref, send_sem=sems[0], recv_sem=sems[1], device_id=right, device_id_type=MESH
        )
        pending.append(whole)
        return whole

    def rows_at(first, size):
        return pl.ds(pl.multiple_of(first, 16), size)

    loads[0].wait()
    loads[1].wait()
    halo_sems = halo_send.at[0], halo_recv.at[0]
    push(xv.at[:, patches - WIN :], halo, halo_sems, right)
    halo_copy = group(halo, halo_sems)
    go = {}

    def send_raw(c):
        here = slice(STARTS[c], STARTS[c] + CHUNKS[c])
        for k, (src, dst) in enumerate(((xv, xr), (cv, cr))):
            sems = go_send.at[c, k], go_recv.at[c, k]
            for d in (2, 1, 3):
                at = rows_at(lax.rem(y + d, 4) * quarter + STARTS[c], CHUNKS[c])
                push(src.at[:, at], dst.at[d * elecs : (d + 1) * elecs, here], sems, peer(y=d))
            go[c, k] = group(dst.at[elecs:, here], sems)

    send_raw(0)
    masks = older, older_low, newer_low
    make_masks(*masks, apart)
    for copy in loads[2:]:
        copy.wait()

    bias0 = jnp.where(tm == 0, NEG, 0.0).astype(F32)

    def project_time(e, carry):
        q_t[e] = (mm(xv[e], w_t[:, :HALF], NN) * SCALE).astype(BF16)
        k_t[e, WIN:] = mm(xv[e], w_t[:, HALF : 2 * HALF], NN).astype(BF16)
        v_t[e, WIN:] = mm(xv[e], w_t[:, 2 * HALF :], NN).astype(BF16)
        g_t[e] = mm(cv[e], wo[HALF:, :], NT).astype(BF16)
        return carry

    lax.fori_loop(0, elecs, project_time, 0)

    def time_block(e, c, bias):
        rows, keys = slice(c * WIN, (c + 1) * WIN), slice(c * WIN, (c + 2) * WIN)
        att, dq, dk, dv = temporal_block(q_t[e, rows], g_t[e, rows], k_t[e, keys], v_t[e, keys], bias, *masks)
        att_t[e, rows] = att.astype(BF16)
        dq_t[e, rows] = dq.astype(BF16)
        return dk, dv

    def later_blocks(e, first_done):
        ones = time_block(e, 1, None)
        twos = time_block(e, 2, None)
        for ref, one, two in zip((dk_t, dv_t), ones, twos):
            if first_done:
                ref[e, :WIN] += one[:WIN]
            else:
                ref[e, :WIN] = one[:WIN]
            ref[e, WIN : 2 * WIN] = one[WIN:] + two[:WIN]
            ref[e, 2 * WIN :] = two[WIN:]

    def first_block(e, first_done):
        k_t[e, :WIN] = mm(halo[e], w_t[:, HALF : 2 * HALF], NN).astype(BF16)
        v_t[e, :WIN] = mm(halo[e], w_t[:, 2 * HALF :], NN).astype(BF16)
        for side, (ref, grad) in enumerate(zip((dk_t, dv_t), time_block(e, 0, bias0))):
            back_out[side, e] = grad[:WIN].astype(BF16)
            if first_done:
                ref[e, :WIN] = grad[WIN:]
            else:
                ref[e, :WIN] += grad[WIN:]

    def first_pair(i, carry):
        first_block(2 + 2 * i, True)
        first_block(3 + 2 * i, True)
        return carry

    def later_one(e, carry):
        later_blocks(e, True)
        return carry

    later_blocks(0, False)
    later_blocks(1, False)
    halo_copy.wait_recv()
    first_block(0, False)
    first_block(1, False)
    lax.fori_loop(0, elecs // 2 - 1, first_pair, 0)
    back_sems = halo_send.at[1], halo_recv.at[1]
    push(back_out, back_in, back_sems, left)
    back_copy = group(back_in, back_sems)
    lax.fori_loop(2, elecs, later_one, 0)
    send_raw(1)

    def span(c):
        return slice(STARTS[c], STARTS[c] + CHUNKS[c]), 4 * elecs * CHUNKS[c]

    def spatial_project(c):
        for k in range(2):
            go[c, k].wait_recv()
        here, rows = span(c)
        xi = xr[:, here].reshape(rows, width)
        shape = (4 * elecs, CHUNKS[c], HALF)
        q_s[:, : CHUNKS[c]] = (mm(xi, w_s[:, :HALF], NN) * SCALE).reshape(shape)
        k_s[:, : CHUNKS[c]] = mm(xi, w_s[:, HALF : 2 * HALF], NN).reshape(shape)
        v_s[:, : CHUNKS[c]] = mm(xi, w_s[:, 2 * HALF :], NN).reshape(shape)
        g_s[:, : CHUNKS[c]] = mm(cr[:, here].reshape(rows, width), wo[:HALF, :], NT).reshape(shape)

    def spatial_attend(c):
        def block(i, carry):
            for j in range(2):
                at = pl.ds(pl.multiple_of(i * 16 + j * 8, 8), 8)
                q, g, k, v = [ref[:, at, :].reshape(WIN, HALF).astype(BF16) for ref in (q_s, g_s, k_s, v_s)]
                for ref, value in zip((g_s, q_s, k_s, v_s), spatial_block(q, g, k, v, apart)):
                    ref[:, at, :] = value.reshape(4 * elecs, 8, HALF)
            return carry

        lax.fori_loop(0, CHUNKS[c] // 16, block, 0)

    def spatial_end(c):
        here, rows = span(c)
        xi = xr[:, here].reshape(rows, width)
        grads = jnp.concatenate(
            [ref[:, : CHUNKS[c]].astype(BF16).reshape(rows, HALF) for ref in (q_s, k_s, v_s)], axis=1
        )
        dxs[:, here] = mm(grads, w_s[...], NT).astype(BF16).reshape(4 * elecs, CHUNKS[c], width)
        add_in = mm(xi, grads, TN)
        att = g_s[:, : CHUNKS[c]].astype(BF16).reshape(rows, HALF)
        add_out = mm(att, cr[:, here].reshape(rows, width), TN)
        if c == 0:
            acc_in_s[...] = add_in
            acc_out_s[...] = add_out
        else:
            acc_in_s[...] += add_in
            acc_out_s[...] += add_out

    returned = {}

    def send_back(c):
        here, _ = span(c)
        sems = ret_send.at[c], ret_recv.at[c]
        for d in (2, 1, 3):
            push(dxs.at[d * elecs : (d + 1) * elecs, here], dxr.at[d - 1, :, here], sems, peer(y=4 - d))
        returned[c] = group(dxr.at[:, :, here], sems)

    def place(c):
        here, _ = span(c)
        returned[c].wait_recv()
        for d in range(4):
            at = rows_at(lax.rem(y + d, 4) * quarter + STARTS[c], CHUNKS[c])
            if d == 0:
                piece = dxs[:elecs, here]
            else:
                piece = dxr[d - 1, :, here]
            out[:, at, :] = (dx_t[:, at, :] + piece.astype(F32)).astype(BF16)

    def summing(n):
        def sems(p, step):
            return ar_send.at[n, p, step], ar_recv.at[n, p, step]

        def spot_of(p, d=0):
            return ar_out.at[n, p, rows_at(core * 1024 + lax.rem(where[orders[p][0]] + d, 4) * 256, 256)]

        waiting, last = [None, None], [None, None]
        for p in range(2):
            push(ar_src.at[n, p, rows_at((1 - core) * 1024, 1024)], recv_c.at[n, p], sems(p, 0), peer(core=1))
            waiting[p] = group(recv_c.at[n, p], sems(p, 0))
        yield
        for p, (a, b) in enumerate(orders):
            waiting[p].wait_recv()
            part_c[n, p] = (
                ar_src[n, p, rows_at(core * 1024, 1024)].astype(F32) + recv_c[n, p].astype(F32)
            ).astype(BF16)
            for d, by in on_axis(a):
                at = rows_at(lax.rem(where[a] + d, 4) * 256, 256)
                push(part_c.at[n, p, at], recv_a.at[n, p, d - 1], sems(p, 1), peer(**by))
            waiting[p] = group(recv_a.at[n, p], sems(p, 1))
        yield
        for p, (a, b) in enumerate(orders):
            waiting[p].wait_recv()
            total = part_c[n, p, rows_at(where[a] * 256, 256)].astype(F32)
            for i in range(3):
                total = total + recv_a[n, p, i].astype(F32)
            part[n, p] = total.astype(BF16)
            for i, by in on_plane(b):
                at = rows_at((lax.rem(where[b] + by[b], 4) * 4 + lax.rem(y + by["y"], 4)) * 16, 16)
                push(part.at[n, p, at], recv_b.at[n, p, i - 1], sems(p, 2), peer(**by))
            waiting[p] = group(recv_b.at[n, p], sems(p, 2))
        yield
        for p, (a, b) in enumerate(orders):
            waiting[p].wait_recv()
            mine = (where[b] * 4 + y) * 16
            total = part[n, p, rows_at(mine, 16)].astype(F32)
            for i in range(15):
                total = total + recv_b[n, p, i].astype(F32)
            at = rows_at(core * 1024 + where[a] * 256 + mine, 16)
            ar_out[n, p, at] = total.astype(BF16)
            for _, by in on_plane(b):
                push(ar_out.at[n, p, at], ar_out.at[n, p, at], sems(p, 3), peer(**by))
            waiting[p] = group(ar_out.at[n, p, :240], sems(p, 3))
        yield
        for p, (a, b) in enumerate(orders):
            waiting[p].wait_recv()
            for _, by in on_axis(a):
                push(spot_of(p), spot_of(p), sems(p, 4), peer(**by))
            waiting[p] = group(ar_out.at[n, p, :768], sems(p, 4))
            push(spot_of(p), spot_of(p), sems(p, 5), peer(core=1))
        yield
        for p in range(2):
            waiting[p].wait_recv()
            for d in range(1, 4):
                push(spot_of(p, d), spot_of(p, d), sems(p, 5), peer(core=1))
            waiting[p] = group(ar_out.at[n, p, :1024], sems(p, 5))
        yield
        for p in range(2):
            waiting[p].wait_recv()
            first = (1 - n) * HALF + p * 128
            for i in range(3):
                w_outs[i][:, first : first + 128] = ar_out[n, p, i * 512 : (i + 1) * 512]
            for i in range(2):
                low, column = (1 - n) * HALF, i * HALF + p * 128
                w_outs[3][low : low + HALF, column : column + 128] = ar_out[
                    n, p, 1536 + i * HALF : 1536 + (i + 1) * HALF
                ]
        yield

    back_copy.wait_recv()
    acc_in_t[...] = jnp.zeros_like(acc_in_t)
    acc_out_t[...] = jnp.zeros_like(acc_out_t)

    def end_time(e, carry):
        def full(own, side):
            tail = own[e, patches - WIN :] + back_in[side, e].astype(F32)
            return jnp.concatenate([own[e, : patches - WIN].astype(BF16), tail.astype(BF16)], axis=0)

        grads = jnp.concatenate([dq_t[e], full(dk_t, 0), full(dv_t, 1)], axis=1)
        dx_t[e] = mm(grads, w_t[...], NT)
        acc_in_t[...] += mm(xv[e], grads, TN)
        acc_out_t[...] += mm(att_t[e], cv[e], TN)
        return carry

    lax.fori_loop(0, elecs, end_time, 0)
    weight_rows(acc_in_t, acc_out_t, ar_src.at[0])
    time_sum, space_sum = summing(0), summing(1)
    next(time_sum)
    spatial_project(0)
    next(time_sum)
    spatial_attend(0)
    next(time_sum)
    send_raw(2)
    spatial_end(0)
    spatial_project(1)
    next(time_sum)
    spatial_attend(1)
    spatial_end(1)
    spatial_project(2)
    next(time_sum)
    send_back(0)
    spatial_attend(2)
    spatial_end(2)
    weight_rows(acc_in_s, acc_out_s, ar_src.at[1])
    next(space_sum)
    next(time_sum)
    next(space_sum)
    send_back(2)
    next(time_sum)
    next(space_sum)
    place(0)
    next(space_sum)
    send_back(1)
    place(2)
    next(space_sum)
    next(space_sum)
    place(1)
    next(space_sum)
    for whole in pending:
        whole.wait_send()


def end_kernel(dx, g0, g1, g2, g3, out, o0, o1, o2, o3):
    out[...] = dx[...]
    for grad, o in zip((g0, g1, g2, g3), (o0, o1, o2, o3)):
        o[...] = grad[...].astype(F32) * (1.0 / math.sqrt(196608))


def sds(shape, dtype):
    return jax.ShapeDtypeStruct(shape, dtype)


def shards(inputs, cotangent, w_query, w_key, w_value, w_out):
    _, elecs, patches, width = inputs.shape
    quarter = patches // 4
    vm, dma = pltpu.VMEM, pltpu.SemaphoreType.DMA
    tokens = (elecs, patches)
    ext = (elecs, patches + WIN)
    everyone = (4 * elecs, quarter)
    scratch = (
        [vm(tokens + (width,), BF16)] * 2
        + [vm((elecs, WIN, width), BF16)]
        + [vm((width, 3 * HALF), BF16)] * 2
        + [vm((width, width), BF16)]
        + [vm(tokens + (HALF,), BF16), vm(ext + (HALF,), BF16), vm(ext + (HALF,), BF16), vm(tokens + (HALF,), BF16)]
        + [vm(tokens + (HALF,), F32)] * 2
        + [vm(tokens + (HALF,), BF16)] * 2
        + [vm((2, elecs, WIN, HALF), BF16)] * 2
        + [vm(tokens + (width,), F32)]
        + [vm(everyone + (width,), BF16)] * 2
        + [vm((4 * elecs, CHUNKS[0], HALF), F32)] * 4
        + [vm(everyone + (width,), BF16), vm((3, elecs, quarter, width), BF16)]
        + [vm((width, 3 * HALF), F32), vm((HALF, width), F32)] * 2
        + [vm((2, 2, 2048, 128), BF16)]
        + [vm((2, 2, 1024, 128), BF16)] * 2
        + [vm((2, 2, 3, 256, 128), BF16), vm((2, 2, 256, 128), BF16), vm((2, 2, 15, 16, 128), BF16)]
        + [vm((2, 2, 2048, 128), BF16)]
        + [vm((WIN, HEADS * WIN), t) for t in (F32, BF16, BF16, F32)]
        + [dma((11,)), dma((2,)), dma((2,))]
        + [dma((3, 2))] * 2
        + [dma((3,))] * 2
        + [dma((2, 2, 6))] * 2
    )
    grad_inputs, *grads = pl.pallas_call(
        layer_kernel,
        out_shape=(sds(tokens + (width,), BF16),) + (sds((width, width), BF16),) * 4,
        in_specs=[pl.BlockSpec(memory_space=pl.ANY)] * 6,
        out_specs=(pl.BlockSpec(memory_space=pltpu.VMEM),) * 5,
        scratch_shapes=scratch,
        compiler_params=pltpu.CompilerParams(
            collective_id=0, has_side_effects=True, vmem_limit_bytes=VMEM_LIMIT
        ),
        cost_estimate=pl.CostEstimate(flops=2 * 10**10, bytes_accessed=10**7, transcendentals=2 * 10**6),
    )(inputs[0], cotangent[0], w_query, w_key, w_value, w_out)
    grad_inputs, *grads = pl.pallas_call(
        end_kernel,
        out_shape=(sds(tokens + (width,), BF16),) + (sds((width, width), F32),) * 4,
        in_specs=[pl.BlockSpec(memory_space=pltpu.VMEM)] * 5,
        out_specs=(pl.BlockSpec(memory_space=pltpu.VMEM),) * 5,
        compiler_params=pltpu.CompilerParams(vmem_limit_bytes=VMEM_LIMIT),
    )(grad_inputs, *grads)
    return (grad_inputs[None],) + tuple(grads)


def solution(mesh):
    return jax.shard_map(
        shards,
        mesh=mesh,
        in_specs=(P("dp", "elec", "tm", None), P("dp", "elec", "tm", None), P(), P(), P(), P()),
        out_specs=(P("dp", "elec", "tm", None), P(), P(), P(), P()),
        check_vma=False,
    )
```

```python
import math

import jax
import jax.numpy as jnp
from jax import lax
from jax.experimental import pallas as pl
from jax.experimental.pallas import tpu as pltpu
from jax.sharding import PartitionSpec as P

BF16 = jnp.bfloat16
F32 = jnp.float32
WIN = 128
HALF = 256
HEAD = 64
HEADS = 4
NEG = -1e30
SCALE = 0.125
VMEM_LIMIT = 56 * 1024 * 1024
MESH = pl.DeviceIdType.MESH

NN = (((1,), (0,)), ((), ()))
NT = (((1,), (1,)), ((), ()))
TN = (((0,), (0,)), ((), ()))


def mm(left, right, dims):
    return lax.dot_general(left, right, dims, preferred_element_type=F32)


def stack_heads(rows):
    column = lax.broadcasted_iota(jnp.int32, (1, HALF), 1)
    keeps = [(column >= h * HEAD) & (column < (h + 1) * HEAD) for h in range(HEADS)]
    return jnp.concatenate([rows * keep.astype(F32).astype(BF16) for keep in keeps], axis=0)


def pick_heads(rows):
    r = rows.shape[0] // HEADS
    even = lax.broadcasted_iota(jnp.int32, (r, 128), 1) < HEAD
    return jnp.concatenate(
        [
            jnp.where(even, rows[:r, :128], rows[r : 2 * r, :128]),
            jnp.where(even, rows[2 * r : 3 * r, 128:], rows[3 * r :, 128:]),
        ],
        axis=1,
    )


def soft(scores, grad_probs):
    ex = jnp.exp(scores - jnp.max(scores, axis=0, keepdims=True))
    probs = ex * (1.0 / jnp.sum(ex, axis=0, keepdims=True))
    delta = jnp.sum(probs * grad_probs, axis=0, keepdims=True)
    return probs.astype(BF16), (probs * (grad_probs - delta)).astype(BF16)


def make_masks(older, older_low, newer_low, apart):
    row = lax.broadcasted_iota(jnp.int32, (WIN, WIN), 0)
    column = lax.broadcasted_iota(jnp.int32, (WIN, WIN), 1)
    old = (row > column).astype(F32)
    far = jnp.where(lax.rem(row, 8) == lax.rem(column, 8), 0.0, NEG).astype(F32)
    for h in range(HEADS):
        at = slice(h * WIN, (h + 1) * WIN)
        older[:, at] = old
        older_low[:, at] = old.astype(BF16)
        newer_low[:, at] = (1.0 - old).astype(BF16)
        apart[:, at] = far


def temporal_block(q, ga, k, v, bias, older, older_low, newer_low):
    qs, gs = stack_heads(q), stack_heads(ga)
    st = mm(k, qs, NT)
    gt = mm(v, gs, NT)
    old = older[...] > 0.5
    early = st[:WIN] if bias is None else st[:WIN] + bias
    probs, grad = soft(jnp.where(old, early, st[WIN:]), jnp.where(old, gt[:WIN], gt[WIN:]))
    pt = jnp.concatenate([probs * older_low[...], probs * newer_low[...]], axis=0)
    dt = jnp.concatenate([grad * older_low[...], grad * newer_low[...]], axis=0)
    att = pick_heads(mm(pt, v, TN))
    dq = pick_heads(mm(dt, k, TN)) * SCALE
    return att, dq, mm(dt, qs, NN), mm(pt, gs, NN)


def spatial_block(q, ga, k, v, apart):
    qs, gs = stack_heads(q), stack_heads(ga)
    pt, dt = soft(mm(k, qs, NT) + apart[...], mm(v, gs, NT))
    att = pick_heads(mm(pt, v, TN))
    dq = pick_heads(mm(dt, k, TN)) * SCALE
    return att, dq, mm(dt, qs, NN), mm(pt, gs, NN)


def coordinates():
    dp, tm, y = lax.axis_index("dp"), lax.axis_index("tm"), lax.axis_index("elec")
    z, rest = lax.div(tm, 4), lax.rem(tm, 4)
    x = lax.div(rest, 2) * 2 + dp
    return x, y, z, lax.rem(rest, 2)


def device_at(x, y, z, core):
    return {"dp": lax.rem(x, 2), "tm": z * 4 + lax.div(x, 2) * 2 + core, "elec": y}


CHUNKS = (48, 32, 16)
STARTS = (0, 48, 80)


def weight_rows(acc_in, acc_out, dst):
    for j in range(2):
        for i in range(3):
            first = i * HALF + j * 128
            dst[j, i * 512 : (i + 1) * 512] = acc_in[:, first : first + 128].astype(BF16)
        for i in range(2):
            first = i * HALF + j * 128
            dst[j, 1536 + i * HALF : 1536 + (i + 1) * HALF] = acc_out[:, first : first + 128].astype(BF16)


def layer_kernel(x_h, cot_h, wq_h, wk_h, wv_h, wo_h, out, *rest):
    w_outs = rest[:4]
    (
        xv, cv, halo, w_t, w_s, wo, q_t, k_t, v_t, g_t, dk_t, dv_t, att_t, dq_t, back_out, back_in, dx_t,
        xr, cr, q_s, k_s, v_s, g_s, dxs, dxr, acc_in_t, acc_out_t, acc_in_s, acc_out_s,
        ar_src, recv_c, part_c, recv_a, part, recv_b, ar_out, older, older_low, newer_low, apart, via, via_back,
        load_sem, halo_send, halo_recv, go_send, go_recv, ret_send, ret_recv, ar_send, ar_recv, via_send, via_recv,
    ) = rest[4:]
    elecs, patches, width = xv.shape
    quarter = patches // 4
    x, y, z, core = coordinates()
    tm = lax.axis_index("tm")
    right = {"tm": lax.rem(tm + 1, 16)}
    left = {"tm": lax.rem(tm + 15, 16)}
    where = {"x": x, "y": y, "z": z, "core": core}

    def peer(**by):
        at = {n: lax.rem(where[n] + by.get(n, 0), 2 if n == "core" else 4) for n in where}
        return device_at(at["x"], at["y"], at["z"], at["core"])

    orders = (("x", "z"), ("z", "x"))

    def on_axis(a):
        return [(d, {a: d}) for d in range(1, 4)]

    def on_plane(b):
        return [(i, {b: i // 4, "y": i % 4}) for i in range(1, 16)]

    loads = []

    def load(src, dst):
        copy = pltpu.make_async_copy(src, dst, load_sem.at[len(loads)])
        copy.start()
        loads.append(copy)

    load(x_h, xv)
    load(cot_h, cv)
    load(wo_h, wo)
    for i, w in enumerate((wq_h, wk_h, wv_h)):
        load(w.at[:, HALF:], w_t.at[:, i * HALF : (i + 1) * HALF])
    for i, w in enumerate((wq_h, wk_h, wv_h)):
        load(w.at[:, :HALF], w_s.at[:, i * HALF : (i + 1) * HALF])
    at = pl.ds(pl.multiple_of(y * quarter, 16), quarter)
    load(x_h.at[:, at], xr.at[:elecs])
    load(cot_h.at[:, at], cr.at[:elecs])

    near = {tuple((n, v) for n, v in by.items() if v) for b in "xz" for _, by in on_plane(b)}
    near = [(("core", 1),)] + sorted(near)
    barrier = pltpu.get_barrier_semaphore()
    for device in [right, left] + [peer(**dict(by)) for by in near]:
        pl.semaphore_signal(barrier, inc=1, device_id=device, device_id_type=MESH)
    pl.semaphore_wait(barrier, 2 + len(near))

    pending = []

    def push(src, dst, sems, device):
        pltpu.make_async_remote_copy(
            src_ref=src, dst_ref=dst, send_sem=sems[0], recv_sem=sems[1], device_id=device, device_id_type=MESH
        ).start()

    def group(ref, sems):
        whole = pltpu.make_async_remote_copy(
            src_ref=ref, dst_ref=ref, send_sem=sems[0], recv_sem=sems[1], device_id=right, device_id_type=MESH
        )
        pending.append(whole)
        return whole

    def rows_at(first, size):
        return pl.ds(pl.multiple_of(first, 16), size)

    loads[0].wait()
    loads[1].wait()
    halo_sems = halo_send.at[0], halo_recv.at[0]
    push(xv.at[:, patches - WIN :], halo, halo_sems, right)
    halo_copy = group(halo, halo_sems)
    go = {}

    ways = (1, 3)
    hops = {}

    def send_raw(c):
        here = slice(STARTS[c], STARTS[c] + CHUNKS[c])

        def part(src, d):
            return src.at[:, rows_at(lax.rem(y + d, 4) * quarter + STARTS[c], CHUNKS[c])]

        for k, src in enumerate((xv, cv)):
            sems = via_send.at[0, c, k], via_recv.at[0, c, k]
            push(part(src, 2), via.at[k, :, here], sems, peer(y=ways[k]))
            hops[c, k] = group(via.at[k, :, here], sems)
        for k, (src, dst) in enumerate(((xv, xr), (cv, cr))):
            sems = go_send.at[c, k], go_recv.at[c, k]
            for d in (1, 3):
                push(part(src, d), dst.at[d * elecs : (d + 1) * elecs, here], sems, peer(y=d))
            go[c, k] = group(dst.at[elecs:, here], sems)

    def pass_raw(c):
        here = slice(STARTS[c], STARTS[c] + CHUNKS[c])
        for k, dst in enumerate((xr, cr)):
            hops[c, k].wait_recv()
            sems = go_send.at[c, k], go_recv.at[c, k]
            push(via.at[k, :, here], dst.at[2 * elecs : 3 * elecs, here], sems, peer(y=ways[k]))

    send_raw(0)
    masks = older, older_low, newer_low
    make_masks(*masks, apart)
    for copy in loads[2:]:
        copy.wait()

    bias0 = jnp.where(tm == 0, NEG, 0.0).astype(F32)

    def project_time(e, carry):
        q_t[e] = (mm(xv[e], w_t[:, :HALF], NN) * SCALE).astype(BF16)
        k_t[e, WIN:] = mm(xv[e], w_t[:, HALF : 2 * HALF], NN).astype(BF16)
        v_t[e, WIN:] = mm(xv[e], w_t[:, 2 * HALF :], NN).astype(BF16)
        g_t[e] = mm(cv[e], wo[HALF:, :], NT).astype(BF16)
        return carry

    lax.fori_loop(0, elecs, project_time, 0)

    def time_block(e, c, bias):
        rows, keys = slice(c * WIN, (c + 1) * WIN), slice(c * WIN, (c + 2) * WIN)
        att, dq, dk, dv = temporal_block(q_t[e, rows], g_t[e, rows], k_t[e, keys], v_t[e, keys], bias, *masks)
        att_t[e, rows] = att.astype(BF16)
        dq_t[e, rows] = dq.astype(BF16)
        return dk, dv

    def later_blocks(e, first_done):
        ones = time_block(e, 1, None)
        twos = time_block(e, 2, None)
        for ref, one, two in zip((dk_t, dv_t), ones, twos):
            if first_done:
                ref[e, :WIN] += one[:WIN]
            else:
                ref[e, :WIN] = one[:WIN]
            ref[e, WIN : 2 * WIN] = one[WIN:] + two[:WIN]
            ref[e, 2 * WIN :] = two[WIN:]

    def first_block(e, first_done):
        k_t[e, :WIN] = mm(halo[e], w_t[:, HALF : 2 * HALF], NN).astype(BF16)
        v_t[e, :WIN] = mm(halo[e], w_t[:, 2 * HALF :], NN).astype(BF16)
        for side, (ref, grad) in enumerate(zip((dk_t, dv_t), time_block(e, 0, bias0))):
            back_out[side, e] = grad[:WIN].astype(BF16)
            if first_done:
                ref[e, :WIN] = grad[WIN:]
            else:
                ref[e, :WIN] += grad[WIN:]

    def first_pair(i, carry):
        first_block(2 + 2 * i, True)
        first_block(3 + 2 * i, True)
        return carry

    def later_one(e, carry):
        later_blocks(e, True)
        return carry

    later_blocks(0, False)
    later_blocks(1, False)
    halo_copy.wait_recv()
    pass_raw(0)
    first_block(0, False)
    first_block(1, False)
    lax.fori_loop(0, elecs // 2 - 1, first_pair, 0)
    back_sems = halo_send.at[1], halo_recv.at[1]
    push(back_out, back_in, back_sems, left)
    back_copy = group(back_in, back_sems)
    lax.fori_loop(2, elecs, later_one, 0)
    send_raw(1)

    def span(c):
        return slice(STARTS[c], STARTS[c] + CHUNKS[c]), 4 * elecs * CHUNKS[c]

    def spatial_project(c):
        for k in range(2):
            go[c, k].wait_recv()
        here, rows = span(c)
        xi = xr[:, here].reshape(rows, width)
        shape = (4 * elecs, CHUNKS[c], HALF)
        q_s[:, : CHUNKS[c]] = (mm(xi, w_s[:, :HALF], NN) * SCALE).reshape(shape)
        k_s[:, : CHUNKS[c]] = mm(xi, w_s[:, HALF : 2 * HALF], NN).reshape(shape)
        v_s[:, : CHUNKS[c]] = mm(xi, w_s[:, 2 * HALF :], NN).reshape(shape)
        g_s[:, : CHUNKS[c]] = mm(cr[:, here].reshape(rows, width), wo[:HALF, :], NT).reshape(shape)

    def spatial_attend(c):
        def block(i, carry):
            for j in range(2):
                at = pl.ds(pl.multiple_of(i * 16 + j * 8, 8), 8)
                q, g, k, v = [ref[:, at, :].reshape(WIN, HALF).astype(BF16) for ref in (q_s, g_s, k_s, v_s)]
                for ref, value in zip((g_s, q_s, k_s, v_s), spatial_block(q, g, k, v, apart)):
                    ref[:, at, :] = value.reshape(4 * elecs, 8, HALF)
            return carry

        lax.fori_loop(0, CHUNKS[c] // 16, block, 0)

    def spatial_end(c):
        here, rows = span(c)
        xi = xr[:, here].reshape(rows, width)
        grads = jnp.concatenate(
            [ref[:, : CHUNKS[c]].astype(BF16).reshape(rows, HALF) for ref in (q_s, k_s, v_s)], axis=1
        )
        dxs[:, here] = mm(grads, w_s[...], NT).astype(BF16).reshape(4 * elecs, CHUNKS[c], width)
        add_in = mm(xi, grads, TN)
        att = g_s[:, : CHUNKS[c]].astype(BF16).reshape(rows, HALF)
        add_out = mm(att, cr[:, here].reshape(rows, width), TN)
        if c == 0:
            acc_in_s[...] = add_in
            acc_out_s[...] = add_out
        else:
            acc_in_s[...] += add_in
            acc_out_s[...] += add_out

    returned, hops_back = {}, {}

    def send_back(c):
        here, _ = span(c)
        for k in range(2):
            first = 2 * elecs + k * (elecs // 2)
            sems = via_send.at[1, c, k], via_recv.at[1, c, k]
            push(dxs.at[first : first + elecs // 2, here], via_back.at[k, :, here], sems, peer(y=ways[k]))
            hops_back[c, k] = group(via_back.at[k, :, here], sems)
        sems = ret_send.at[c], ret_recv.at[c]
        for d in (1, 3):
            push(dxs.at[d * elecs : (d + 1) * elecs, here], dxr.at[d - 1, :, here], sems, peer(y=4 - d))
        returned[c] = group(dxr.at[:, :, here], sems)

    def pass_back(c):
        here, _ = span(c)
        for k in range(2):
            hops_back[c, k].wait_recv()
            half = slice(k * (elecs // 2), (k + 1) * (elecs // 2))
            sems = ret_send.at[c], ret_recv.at[c]
            push(via_back.at[k, :, here], dxr.at[1, half, here], sems, peer(y=ways[k]))

    def place(c):
        here, _ = span(c)
        returned[c].wait_recv()
        for d in range(4):
            at = rows_at(lax.rem(y + d, 4) * quarter + STARTS[c], CHUNKS[c])
            if d == 0:
                piece = dxs[:elecs, here]
            else:
                piece = dxr[d - 1, :, here]
            out[:, at, :] = (dx_t[:, at, :] + piece.astype(F32)).astype(BF16)

    def summing(n):
        def sems(p, step):
            return ar_send.at[n, p, step], ar_recv.at[n, p, step]

        def spot_of(p, d=0):
            return ar_out.at[n, p, rows_at(core * 1024 + lax.rem(where[orders[p][0]] + d, 4) * 256, 256)]

        waiting, last = [None, None], [None, None]
        for p in range(2):
            push(ar_src.at[n, p, rows_at((1 - core) * 1024, 1024)], recv_c.at[n, p], sems(p, 0), peer(core=1))
            waiting[p] = group(recv_c.at[n, p], sems(p, 0))
        yield
        for p, (a, b) in enumerate(orders):
            waiting[p].wait_recv()
            part_c[n, p] = (
                ar_src[n, p, rows_at(core * 1024, 1024)].astype(F32) + recv_c[n, p].astype(F32)
            ).astype(BF16)
            for d, by in on_axis(a):
                at = rows_at(lax.rem(where[a] + d, 4) * 256, 256)
                push(part_c.at[n, p, at], recv_a.at[n, p, d - 1], sems(p, 1), peer(**by))
            waiting[p] = group(recv_a.at[n, p], sems(p, 1))
        yield
        for p, (a, b) in enumerate(orders):
            waiting[p].wait_recv()
            total = part_c[n, p, rows_at(where[a] * 256, 256)].astype(F32)
            for i in range(3):
                total = total + recv_a[n, p, i].astype(F32)
            part[n, p] = total.astype(BF16)
            for i, by in on_plane(b):
                at = rows_at((lax.rem(where[b] + by[b], 4) * 4 + lax.rem(y + by["y"], 4)) * 16, 16)
                push(part.at[n, p, at], recv_b.at[n, p, i - 1], sems(p, 2), peer(**by))
            waiting[p] = group(recv_b.at[n, p], sems(p, 2))
        yield
        for p, (a, b) in enumerate(orders):
            waiting[p].wait_recv()
            mine = (where[b] * 4 + y) * 16
            total = part[n, p, rows_at(mine, 16)].astype(F32)
            for i in range(15):
                total = total + recv_b[n, p, i].astype(F32)
            at = rows_at(core * 1024 + where[a] * 256 + mine, 16)
            ar_out[n, p, at] = total.astype(BF16)
            for _, by in on_plane(b):
                push(ar_out.at[n, p, at], ar_out.at[n, p, at], sems(p, 3), peer(**by))
            waiting[p] = group(ar_out.at[n, p, :240], sems(p, 3))
        yield
        for p, (a, b) in enumerate(orders):
            waiting[p].wait_recv()
            for _, by in on_axis(a):
                push(spot_of(p), spot_of(p), sems(p, 4), peer(**by))
            waiting[p] = group(ar_out.at[n, p, :768], sems(p, 4))
            push(spot_of(p), spot_of(p), sems(p, 5), peer(core=1))
        yield
        for p in range(2):
            waiting[p].wait_recv()
            for d in range(1, 4):
                push(spot_of(p, d), spot_of(p, d), sems(p, 5), peer(core=1))
            waiting[p] = group(ar_out.at[n, p, :1024], sems(p, 5))
        yield
        for p in range(2):
            waiting[p].wait_recv()
            first = (1 - n) * HALF + p * 128
            for i in range(3):
                w_outs[i][:, first : first + 128] = ar_out[n, p, i * 512 : (i + 1) * 512]
            for i in range(2):
                low, column = (1 - n) * HALF, i * HALF + p * 128
                w_outs[3][low : low + HALF, column : column + 128] = ar_out[
                    n, p, 1536 + i * HALF : 1536 + (i + 1) * HALF
                ]
        yield

    back_copy.wait_recv()
    acc_in_t[...] = jnp.zeros_like(acc_in_t)
    acc_out_t[...] = jnp.zeros_like(acc_out_t)

    def end_time(e, carry):
        def full(own, side):
            tail = own[e, patches - WIN :] + back_in[side, e].astype(F32)
            return jnp.concatenate([own[e, : patches - WIN].astype(BF16), tail.astype(BF16)], axis=0)

        grads = jnp.concatenate([dq_t[e], full(dk_t, 0), full(dv_t, 1)], axis=1)
        dx_t[e] = mm(grads, w_t[...], NT)
        acc_in_t[...] += mm(xv[e], grads, TN)
        acc_out_t[...] += mm(att_t[e], cv[e], TN)
        return carry

    lax.fori_loop(0, elecs, end_time, 0)
    weight_rows(acc_in_t, acc_out_t, ar_src.at[0])
    time_sum, space_sum = summing(0), summing(1)
    next(time_sum)
    spatial_project(0)
    next(time_sum)
    pass_raw(1)
    spatial_attend(0)
    next(time_sum)
    send_raw(2)
    spatial_end(0)
    spatial_project(1)
    pass_raw(2)
    next(time_sum)
    spatial_attend(1)
    spatial_end(1)
    spatial_project(2)
    next(time_sum)
    send_back(0)
    spatial_attend(2)
    spatial_end(2)
    weight_rows(acc_in_s, acc_out_s, ar_src.at[1])
    next(space_sum)
    pass_back(0)
    next(time_sum)
    send_back(2)
    next(space_sum)
    next(time_sum)
    pass_back(2)
    next(space_sum)
    place(0)
    next(space_sum)
    send_back(1)
    place(2)
    next(space_sum)
    pass_back(1)
    next(space_sum)
    place(1)
    next(space_sum)
    for whole in pending:
        whole.wait_send()


def end_kernel(dx, g0, g1, g2, g3, out, o0, o1, o2, o3):
    out[...] = dx[...]
    for grad, o in zip((g0, g1, g2, g3), (o0, o1, o2, o3)):
        o[...] = grad[...].astype(F32) * (1.0 / math.sqrt(196608))


def sds(shape, dtype):
    return jax.ShapeDtypeStruct(shape, dtype)


def shards(inputs, cotangent, w_query, w_key, w_value, w_out):
    _, elecs, patches, width = inputs.shape
    quarter = patches // 4
    vm, dma = pltpu.VMEM, pltpu.SemaphoreType.DMA
    tokens = (elecs, patches)
    ext = (elecs, patches + WIN)
    everyone = (4 * elecs, quarter)
    scratch = (
        [vm(tokens + (width,), BF16)] * 2
        + [vm((elecs, WIN, width), BF16)]
        + [vm((width, 3 * HALF), BF16)] * 2
        + [vm((width, width), BF16)]
        + [vm(tokens + (HALF,), BF16), vm(ext + (HALF,), BF16), vm(ext + (HALF,), BF16), vm(tokens + (HALF,), BF16)]
        + [vm(tokens + (HALF,), F32)] * 2
        + [vm(tokens + (HALF,), BF16)] * 2
        + [vm((2, elecs, WIN, HALF), BF16)] * 2
        + [vm(tokens + (width,), F32)]
        + [vm(everyone + (width,), BF16)] * 2
        + [vm((4 * elecs, CHUNKS[0], HALF), F32)] * 4
        + [vm(everyone + (width,), BF16), vm((3, elecs, quarter, width), BF16)]
        + [vm((width, 3 * HALF), F32), vm((HALF, width), F32)] * 2
        + [vm((2, 2, 2048, 128), BF16)]
        + [vm((2, 2, 1024, 128), BF16)] * 2
        + [vm((2, 2, 3, 256, 128), BF16), vm((2, 2, 256, 128), BF16), vm((2, 2, 15, 16, 128), BF16)]
        + [vm((2, 2, 2048, 128), BF16)]
        + [vm((WIN, HEADS * WIN), t) for t in (F32, BF16, BF16, F32)]
        + [vm((2, elecs, quarter, width), BF16), vm((2, elecs // 2, quarter, width), BF16)]
        + [dma((11,)), dma((2,)), dma((2,))]
        + [dma((3, 2))] * 2
        + [dma((3,))] * 2
        + [dma((2, 2, 6))] * 2
        + [dma((2, 3, 2))] * 2
    )
    grad_inputs, *grads = pl.pallas_call(
        layer_kernel,
        out_shape=(sds(tokens + (width,), BF16),) + (sds((width, width), BF16),) * 4,
        in_specs=[pl.BlockSpec(memory_space=pl.ANY)] * 6,
        out_specs=(pl.BlockSpec(memory_space=pltpu.VMEM),) * 5,
        scratch_shapes=scratch,
        compiler_params=pltpu.CompilerParams(
            collective_id=0, has_side_effects=True, vmem_limit_bytes=VMEM_LIMIT
        ),
        cost_estimate=pl.CostEstimate(flops=2 * 10**10, bytes_accessed=10**7, transcendentals=2 * 10**6),
    )(inputs[0], cotangent[0], w_query, w_key, w_value, w_out)
    grad_inputs, *grads = pl.pallas_call(
        end_kernel,
        out_shape=(sds(tokens + (width,), BF16),) + (sds((width, width), F32),) * 4,
        in_specs=[pl.BlockSpec(memory_space=pltpu.VMEM)] * 5,
        out_specs=(pl.BlockSpec(memory_space=pltpu.VMEM),) * 5,
        compiler_params=pltpu.CompilerParams(vmem_limit_bytes=VMEM_LIMIT),
    )(grad_inputs, *grads)
    return (grad_inputs[None],) + tuple(grads)


def solution(mesh):
    return jax.shard_map(
        shards,
        mesh=mesh,
        in_specs=(P("dp", "elec", "tm", None), P("dp", "elec", "tm", None), P(), P(), P(), P()),
        out_specs=(P("dp", "elec", "tm", None), P(), P(), P(), P()),
        check_vma=False,
    )
```

```python
import math

import jax
import jax.numpy as jnp
from jax import lax
from jax.experimental import pallas as pl
from jax.experimental.pallas import tpu as pltpu
from jax.sharding import PartitionSpec as P

BF16 = jnp.bfloat16
F32 = jnp.float32
WIN = 128
HALF = 256
HEAD = 64
HEADS = 4
NEG = -1e30
SCALE = 0.125
VMEM_LIMIT = 56 * 1024 * 1024
MESH = pl.DeviceIdType.MESH

NN = (((1,), (0,)), ((), ()))
NT = (((1,), (1,)), ((), ()))
TN = (((0,), (0,)), ((), ()))


def mm(left, right, dims):
    return lax.dot_general(left, right, dims, preferred_element_type=F32)


def stack_heads(rows):
    column = lax.broadcasted_iota(jnp.int32, (1, HALF), 1)
    keeps = [(column >= h * HEAD) & (column < (h + 1) * HEAD) for h in range(HEADS)]
    return jnp.concatenate([rows * keep.astype(F32).astype(BF16) for keep in keeps], axis=0)


def pick_heads(rows):
    r = rows.shape[0] // HEADS
    even = lax.broadcasted_iota(jnp.int32, (r, 128), 1) < HEAD
    return jnp.concatenate(
        [
            jnp.where(even, rows[:r, :128], rows[r : 2 * r, :128]),
            jnp.where(even, rows[2 * r : 3 * r, 128:], rows[3 * r :, 128:]),
        ],
        axis=1,
    )


def soft(scores, grad_probs):
    ex = jnp.exp(scores - jnp.max(scores, axis=0, keepdims=True))
    probs = ex * (1.0 / jnp.sum(ex, axis=0, keepdims=True))
    delta = jnp.sum(probs * grad_probs, axis=0, keepdims=True)
    return probs.astype(BF16), (probs * (grad_probs - delta)).astype(BF16)


def make_masks(older, older_low, newer_low, apart):
    row = lax.broadcasted_iota(jnp.int32, (WIN, WIN), 0)
    column = lax.broadcasted_iota(jnp.int32, (WIN, WIN), 1)
    old = (row > column).astype(F32)
    far = jnp.where(lax.rem(row, 8) == lax.rem(column, 8), 0.0, NEG).astype(F32)
    for h in range(HEADS):
        at = slice(h * WIN, (h + 1) * WIN)
        older[:, at] = old
        older_low[:, at] = old.astype(BF16)
        newer_low[:, at] = (1.0 - old).astype(BF16)
        apart[:, at] = far


def diagonal(cols):
    return jnp.concatenate(
        [cols[h * HEAD : (h + 1) * HEAD, h * WIN : (h + 1) * WIN] for h in range(HEADS)], axis=0
    )


def temporal_block(q, ga, k, v, k_cols, v_cols, bias, older, older_low, newer_low):
    qs, gs = stack_heads(q), stack_heads(ga)
    st = mm(k, qs, NT)
    gt = mm(v, gs, NT)
    old = older[...] > 0.5
    early = st[:WIN] if bias is None else st[:WIN] + bias
    probs, grad = soft(jnp.where(old, early, st[WIN:]), jnp.where(old, gt[:WIN], gt[WIN:]))
    pt = jnp.concatenate([probs * older_low[...], probs * newer_low[...]], axis=0)
    dt = jnp.concatenate([grad * older_low[...], grad * newer_low[...]], axis=0)
    att = diagonal(mm(v_cols, pt, NN)).astype(BF16)
    dq = (diagonal(mm(k_cols, dt, NN)) * SCALE).astype(BF16)
    return att, dq.T, mm(dt, qs, NN), mm(pt, gs, NN)


def spatial_block(q, ga, k, v, apart):
    qs, gs = stack_heads(q), stack_heads(ga)
    pt, dt = soft(mm(k, qs, NT) + apart[...], mm(v, gs, NT))
    att = pick_heads(mm(pt, v, TN))
    dq = pick_heads(mm(dt, k, TN)) * SCALE
    return att, dq, mm(dt, qs, NN), mm(pt, gs, NN)


def coordinates():
    dp, tm, y = lax.axis_index("dp"), lax.axis_index("tm"), lax.axis_index("elec")
    z, rest = lax.div(tm, 4), lax.rem(tm, 4)
    x = lax.div(rest, 2) * 2 + dp
    return x, y, z, lax.rem(rest, 2)


def device_at(x, y, z, core):
    return {"dp": lax.rem(x, 2), "tm": z * 4 + lax.div(x, 2) * 2 + core, "elec": y}


CHUNKS = (48, 32, 16)
STARTS = (0, 48, 80)


def weight_rows(acc_in, acc_out, dst):
    for j in range(2):
        for i in range(3):
            first = i * HALF + j * 128
            dst[j, i * 512 : (i + 1) * 512] = acc_in[:, first : first + 128].astype(BF16)
        for i in range(2):
            first = i * HALF + j * 128
            dst[j, 1536 + i * HALF : 1536 + (i + 1) * HALF] = acc_out[:, first : first + 128].astype(BF16)


def layer_kernel(x_h, cot_h, wq_h, wk_h, wv_h, wo_h, out, *rest):
    w_outs = rest[:4]
    (
        xv, cv, halo, w_t, w_s, wo, q_t, k_t, v_t, g_t, dk_t, dv_t, att_t, dq_t, kc_t, vc_t, back_out, back_in, dx_t,
        xr, cr, q_s, k_s, v_s, g_s, dxs, dxr, acc_in_t, acc_out_t, acc_in_s, acc_out_s,
        ar_src, recv_c, part_c, recv_a, part, recv_b, ar_out, older, older_low, newer_low, apart,
        load_sem, halo_send, halo_recv, go_send, go_recv, ret_send, ret_recv, ar_send, ar_recv,
    ) = rest[4:]
    elecs, patches, width = xv.shape
    quarter = patches // 4
    x, y, z, core = coordinates()
    tm = lax.axis_index("tm")
    right = {"tm": lax.rem(tm + 1, 16)}
    left = {"tm": lax.rem(tm + 15, 16)}
    where = {"x": x, "y": y, "z": z, "core": core}

    def peer(**by):
        at = {n: lax.rem(where[n] + by.get(n, 0), 2 if n == "core" else 4) for n in where}
        return device_at(at["x"], at["y"], at["z"], at["core"])

    orders = (("x", "z"), ("z", "x"))

    def on_axis(a):
        return [(d, {a: d}) for d in range(1, 4)]

    def on_plane(b):
        return [(i, {b: i // 4, "y": i % 4}) for i in range(1, 16)]

    loads = []

    def load(src, dst):
        copy = pltpu.make_async_copy(src, dst, load_sem.at[len(loads)])
        copy.start()
        loads.append(copy)

    load(x_h, xv)
    load(cot_h, cv)
    load(wo_h, wo)
    for i, w in enumerate((wq_h, wk_h, wv_h)):
        load(w.at[:, HALF:], w_t.at[:, i * HALF : (i + 1) * HALF])
    for i, w in enumerate((wq_h, wk_h, wv_h)):
        load(w.at[:, :HALF], w_s.at[:, i * HALF : (i + 1) * HALF])
    at = pl.ds(pl.multiple_of(y * quarter, 16), quarter)
    load(x_h.at[:, at], xr.at[:elecs])
    load(cot_h.at[:, at], cr.at[:elecs])

    near = {tuple((n, v) for n, v in by.items() if v) for b in "xz" for _, by in on_plane(b)}
    near = [(("core", 1),)] + sorted(near)
    barrier = pltpu.get_barrier_semaphore()
    for device in [right, left] + [peer(**dict(by)) for by in near]:
        pl.semaphore_signal(barrier, inc=1, device_id=device, device_id_type=MESH)
    pl.semaphore_wait(barrier, 2 + len(near))

    pending = []

    def push(src, dst, sems, device):
        pltpu.make_async_remote_copy(
            src_ref=src, dst_ref=dst, send_sem=sems[0], recv_sem=sems[1], device_id=device, device_id_type=MESH
        ).start()

    def group(ref, sems):
        whole = pltpu.make_async_remote_copy(
            src_ref=ref, dst_ref=ref, send_sem=sems[0], recv_sem=sems[1], device_id=right, device_id_type=MESH
        )
        pending.append(whole)
        return whole

    def rows_at(first, size):
        return pl.ds(pl.multiple_of(first, 16), size)

    loads[0].wait()
    loads[1].wait()
    halo_sems = halo_send.at[0], halo_recv.at[0]
    push(xv.at[:, patches - WIN :], halo, halo_sems, right)
    halo_copy = group(halo, halo_sems)
    go = {}

    def send_raw(c):
        here = slice(STARTS[c], STARTS[c] + CHUNKS[c])
        for k, (src, dst) in enumerate(((xv, xr), (cv, cr))):
            sems = go_send.at[c, k], go_recv.at[c, k]
            for d in (2, 1, 3):
                at = rows_at(lax.rem(y + d, 4) * quarter + STARTS[c], CHUNKS[c])
                push(src.at[:, at], dst.at[d * elecs : (d + 1) * elecs, here], sems, peer(y=d))
            go[c, k] = group(dst.at[elecs:, here], sems)

    send_raw(0)
    masks = older, older_low, newer_low
    make_masks(*masks, apart)
    for copy in loads[2:]:
        copy.wait()

    bias0 = jnp.where(tm == 0, NEG, 0.0).astype(F32)

    def project_time(e, carry):
        q_t[e] = (mm(xv[e], w_t[:, :HALF], NN) * SCALE).astype(BF16)
        for own, cols, i in ((k_t, kc_t, 1), (v_t, vc_t, 2)):
            t = mm(xv[e], w_t[:, i * HALF : (i + 1) * HALF], NN).astype(BF16)
            own[e, WIN:] = t
            cols[e, :, WIN:] = t.T
        g_t[e] = mm(cv[e], wo[HALF:, :], NT).astype(BF16)
        return carry

    lax.fori_loop(0, elecs, project_time, 0)

    def time_block(e, c, bias):
        rows, keys = slice(c * WIN, (c + 1) * WIN), slice(c * WIN, (c + 2) * WIN)
        att, dq, dk, dv = temporal_block(
            q_t[e, rows], g_t[e, rows], k_t[e, keys], v_t[e, keys], kc_t[e, :, keys], vc_t[e, :, keys], bias, *masks
        )
        att_t[e, :, rows] = att
        dq_t[e, rows] = dq
        return dk, dv

    def later_blocks(e, first_done):
        ones = time_block(e, 1, None)
        twos = time_block(e, 2, None)
        for ref, one, two in zip((dk_t, dv_t), ones, twos):
            if first_done:
                ref[e, :WIN] += one[:WIN]
            else:
                ref[e, :WIN] = one[:WIN]
            ref[e, WIN : 2 * WIN] = one[WIN:] + two[:WIN]
            ref[e, 2 * WIN :] = two[WIN:]

    def first_block(e, first_done):
        for own, cols, i in ((k_t, kc_t, 1), (v_t, vc_t, 2)):
            t = mm(halo[e], w_t[:, i * HALF : (i + 1) * HALF], NN).astype(BF16)
            own[e, :WIN] = t
            cols[e, :, :WIN] = t.T
        for side, (ref, grad) in enumerate(zip((dk_t, dv_t), time_block(e, 0, bias0))):
            back_out[side, e] = grad[:WIN].astype(BF16)
            if first_done:
                ref[e, :WIN] = grad[WIN:]
            else:
                ref[e, :WIN] += grad[WIN:]

    def first_pair(i, carry):
        first_block(2 + 2 * i, True)
        first_block(3 + 2 * i, True)
        return carry

    def later_one(e, carry):
        later_blocks(e, True)
        return carry

    later_blocks(0, False)
    later_blocks(1, False)
    halo_copy.wait_recv()
    first_block(0, False)
    first_block(1, False)
    lax.fori_loop(0, elecs // 2 - 1, first_pair, 0)
    back_sems = halo_send.at[1], halo_recv.at[1]
    push(back_out, back_in, back_sems, left)
    back_copy = group(back_in, back_sems)
    lax.fori_loop(2, elecs, later_one, 0)
    send_raw(1)

    def span(c):
        return slice(STARTS[c], STARTS[c] + CHUNKS[c]), 4 * elecs * CHUNKS[c]

    def spatial_project(c):
        for k in range(2):
            go[c, k].wait_recv()
        here, rows = span(c)
        xi = xr[:, here].reshape(rows, width)
        shape = (4 * elecs, CHUNKS[c], HALF)
        q_s[:, : CHUNKS[c]] = (mm(xi, w_s[:, :HALF], NN) * SCALE).reshape(shape)
        k_s[:, : CHUNKS[c]] = mm(xi, w_s[:, HALF : 2 * HALF], NN).reshape(shape)
        v_s[:, : CHUNKS[c]] = mm(xi, w_s[:, 2 * HALF :], NN).reshape(shape)
        g_s[:, : CHUNKS[c]] = mm(cr[:, here].reshape(rows, width), wo[:HALF, :], NT).reshape(shape)

    def spatial_attend(c):
        def block(i, carry):
            for j in range(2):
                at = pl.ds(pl.multiple_of(i * 16 + j * 8, 8), 8)
                q, g, k, v = [ref[:, at, :].reshape(WIN, HALF).astype(BF16) for ref in (q_s, g_s, k_s, v_s)]
                for ref, value in zip((g_s, q_s, k_s, v_s), spatial_block(q, g, k, v, apart)):
                    ref[:, at, :] = value.reshape(4 * elecs, 8, HALF)
            return carry

        lax.fori_loop(0, CHUNKS[c] // 16, block, 0)

    def spatial_end(c):
        here, rows = span(c)
        xi = xr[:, here].reshape(rows, width)
        grads = jnp.concatenate(
            [ref[:, : CHUNKS[c]].astype(BF16).reshape(rows, HALF) for ref in (q_s, k_s, v_s)], axis=1
        )
        dxs[:, here] = mm(grads, w_s[...], NT).astype(BF16).reshape(4 * elecs, CHUNKS[c], width)
        add_in = mm(xi, grads, TN)
        att = g_s[:, : CHUNKS[c]].astype(BF16).reshape(rows, HALF)
        add_out = mm(att, cr[:, here].reshape(rows, width), TN)
        if c == 0:
            acc_in_s[...] = add_in
            acc_out_s[...] = add_out
        else:
            acc_in_s[...] += add_in
            acc_out_s[...] += add_out

    returned = {}

    def send_back(c, steps):
        here, _ = span(c)
        sems = ret_send.at[c, steps[0] % 2], ret_recv.at[c, steps[0] % 2]
        for d in steps:
            push(dxs.at[d * elecs : (d + 1) * elecs, here], dxr.at[d - 1, :, here], sems, peer(y=4 - d))
        returned[c, steps[0] % 2] = group(dxr.at[: len(steps), :, here], sems)

    def place(c):
        here, _ = span(c)
        for i in range(2):
            returned[c, i].wait_recv()
        for d in range(4):
            at = rows_at(lax.rem(y + d, 4) * quarter + STARTS[c], CHUNKS[c])
            if d == 0:
                piece = dxs[:elecs, here]
            else:
                piece = dxr[d - 1, :, here]
            out[:, at, :] = (dx_t[:, at, :] + piece.astype(F32)).astype(BF16)

    def summing(n):
        def sems(p, step):
            return ar_send.at[n, p, step], ar_recv.at[n, p, step]

        def spot_of(p, d=0):
            return ar_out.at[n, p, rows_at(core * 1024 + lax.rem(where[orders[p][0]] + d, 4) * 256, 256)]

        waiting, last = [None, None], [None, None]
        for p in range(2):
            push(ar_src.at[n, p, rows_at((1 - core) * 1024, 1024)], recv_c.at[n, p], sems(p, 0), peer(core=1))
            waiting[p] = group(recv_c.at[n, p], sems(p, 0))
        yield
        for p, (a, b) in enumerate(orders):
            waiting[p].wait_recv()
            part_c[n, p] = (
                ar_src[n, p, rows_at(core * 1024, 1024)].astype(F32) + recv_c[n, p].astype(F32)
            ).astype(BF16)
            for d, by in on_axis(a):
                at = rows_at(lax.rem(where[a] + d, 4) * 256, 256)
                push(part_c.at[n, p, at], recv_a.at[n, p, d - 1], sems(p, 1), peer(**by))
            waiting[p] = group(recv_a.at[n, p], sems(p, 1))
        yield
        for p, (a, b) in enumerate(orders):
            waiting[p].wait_recv()
            total = part_c[n, p, rows_at(where[a] * 256, 256)].astype(F32)
            for i in range(3):
                total = total + recv_a[n, p, i].astype(F32)
            part[n, p] = total.astype(BF16)
            for i, by in on_plane(b):
                at = rows_at((lax.rem(where[b] + by[b], 4) * 4 + lax.rem(y + by["y"], 4)) * 16, 16)
                push(part.at[n, p, at], recv_b.at[n, p, i - 1], sems(p, 2), peer(**by))
            waiting[p] = group(recv_b.at[n, p], sems(p, 2))
        yield
        for p, (a, b) in enumerate(orders):
            waiting[p].wait_recv()
            mine = (where[b] * 4 + y) * 16
            total = part[n, p, rows_at(mine, 16)].astype(F32)
            for i in range(15):
                total = total + recv_b[n, p, i].astype(F32)
            at = rows_at(core * 1024 + where[a] * 256 + mine, 16)
            ar_out[n, p, at] = total.astype(BF16)
            for _, by in on_plane(b):
                push(ar_out.at[n, p, at], ar_out.at[n, p, at], sems(p, 3), peer(**by))
            waiting[p] = group(ar_out.at[n, p, :240], sems(p, 3))
        yield
        for p, (a, b) in enumerate(orders):
            waiting[p].wait_recv()
            for _, by in on_axis(a):
                push(spot_of(p), spot_of(p), sems(p, 4), peer(**by))
            waiting[p] = group(ar_out.at[n, p, :768], sems(p, 4))
            push(spot_of(p), spot_of(p), sems(p, 5), peer(core=1))
        yield
        for p in range(2):
            waiting[p].wait_recv()
            for d in range(1, 4):
                push(spot_of(p, d), spot_of(p, d), sems(p, 5), peer(core=1))
            waiting[p] = group(ar_out.at[n, p, :1024], sems(p, 5))
        yield
        for p in range(2):
            waiting[p].wait_recv()
            first = (1 - n) * HALF + p * 128
            for i in range(3):
                w_outs[i][:, first : first + 128] = ar_out[n, p, i * 512 : (i + 1) * 512]
            for i in range(2):
                low, column = (1 - n) * HALF, i * HALF + p * 128
                w_outs[3][low : low + HALF, column : column + 128] = ar_out[
                    n, p, 1536 + i * HALF : 1536 + (i + 1) * HALF
                ]
        yield

    back_copy.wait_recv()
    acc_in_t[...] = jnp.zeros_like(acc_in_t)
    acc_out_t[...] = jnp.zeros_like(acc_out_t)

    def end_time(e, carry):
        def full(own, side):
            tail = own[e, patches - WIN :] + back_in[side, e].astype(F32)
            return jnp.concatenate([own[e, : patches - WIN].astype(BF16), tail.astype(BF16)], axis=0)

        grads = jnp.concatenate([dq_t[e], full(dk_t, 0), full(dv_t, 1)], axis=1)
        dx_t[e] = mm(grads, w_t[...], NT)
        acc_in_t[...] += mm(xv[e], grads, TN)
        acc_out_t[...] += mm(att_t[e], cv[e], NN)
        return carry

    lax.fori_loop(0, elecs, end_time, 0)
    weight_rows(acc_in_t, acc_out_t, ar_src.at[0])
    time_sum, space_sum = summing(0), summing(1)
    next(time_sum)
    spatial_project(0)
    next(time_sum)
    spatial_attend(0)
    next(time_sum)
    send_raw(2)
    spatial_end(0)
    spatial_project(1)
    next(time_sum)
    send_back(0, (2,))
    send_back(0, (1, 3))
    spatial_attend(1)
    spatial_end(1)
    spatial_project(2)
    next(time_sum)
    spatial_attend(2)
    spatial_end(2)
    weight_rows(acc_in_s, acc_out_s, ar_src.at[1])
    next(space_sum)
    next(time_sum)
    next(space_sum)
    next(time_sum)
    next(space_sum)
    send_back(1, (1, 3))
    place(0)
    next(space_sum)
    send_back(1, (2,))
    send_back(2, (2,))
    send_back(2, (1, 3))
    next(space_sum)
    next(space_sum)
    place(1)
    place(2)
    next(space_sum)
    for whole in pending:
        whole.wait_send()


def end_kernel(dx, g0, g1, g2, g3, out, o0, o1, o2, o3):
    out[...] = dx[...]
    for grad, o in zip((g0, g1, g2, g3), (o0, o1, o2, o3)):
        o[...] = grad[...].astype(F32) * (1.0 / math.sqrt(196608))


def sds(shape, dtype):
    return jax.ShapeDtypeStruct(shape, dtype)


def shards(inputs, cotangent, w_query, w_key, w_value, w_out):
    _, elecs, patches, width = inputs.shape
    quarter = patches // 4
    vm, dma = pltpu.VMEM, pltpu.SemaphoreType.DMA
    tokens = (elecs, patches)
    ext = (elecs, patches + WIN)
    everyone = (4 * elecs, quarter)
    scratch = (
        [vm(tokens + (width,), BF16)] * 2
        + [vm((elecs, WIN, width), BF16)]
        + [vm((width, 3 * HALF), BF16)] * 2
        + [vm((width, width), BF16)]
        + [vm(tokens + (HALF,), BF16), vm(ext + (HALF,), BF16), vm(ext + (HALF,), BF16), vm(tokens + (HALF,), BF16)]
        + [vm(tokens + (HALF,), F32)] * 2
        + [vm((elecs, HALF, patches), BF16), vm(tokens + (HALF,), BF16)]
        + [vm((elecs, HALF, patches + WIN), BF16)] * 2
        + [vm((2, elecs, WIN, HALF), BF16)] * 2
        + [vm(tokens + (width,), F32)]
        + [vm(everyone + (width,), BF16)] * 2
        + [vm((4 * elecs, CHUNKS[0], HALF), F32)] * 4
        + [vm(everyone + (width,), BF16), vm((3, elecs, quarter, width), BF16)]
        + [vm((width, 3 * HALF), F32), vm((HALF, width), F32)] * 2
        + [vm((2, 2, 2048, 128), BF16)]
        + [vm((2, 2, 1024, 128), BF16)] * 2
        + [vm((2, 2, 3, 256, 128), BF16), vm((2, 2, 256, 128), BF16), vm((2, 2, 15, 16, 128), BF16)]
        + [vm((2, 2, 2048, 128), BF16)]
        + [vm((WIN, HEADS * WIN), t) for t in (F32, BF16, BF16, F32)]
        + [dma((11,)), dma((2,)), dma((2,))]
        + [dma((3, 2))] * 2
        + [dma((3, 2))] * 2
        + [dma((2, 2, 6))] * 2
    )
    grad_inputs, *grads = pl.pallas_call(
        layer_kernel,
        out_shape=(sds(tokens + (width,), BF16),) + (sds((width, width), BF16),) * 4,
        in_specs=[pl.BlockSpec(memory_space=pl.ANY)] * 6,
        out_specs=(pl.BlockSpec(memory_space=pltpu.VMEM),) * 5,
        scratch_shapes=scratch,
        compiler_params=pltpu.CompilerParams(
            collective_id=0, has_side_effects=True, vmem_limit_bytes=VMEM_LIMIT
        ),
        cost_estimate=pl.CostEstimate(flops=2 * 10**10, bytes_accessed=10**7, transcendentals=2 * 10**6),
    )(inputs[0], cotangent[0], w_query, w_key, w_value, w_out)
    grad_inputs, *grads = pl.pallas_call(
        end_kernel,
        out_shape=(sds(tokens + (width,), BF16),) + (sds((width, width), F32),) * 4,
        in_specs=[pl.BlockSpec(memory_space=pltpu.VMEM)] * 5,
        out_specs=(pl.BlockSpec(memory_space=pltpu.VMEM),) * 5,
        compiler_params=pltpu.CompilerParams(vmem_limit_bytes=VMEM_LIMIT),
    )(grad_inputs, *grads)
    return (grad_inputs[None],) + tuple(grads)


def solution(mesh):
    return jax.shard_map(
        shards,
        mesh=mesh,
        in_specs=(P("dp", "elec", "tm", None), P("dp", "elec", "tm", None), P(), P(), P(), P()),
        out_specs=(P("dp", "elec", "tm", None), P(), P(), P(), P()),
        check_vma=False,
    )
```

```python
import math

import jax
import jax.numpy as jnp
from jax import lax
from jax.experimental import pallas as pl
from jax.experimental.pallas import tpu as pltpu
from jax.sharding import PartitionSpec as P

BF16 = jnp.bfloat16
F32 = jnp.float32
WIN = 128
HALF = 256
HEAD = 64
HEADS = 4
NEG = -1e30
SCALE = 0.125
VMEM_LIMIT = 56 * 1024 * 1024
MESH = pl.DeviceIdType.MESH

NN = (((1,), (0,)), ((), ()))
NT = (((1,), (1,)), ((), ()))
TN = (((0,), (0,)), ((), ()))


def mm(left, right, dims):
    return lax.dot_general(left, right, dims, preferred_element_type=F32)


def stack_heads(rows):
    column = lax.broadcasted_iota(jnp.int32, (1, HALF), 1)
    keeps = [(column >= h * HEAD) & (column < (h + 1) * HEAD) for h in range(HEADS)]
    return jnp.concatenate([rows * keep.astype(F32).astype(BF16) for keep in keeps], axis=0)


def pick_heads(rows):
    r = rows.shape[0] // HEADS
    even = lax.broadcasted_iota(jnp.int32, (r, 128), 1) < HEAD
    return jnp.concatenate(
        [
            jnp.where(even, rows[:r, :128], rows[r : 2 * r, :128]),
            jnp.where(even, rows[2 * r : 3 * r, 128:], rows[3 * r :, 128:]),
        ],
        axis=1,
    )


def soft(scores, grad_probs):
    ex = jnp.exp(scores - jnp.max(scores, axis=0, keepdims=True))
    probs = ex * (1.0 / jnp.sum(ex, axis=0, keepdims=True))
    delta = jnp.sum(probs * grad_probs, axis=0, keepdims=True)
    return probs.astype(BF16), (probs * (grad_probs - delta)).astype(BF16)


def make_masks(older, older_low, newer_low, apart):
    row = lax.broadcasted_iota(jnp.int32, (WIN, WIN), 0)
    column = lax.broadcasted_iota(jnp.int32, (WIN, WIN), 1)
    old = (row > column).astype(F32)
    far = jnp.where(lax.rem(row, 8) == lax.rem(column, 8), 0.0, NEG).astype(F32)
    for h in range(HEADS):
        at = slice(h * WIN, (h + 1) * WIN)
        older[:, at] = old
        older_low[:, at] = old.astype(BF16)
        newer_low[:, at] = (1.0 - old).astype(BF16)
        apart[:, at] = far


def diagonal(cols):
    return jnp.concatenate(
        [cols[h * HEAD : (h + 1) * HEAD, h * WIN : (h + 1) * WIN] for h in range(HEADS)], axis=0
    )


def temporal_block(q, ga, k, v, k_cols, v_cols, bias, older, older_low, newer_low):
    qs, gs = stack_heads(q), stack_heads(ga)
    st = mm(k, qs, NT)
    gt = mm(v, gs, NT)
    old = older[...] > 0.5
    early = st[:WIN] if bias is None else st[:WIN] + bias
    probs, grad = soft(jnp.where(old, early, st[WIN:]), jnp.where(old, gt[:WIN], gt[WIN:]))
    pt = jnp.concatenate([probs * older_low[...], probs * newer_low[...]], axis=0)
    dt = jnp.concatenate([grad * older_low[...], grad * newer_low[...]], axis=0)
    att = diagonal(mm(v_cols, pt, NN)).astype(BF16)
    dq = (diagonal(mm(k_cols, dt, NN)) * SCALE).astype(BF16)
    return att, dq.T, mm(dt, qs, NN), mm(pt, gs, NN)


def spatial_block(q, ga, k, v, apart):
    qs, gs = stack_heads(q), stack_heads(ga)
    pt, dt = soft(mm(k, qs, NT) + apart[...], mm(v, gs, NT))
    att = pick_heads(mm(pt, v, TN))
    dq = pick_heads(mm(dt, k, TN)) * SCALE
    return att, dq, mm(dt, qs, NN), mm(pt, gs, NN)


def coordinates():
    dp, tm, y = lax.axis_index("dp"), lax.axis_index("tm"), lax.axis_index("elec")
    z, rest = lax.div(tm, 4), lax.rem(tm, 4)
    x = lax.div(rest, 2) * 2 + dp
    return x, y, z, lax.rem(rest, 2)


def device_at(x, y, z, core):
    return {"dp": lax.rem(x, 2), "tm": z * 4 + lax.div(x, 2) * 2 + core, "elec": y}


CHUNKS = (48, 32, 16)
STARTS = (0, 48, 80)


def weight_rows(acc_in, acc_out, dst):
    for j in range(2):
        for i in range(3):
            first = i * HALF + j * 128
            dst[j, i * 512 : (i + 1) * 512] = acc_in[:, first : first + 128].astype(BF16)
        for i in range(2):
            first = i * HALF + j * 128
            dst[j, 1536 + i * HALF : 1536 + (i + 1) * HALF] = acc_out[:, first : first + 128].astype(BF16)


def layer_kernel(x_h, cot_h, wq_h, wk_h, wv_h, wo_h, out, *rest):
    w_outs = rest[:4]
    (
        xv, cv, halo, w_t, w_s, wo, q_t, k_t, v_t, g_t, dk_t, dv_t, att_t, dq_t, kc_t, vc_t, back_out, back_in, dx_t,
        xr, cr, q_s, k_s, v_s, g_s, dxs, dxr, acc_in_t, acc_out_t, acc_in_s, acc_out_s,
        ar_src, recv_c, part_c, recv_a, part, recv_b, ar_out, older, older_low, newer_low, apart,
        load_sem, halo_send, halo_recv, go_send, go_recv, ret_send, ret_recv, ar_send, ar_recv, all_send, all_recv,
    ) = rest[4:]
    elecs, patches, width = xv.shape
    quarter = patches // 4
    x, y, z, core = coordinates()
    tm = lax.axis_index("tm")
    right = {"tm": lax.rem(tm + 1, 16)}
    left = {"tm": lax.rem(tm + 15, 16)}
    where = {"x": x, "y": y, "z": z, "core": core}

    def peer(**by):
        at = {n: lax.rem(where[n] + by.get(n, 0), 2 if n == "core" else 4) for n in where}
        return device_at(at["x"], at["y"], at["z"], at["core"])

    orders = (("x", "z"), ("z", "x"))

    def on_axis(a):
        return [(d, {a: d}) for d in range(1, 4)]

    def on_plane(b):
        return [(i, {b: i // 4, "y": i % 4}) for i in range(1, 16)]

    loads = []

    def load(src, dst):
        copy = pltpu.make_async_copy(src, dst, load_sem.at[len(loads)])
        copy.start()
        loads.append(copy)

    load(x_h, xv)
    load(cot_h, cv)
    load(wo_h, wo)
    for i, w in enumerate((wq_h, wk_h, wv_h)):
        load(w.at[:, HALF:], w_t.at[:, i * HALF : (i + 1) * HALF])
    for i, w in enumerate((wq_h, wk_h, wv_h)):
        load(w.at[:, :HALF], w_s.at[:, i * HALF : (i + 1) * HALF])
    at = pl.ds(pl.multiple_of(y * quarter, 16), quarter)
    load(x_h.at[:, at], xr.at[:elecs])
    load(cot_h.at[:, at], cr.at[:elecs])

    near = {tuple((n, v) for n, v in by.items() if v) for b in "xz" for _, by in on_plane(b)}
    near = [(("core", 1),)] + sorted(near)
    barrier = pltpu.get_barrier_semaphore()
    for device in [right, left] + [peer(**dict(by)) for by in near]:
        pl.semaphore_signal(barrier, inc=1, device_id=device, device_id_type=MESH)
    pl.semaphore_wait(barrier, 2 + len(near))

    pending = []

    def push(src, dst, sems, device):
        pltpu.make_async_remote_copy(
            src_ref=src, dst_ref=dst, send_sem=sems[0], recv_sem=sems[1], device_id=device, device_id_type=MESH
        ).start()

    def group(ref, sems):
        whole = pltpu.make_async_remote_copy(
            src_ref=ref, dst_ref=ref, send_sem=sems[0], recv_sem=sems[1], device_id=right, device_id_type=MESH
        )
        pending.append(whole)
        return whole

    def rows_at(first, size):
        return pl.ds(pl.multiple_of(first, 16), size)

    loads[0].wait()
    loads[1].wait()
    halo_sems = halo_send.at[0], halo_recv.at[0]
    push(xv.at[:, patches - WIN :], halo, halo_sems, right)
    halo_copy = group(halo, halo_sems)
    go = {}

    def send_raw(c):
        here = slice(STARTS[c], STARTS[c] + CHUNKS[c])
        for k, (src, dst) in enumerate(((xv, xr), (cv, cr))):
            sems = go_send.at[c, k], go_recv.at[c, k]
            for d in (2, 1, 3):
                at = rows_at(lax.rem(y + d, 4) * quarter + STARTS[c], CHUNKS[c])
                push(src.at[:, at], dst.at[d * elecs : (d + 1) * elecs, here], sems, peer(y=d))
            go[c, k] = group(dst.at[elecs:, here], sems)

    send_raw(0)
    masks = older, older_low, newer_low
    make_masks(*masks, apart)
    for copy in loads[2:]:
        copy.wait()

    bias0 = jnp.where(tm == 0, NEG, 0.0).astype(F32)

    def project_time(e, carry):
        q_t[e] = (mm(xv[e], w_t[:, :HALF], NN) * SCALE).astype(BF16)
        for own, cols, i in ((k_t, kc_t, 1), (v_t, vc_t, 2)):
            t = mm(xv[e], w_t[:, i * HALF : (i + 1) * HALF], NN).astype(BF16)
            own[e, WIN:] = t
            cols[e, :, WIN:] = t.T
        g_t[e] = mm(cv[e], wo[HALF:, :], NT).astype(BF16)
        return carry

    lax.fori_loop(0, elecs, project_time, 0)

    def time_block(e, c, bias):
        rows, keys = slice(c * WIN, (c + 1) * WIN), slice(c * WIN, (c + 2) * WIN)
        att, dq, dk, dv = temporal_block(
            q_t[e, rows], g_t[e, rows], k_t[e, keys], v_t[e, keys], kc_t[e, :, keys], vc_t[e, :, keys], bias, *masks
        )
        att_t[e, :, rows] = att
        dq_t[e, rows] = dq
        return dk, dv

    def later_blocks(e, first_done):
        ones = time_block(e, 1, None)
        twos = time_block(e, 2, None)
        for ref, one, two in zip((dk_t, dv_t), ones, twos):
            if first_done:
                ref[e, :WIN] += one[:WIN]
            else:
                ref[e, :WIN] = one[:WIN]
            ref[e, WIN : 2 * WIN] = one[WIN:] + two[:WIN]
            ref[e, 2 * WIN :] = two[WIN:]

    def first_block(e, first_done):
        for own, cols, i in ((k_t, kc_t, 1), (v_t, vc_t, 2)):
            t = mm(halo[e], w_t[:, i * HALF : (i + 1) * HALF], NN).astype(BF16)
            own[e, :WIN] = t
            cols[e, :, :WIN] = t.T
        for side, (ref, grad) in enumerate(zip((dk_t, dv_t), time_block(e, 0, bias0))):
            back_out[side, e] = grad[:WIN].astype(BF16)
            if first_done:
                ref[e, :WIN] = grad[WIN:]
            else:
                ref[e, :WIN] += grad[WIN:]

    def first_pair(i, carry):
        first_block(2 + 2 * i, True)
        first_block(3 + 2 * i, True)
        return carry

    def later_one(e, carry):
        later_blocks(e, True)
        return carry

    later_blocks(0, False)
    later_blocks(1, False)
    halo_copy.wait_recv()
    first_block(0, False)
    first_block(1, False)
    lax.fori_loop(0, elecs // 2 - 1, first_pair, 0)
    back_sems = halo_send.at[1], halo_recv.at[1]
    push(back_out, back_in, back_sems, left)
    back_copy = group(back_in, back_sems)
    lax.fori_loop(2, elecs, later_one, 0)
    send_raw(1)

    def span(c):
        return slice(STARTS[c], STARTS[c] + CHUNKS[c]), 4 * elecs * CHUNKS[c]

    def spatial_project(c):
        for k in range(2):
            go[c, k].wait_recv()
        here, rows = span(c)
        xi = xr[:, here].reshape(rows, width)
        shape = (4 * elecs, CHUNKS[c], HALF)
        q_s[:, : CHUNKS[c]] = (mm(xi, w_s[:, :HALF], NN) * SCALE).reshape(shape)
        k_s[:, : CHUNKS[c]] = mm(xi, w_s[:, HALF : 2 * HALF], NN).reshape(shape)
        v_s[:, : CHUNKS[c]] = mm(xi, w_s[:, 2 * HALF :], NN).reshape(shape)
        g_s[:, : CHUNKS[c]] = mm(cr[:, here].reshape(rows, width), wo[:HALF, :], NT).reshape(shape)

    def spatial_attend(c):
        def block(i, carry):
            for j in range(2):
                at = pl.ds(pl.multiple_of(i * 16 + j * 8, 8), 8)
                q, g, k, v = [ref[:, at, :].reshape(WIN, HALF).astype(BF16) for ref in (q_s, g_s, k_s, v_s)]
                for ref, value in zip((g_s, q_s, k_s, v_s), spatial_block(q, g, k, v, apart)):
                    ref[:, at, :] = value.reshape(4 * elecs, 8, HALF)
            return carry

        lax.fori_loop(0, CHUNKS[c] // 16, block, 0)

    def spatial_end(c):
        here, rows = span(c)
        xi = xr[:, here].reshape(rows, width)
        grads = jnp.concatenate(
            [ref[:, : CHUNKS[c]].astype(BF16).reshape(rows, HALF) for ref in (q_s, k_s, v_s)], axis=1
        )
        dxs[:, here] = mm(grads, w_s[...], NT).astype(BF16).reshape(4 * elecs, CHUNKS[c], width)
        add_in = mm(xi, grads, TN)
        att = g_s[:, : CHUNKS[c]].astype(BF16).reshape(rows, HALF)
        add_out = mm(att, cr[:, here].reshape(rows, width), TN)
        if c == 0:
            acc_in_s[...] = add_in
            acc_out_s[...] = add_out
        else:
            acc_in_s[...] += add_in
            acc_out_s[...] += add_out

    returned = {}

    def send_back(c, steps):
        here, _ = span(c)
        sems = ret_send.at[c, steps[0] % 2], ret_recv.at[c, steps[0] % 2]
        for d in steps:
            push(dxs.at[d * elecs : (d + 1) * elecs, here], dxr.at[d - 1, :, here], sems, peer(y=4 - d))
        returned[c, steps[0] % 2] = group(dxr.at[: len(steps), :, here], sems)

    def place(c):
        here, _ = span(c)
        for i in range(2):
            returned[c, i].wait_recv()
        for d in range(4):
            at = rows_at(lax.rem(y + d, 4) * quarter + STARTS[c], CHUNKS[c])
            if d == 0:
                piece = dxs[:elecs, here]
            else:
                piece = dxr[d - 1, :, here]
            out[:, at, :] = (dx_t[:, at, :] + piece.astype(F32)).astype(BF16)

    waiting = {}

    def gather(n):
        def sems(p, step):
            return ar_send.at[n, p, step], ar_recv.at[n, p, step]

        for p in range(2):
            push(ar_src.at[n, p, rows_at((1 - core) * 1024, 1024)], recv_c.at[n, p], sems(p, 0), peer(core=1))
            waiting[n, p] = group(recv_c.at[n, p], sems(p, 0))
        yield
        for p, (a, b) in enumerate(orders):
            waiting[n, p].wait_recv()
            part_c[n, p] = (
                ar_src[n, p, rows_at(core * 1024, 1024)].astype(F32) + recv_c[n, p].astype(F32)
            ).astype(BF16)
            for d, by in on_axis(a):
                at = rows_at(lax.rem(where[a] + d, 4) * 256, 256)
                push(part_c.at[n, p, at], recv_a.at[n, p, d - 1], sems(p, 1), peer(**by))
            waiting[n, p] = group(recv_a.at[n, p], sems(p, 1))
        yield

    def finish():
        def sems(p, step):
            return all_send.at[p, step], all_recv.at[p, step]

        def spot_of(p, d=0):
            return ar_out.at[p, :, rows_at(core * 1024 + lax.rem(where[orders[p][0]] + d, 4) * 256, 256)]

        for p, (a, b) in enumerate(orders):
            for n in range(2):
                waiting[n, p].wait_recv()
                total = part_c[n, p, rows_at(where[a] * 256, 256)].astype(F32)
                for i in range(3):
                    total = total + recv_a[n, p, i].astype(F32)
                part[p, n] = total.astype(BF16)
            for i, by in on_plane(b):
                at = rows_at((lax.rem(where[b] + by[b], 4) * 4 + lax.rem(y + by["y"], 4)) * 16, 16)
                push(part.at[p, :, at], recv_b.at[p, i - 1], sems(p, 0), peer(**by))
            waiting[p] = group(recv_b.at[p], sems(p, 0))
        yield
        for p, (a, b) in enumerate(orders):
            waiting[p].wait_recv()
            mine = (where[b] * 4 + y) * 16
            total = part[p, :, rows_at(mine, 16)].astype(F32)
            for i in range(15):
                total = total + recv_b[p, i].astype(F32)
            at = rows_at(core * 1024 + where[a] * 256 + mine, 16)
            ar_out[p, :, at] = total.astype(BF16)
            for _, by in on_plane(b):
                push(ar_out.at[p, :, at], ar_out.at[p, :, at], sems(p, 1), peer(**by))
            waiting[p] = group(ar_out.at[p, :, :240], sems(p, 1))
        yield
        for p, (a, b) in enumerate(orders):
            waiting[p].wait_recv()
            for _, by in on_axis(a):
                push(spot_of(p), spot_of(p), sems(p, 2), peer(**by))
            waiting[p] = group(ar_out.at[p, :, :768], sems(p, 2))
            push(spot_of(p), spot_of(p), sems(p, 3), peer(core=1))
        yield
        for p in range(2):
            waiting[p].wait_recv()
            for d in range(1, 4):
                push(spot_of(p, d), spot_of(p, d), sems(p, 3), peer(core=1))
            waiting[p] = group(ar_out.at[p, :, :1024], sems(p, 3))
        yield
        for p in range(2):
            waiting[p].wait_recv()
            for n in range(2):
                low = (1 - n) * HALF
                first = low + p * 128
                for i in range(3):
                    w_outs[i][:, first : first + 128] = ar_out[p, n, i * 512 : (i + 1) * 512]
                for i in range(2):
                    column = i * HALF + p * 128
                    w_outs[3][low : low + HALF, column : column + 128] = ar_out[
                        p, n, 1536 + i * HALF : 1536 + (i + 1) * HALF
                    ]
        yield

    back_copy.wait_recv()
    acc_in_t[...] = jnp.zeros_like(acc_in_t)
    acc_out_t[...] = jnp.zeros_like(acc_out_t)

    def end_time(e, carry):
        def full(own, side):
            tail = own[e, patches - WIN :] + back_in[side, e].astype(F32)
            return jnp.concatenate([own[e, : patches - WIN].astype(BF16), tail.astype(BF16)], axis=0)

        grads = jnp.concatenate([dq_t[e], full(dk_t, 0), full(dv_t, 1)], axis=1)
        dx_t[e] = mm(grads, w_t[...], NT)
        acc_in_t[...] += mm(xv[e], grads, TN)
        acc_out_t[...] += mm(att_t[e], cv[e], NN)
        return carry

    lax.fori_loop(0, elecs, end_time, 0)
    weight_rows(acc_in_t, acc_out_t, ar_src.at[0])
    time_sum, space_sum, both = gather(0), gather(1), finish()
    next(time_sum)
    spatial_project(0)
    send_raw(2)
    spatial_attend(0)
    next(time_sum)
    spatial_end(0)
    spatial_project(1)
    spatial_attend(1)
    spatial_end(1)
    spatial_project(2)
    send_back(0, (2,))
    send_back(0, (1, 3))
    spatial_attend(2)
    spatial_end(2)
    weight_rows(acc_in_s, acc_out_s, ar_src.at[1])
    next(space_sum)
    next(space_sum)
    send_back(2, (2,))
    send_back(2, (1, 3))
    next(both)
    place(0)
    next(both)
    send_back(1, (2,))
    send_back(1, (1, 3))
    place(2)
    next(both)
    next(both)
    place(1)
    next(both)
    for whole in pending:
        whole.wait_send()


def end_kernel(dx, g0, g1, g2, g3, out, o0, o1, o2, o3):
    out[...] = dx[...]
    for grad, o in zip((g0, g1, g2, g3), (o0, o1, o2, o3)):
        o[...] = grad[...].astype(F32) * (1.0 / math.sqrt(196608))


def sds(shape, dtype):
    return jax.ShapeDtypeStruct(shape, dtype)


def shards(inputs, cotangent, w_query, w_key, w_value, w_out):
    _, elecs, patches, width = inputs.shape
    quarter = patches // 4
    vm, dma = pltpu.VMEM, pltpu.SemaphoreType.DMA
    tokens = (elecs, patches)
    ext = (elecs, patches + WIN)
    everyone = (4 * elecs, quarter)
    scratch = (
        [vm(tokens + (width,), BF16)] * 2
        + [vm((elecs, WIN, width), BF16)]
        + [vm((width, 3 * HALF), BF16)] * 2
        + [vm((width, width), BF16)]
        + [vm(tokens + (HALF,), BF16), vm(ext + (HALF,), BF16), vm(ext + (HALF,), BF16), vm(tokens + (HALF,), BF16)]
        + [vm(tokens + (HALF,), F32)] * 2
        + [vm((elecs, HALF, patches), BF16), vm(tokens + (HALF,), BF16)]
        + [vm((elecs, HALF, patches + WIN), BF16)] * 2
        + [vm((2, elecs, WIN, HALF), BF16)] * 2
        + [vm(tokens + (width,), F32)]
        + [vm(everyone + (width,), BF16)] * 2
        + [vm((4 * elecs, CHUNKS[0], HALF), F32)] * 4
        + [vm(everyone + (width,), BF16), vm((3, elecs, quarter, width), BF16)]
        + [vm((width, 3 * HALF), F32), vm((HALF, width), F32)] * 2
        + [vm((2, 2, 2048, 128), BF16)]
        + [vm((2, 2, 1024, 128), BF16)] * 2
        + [vm((2, 2, 3, 256, 128), BF16), vm((2, 2, 256, 128), BF16), vm((2, 15, 2, 16, 128), BF16)]
        + [vm((2, 2, 2048, 128), BF16)]
        + [vm((WIN, HEADS * WIN), t) for t in (F32, BF16, BF16, F32)]
        + [dma((11,)), dma((2,)), dma((2,))]
        + [dma((3, 2))] * 2
        + [dma((3, 2))] * 2
        + [dma((2, 2, 2))] * 2
        + [dma((2, 4))] * 2
    )
    grad_inputs, *grads = pl.pallas_call(
        layer_kernel,
        out_shape=(sds(tokens + (width,), BF16),) + (sds((width, width), BF16),) * 4,
        in_specs=[pl.BlockSpec(memory_space=pl.ANY)] * 6,
        out_specs=(pl.BlockSpec(memory_space=pltpu.VMEM),) * 5,
        scratch_shapes=scratch,
        compiler_params=pltpu.CompilerParams(
            collective_id=0, has_side_effects=True, vmem_limit_bytes=VMEM_LIMIT
        ),
        cost_estimate=pl.CostEstimate(flops=2 * 10**10, bytes_accessed=10**7, transcendentals=2 * 10**6),
    )(inputs[0], cotangent[0], w_query, w_key, w_value, w_out)
    grad_inputs, *grads = pl.pallas_call(
        end_kernel,
        out_shape=(sds(tokens + (width,), BF16),) + (sds((width, width), F32),) * 4,
        in_specs=[pl.BlockSpec(memory_space=pltpu.VMEM)] * 5,
        out_specs=(pl.BlockSpec(memory_space=pltpu.VMEM),) * 5,
        compiler_params=pltpu.CompilerParams(vmem_limit_bytes=VMEM_LIMIT),
    )(grad_inputs, *grads)
    return (grad_inputs[None],) + tuple(grads)


def solution(mesh):
    return jax.shard_map(
        shards,
        mesh=mesh,
        in_specs=(P("dp", "elec", "tm", None), P("dp", "elec", "tm", None), P(), P(), P(), P()),
        out_specs=(P("dp", "elec", "tm", None), P(), P(), P(), P()),
        check_vma=False,
    )
```

```python
import math

import jax
import jax.numpy as jnp
from jax import lax
from jax.experimental import pallas as pl
from jax.experimental.pallas import tpu as pltpu
from jax.sharding import PartitionSpec as P

BF16 = jnp.bfloat16
F32 = jnp.float32
WIN = 128
HALF = 256
HEAD = 64
HEADS = 4
NEG = -1e30
SCALE = 0.125
VMEM_LIMIT = 56 * 1024 * 1024
MESH = pl.DeviceIdType.MESH

NN = (((1,), (0,)), ((), ()))
NT = (((1,), (1,)), ((), ()))
TN = (((0,), (0,)), ((), ()))


def mm(left, right, dims):
    return lax.dot_general(left, right, dims, preferred_element_type=F32)


def stack_heads(rows):
    column = lax.broadcasted_iota(jnp.int32, (1, HALF), 1)
    keeps = [(column >= h * HEAD) & (column < (h + 1) * HEAD) for h in range(HEADS)]
    return jnp.concatenate([rows * keep.astype(F32).astype(BF16) for keep in keeps], axis=0)


def pick_heads(rows):
    r = rows.shape[0] // HEADS
    even = lax.broadcasted_iota(jnp.int32, (r, 128), 1) < HEAD
    return jnp.concatenate(
        [
            jnp.where(even, rows[:r, :128], rows[r : 2 * r, :128]),
            jnp.where(even, rows[2 * r : 3 * r, 128:], rows[3 * r :, 128:]),
        ],
        axis=1,
    )


def soft(scores, grad_probs):
    ex = jnp.exp(scores - jnp.max(scores, axis=0, keepdims=True))
    probs = ex * (1.0 / jnp.sum(ex, axis=0, keepdims=True))
    delta = jnp.sum(probs * grad_probs, axis=0, keepdims=True)
    return probs.astype(BF16), (probs * (grad_probs - delta)).astype(BF16)


def make_masks(older, older_low, newer_low, apart):
    row = lax.broadcasted_iota(jnp.int32, (WIN, WIN), 0)
    column = lax.broadcasted_iota(jnp.int32, (WIN, WIN), 1)
    old = (row > column).astype(F32)
    far = jnp.where(lax.rem(row, 8) == lax.rem(column, 8), 0.0, NEG).astype(F32)
    for h in range(HEADS):
        at = slice(h * WIN, (h + 1) * WIN)
        older[:, at] = old
        older_low[:, at] = old.astype(BF16)
        newer_low[:, at] = (1.0 - old).astype(BF16)
        apart[:, at] = far


def diagonal(cols):
    return jnp.concatenate(
        [cols[h * HEAD : (h + 1) * HEAD, h * WIN : (h + 1) * WIN] for h in range(HEADS)], axis=0
    )


def temporal_block(q, ga, k, v, k_cols, v_cols, bias, older, older_low, newer_low):
    qs, gs = stack_heads(q), stack_heads(ga)
    st = mm(k, qs, NT)
    gt = mm(v, gs, NT)
    old = older[...] > 0.5
    early = st[:WIN] if bias is None else st[:WIN] + bias
    probs, grad = soft(jnp.where(old, early, st[WIN:]), jnp.where(old, gt[:WIN], gt[WIN:]))
    pt = jnp.concatenate([probs * older_low[...], probs * newer_low[...]], axis=0)
    dt = jnp.concatenate([grad * older_low[...], grad * newer_low[...]], axis=0)
    att = diagonal(mm(v_cols, pt, NN)).astype(BF16)
    dq = (diagonal(mm(k_cols, dt, NN)) * SCALE).astype(BF16)
    return att, dq.T, mm(dt, qs, NN), mm(pt, gs, NN)


def spatial_block(q, ga, k, v, apart):
    qs, gs = stack_heads(q), stack_heads(ga)
    pt, dt = soft(mm(k, qs, NT) + apart[...], mm(v, gs, NT))
    att = pick_heads(mm(pt, v, TN))
    dq = pick_heads(mm(dt, k, TN)) * SCALE
    return att, dq, mm(dt, qs, NN), mm(pt, gs, NN)


def coordinates():
    dp, tm, y = lax.axis_index("dp"), lax.axis_index("tm"), lax.axis_index("elec")
    z, rest = lax.div(tm, 4), lax.rem(tm, 4)
    x = lax.div(rest, 2) * 2 + dp
    return x, y, z, lax.rem(rest, 2)


def device_at(x, y, z, core):
    return {"dp": lax.rem(x, 2), "tm": z * 4 + lax.div(x, 2) * 2 + core, "elec": y}


CHUNKS = (48, 32, 16)
STARTS = (0, 48, 80)


def weight_rows(acc_in, acc_out, dst):
    for j in range(2):
        for i in range(3):
            first = i * HALF + j * 128
            dst[j, i * 512 : (i + 1) * 512] = acc_in[:, first : first + 128].astype(BF16)
        for i in range(2):
            first = i * HALF + j * 128
            dst[j, 1536 + i * HALF : 1536 + (i + 1) * HALF] = acc_out[:, first : first + 128].astype(BF16)


def layer_kernel(x_h, cot_h, wq_h, wk_h, wv_h, wo_h, out, *rest):
    w_outs = rest[:4]
    (
        xv, cv, halo, w_t, w_s, wo, q_t, k_t, v_t, g_t, dk_t, dv_t, att_t, dq_t, kc_t, vc_t, back_out, back_in, dx_t,
        xr, cr, q_s, k_s, v_s, g_s, dxs, dxr, acc_in_t, acc_out_t, acc_in_s, acc_out_s,
        ar_src, recv_c, part_c, recv_a, part, recv_b, ar_out, older, older_low, newer_low, apart,
        load_sem, halo_send, halo_recv, go_send, go_recv, ret_send, ret_recv, ar_send, ar_recv,
    ) = rest[4:]
    elecs, patches, width = xv.shape
    quarter = patches // 4
    x, y, z, core = coordinates()
    tm = lax.axis_index("tm")
    right = {"tm": lax.rem(tm + 1, 16)}
    left = {"tm": lax.rem(tm + 15, 16)}
    where = {"x": x, "y": y, "z": z, "core": core}

    def peer(**by):
        at = {n: lax.rem(where[n] + by.get(n, 0), 2 if n == "core" else 4) for n in where}
        return device_at(at["x"], at["y"], at["z"], at["core"])

    orders = (("x", "z"), ("z", "x"))

    def on_axis(a):
        return [(d, {a: d}) for d in range(1, 4)]

    def on_plane(b):
        return [(i, {b: i // 4, "y": i % 4}) for i in range(1, 16)]

    loads = []

    def load(src, dst):
        copy = pltpu.make_async_copy(src, dst, load_sem.at[len(loads)])
        copy.start()
        loads.append(copy)

    load(x_h, xv)
    load(cot_h, cv)
    load(wo_h, wo)
    for i, w in enumerate((wq_h, wk_h, wv_h)):
        load(w.at[:, HALF:], w_t.at[:, i * HALF : (i + 1) * HALF])
    for i, w in enumerate((wq_h, wk_h, wv_h)):
        load(w.at[:, :HALF], w_s.at[:, i * HALF : (i + 1) * HALF])
    at = pl.ds(pl.multiple_of(y * quarter, 16), quarter)
    load(x_h.at[:, at], xr.at[:elecs])
    load(cot_h.at[:, at], cr.at[:elecs])

    near = {tuple((n, v) for n, v in by.items() if v) for b in "xz" for _, by in on_plane(b)}
    near = [(("core", 1),)] + sorted(near)
    barrier = pltpu.get_barrier_semaphore()
    for device in [right, left] + [peer(**dict(by)) for by in near]:
        pl.semaphore_signal(barrier, inc=1, device_id=device, device_id_type=MESH)
    pl.semaphore_wait(barrier, 2 + len(near))

    pending = []

    def push(src, dst, sems, device):
        pltpu.make_async_remote_copy(
            src_ref=src, dst_ref=dst, send_sem=sems[0], recv_sem=sems[1], device_id=device, device_id_type=MESH
        ).start()

    def group(ref, sems):
        whole = pltpu.make_async_remote_copy(
            src_ref=ref, dst_ref=ref, send_sem=sems[0], recv_sem=sems[1], device_id=right, device_id_type=MESH
        )
        pending.append(whole)
        return whole

    def rows_at(first, size):
        return pl.ds(pl.multiple_of(first, 16), size)

    loads[0].wait()
    loads[1].wait()
    halo_sems = halo_send.at[0], halo_recv.at[0]
    push(xv.at[:, patches - WIN :], halo, halo_sems, right)
    halo_copy = group(halo, halo_sems)
    go = {}

    def send_raw(c):
        here = slice(STARTS[c], STARTS[c] + CHUNKS[c])
        for k, (src, dst) in enumerate(((xv, xr), (cv, cr))):
            sems = go_send.at[c, k], go_recv.at[c, k]
            for d in (2, 1, 3):
                at = rows_at(lax.rem(y + d, 4) * quarter + STARTS[c], CHUNKS[c])
                push(src.at[:, at], dst.at[d * elecs : (d + 1) * elecs, here], sems, peer(y=d))
            go[c, k] = group(dst.at[elecs:, here], sems)

    send_raw(0)
    masks = older, older_low, newer_low
    make_masks(*masks, apart)
    for copy in loads[2:]:
        copy.wait()

    bias0 = jnp.where(tm == 0, NEG, 0.0).astype(F32)

    def project_time(e, carry):
        q_t[e] = (mm(xv[e], w_t[:, :HALF], NN) * SCALE).astype(BF16)
        for own, cols, i in ((k_t, kc_t, 1), (v_t, vc_t, 2)):
            t = mm(xv[e], w_t[:, i * HALF : (i + 1) * HALF], NN).astype(BF16)
            own[e, WIN:] = t
            cols[e, :, WIN:] = t.T
        g_t[e] = mm(cv[e], wo[HALF:, :], NT).astype(BF16)
        return carry

    lax.fori_loop(0, elecs, project_time, 0)

    def time_block(e, c, bias):
        rows, keys = slice(c * WIN, (c + 1) * WIN), slice(c * WIN, (c + 2) * WIN)
        att, dq, dk, dv = temporal_block(
            q_t[e, rows], g_t[e, rows], k_t[e, keys], v_t[e, keys], kc_t[e, :, keys], vc_t[e, :, keys], bias, *masks
        )
        att_t[e, :, rows] = att
        dq_t[e, rows] = dq
        return dk, dv

    def later_blocks(e, first_done):
        ones = time_block(e, 1, None)
        twos = time_block(e, 2, None)
        for ref, one, two in zip((dk_t, dv_t), ones, twos):
            if first_done:
                ref[e, :WIN] += one[:WIN]
            else:
                ref[e, :WIN] = one[:WIN]
            ref[e, WIN : 2 * WIN] = one[WIN:] + two[:WIN]
            ref[e, 2 * WIN :] = two[WIN:]

    def first_block(e, first_done):
        for own, cols, i in ((k_t, kc_t, 1), (v_t, vc_t, 2)):
            t = mm(halo[e], w_t[:, i * HALF : (i + 1) * HALF], NN).astype(BF16)
            own[e, :WIN] = t
            cols[e, :, :WIN] = t.T
        for side, (ref, grad) in enumerate(zip((dk_t, dv_t), time_block(e, 0, bias0))):
            back_out[side, e] = grad[:WIN].astype(BF16)
            if first_done:
                ref[e, :WIN] = grad[WIN:]
            else:
                ref[e, :WIN] += grad[WIN:]

    def first_pair(i, carry):
        first_block(2 + 2 * i, True)
        first_block(3 + 2 * i, True)
        return carry

    def later_one(e, carry):
        later_blocks(e, True)
        return carry

    later_blocks(0, False)
    later_blocks(1, False)
    halo_copy.wait_recv()
    first_block(0, False)
    first_block(1, False)
    lax.fori_loop(0, elecs // 2 - 1, first_pair, 0)
    back_sems = halo_send.at[1], halo_recv.at[1]
    push(back_out, back_in, back_sems, left)
    back_copy = group(back_in, back_sems)
    lax.fori_loop(2, elecs, later_one, 0)
    send_raw(1)

    def span(c):
        return slice(STARTS[c], STARTS[c] + CHUNKS[c]), 4 * elecs * CHUNKS[c]

    def spatial_project(c):
        for k in range(2):
            go[c, k].wait_recv()
        here, rows = span(c)
        xi = xr[:, here].reshape(rows, width)
        shape = (4 * elecs, CHUNKS[c], HALF)
        q_s[:, : CHUNKS[c]] = (mm(xi, w_s[:, :HALF], NN) * SCALE).reshape(shape)
        k_s[:, : CHUNKS[c]] = mm(xi, w_s[:, HALF : 2 * HALF], NN).reshape(shape)
        v_s[:, : CHUNKS[c]] = mm(xi, w_s[:, 2 * HALF :], NN).reshape(shape)
        g_s[:, : CHUNKS[c]] = mm(cr[:, here].reshape(rows, width), wo[:HALF, :], NT).reshape(shape)

    def spatial_attend(c):
        def block(i, carry):
            for j in range(2):
                at = pl.ds(pl.multiple_of(i * 16 + j * 8, 8), 8)
                q, g, k, v = [ref[:, at, :].reshape(WIN, HALF).astype(BF16) for ref in (q_s, g_s, k_s, v_s)]
                for ref, value in zip((g_s, q_s, k_s, v_s), spatial_block(q, g, k, v, apart)):
                    ref[:, at, :] = value.reshape(4 * elecs, 8, HALF)
            return carry

        lax.fori_loop(0, CHUNKS[c] // 16, block, 0)

    def spatial_end(c):
        here, rows = span(c)
        xi = xr[:, here].reshape(rows, width)
        grads = jnp.concatenate(
            [ref[:, : CHUNKS[c]].astype(BF16).reshape(rows, HALF) for ref in (q_s, k_s, v_s)], axis=1
        )
        dxs[:, here] = mm(grads, w_s[...], NT).astype(BF16).reshape(4 * elecs, CHUNKS[c], width)
        add_in = mm(xi, grads, TN)
        att = g_s[:, : CHUNKS[c]].astype(BF16).reshape(rows, HALF)
        add_out = mm(att, cr[:, here].reshape(rows, width), TN)
        if c == 0:
            acc_in_s[...] = add_in
            acc_out_s[...] = add_out
        else:
            acc_in_s[...] += add_in
            acc_out_s[...] += add_out

    returned = {}

    def send_back(c, steps):
        here, _ = span(c)
        sems = ret_send.at[c, steps[0] % 2], ret_recv.at[c, steps[0] % 2]
        for d in steps:
            push(dxs.at[d * elecs : (d + 1) * elecs, here], dxr.at[d - 1, :, here], sems, peer(y=4 - d))
        returned[c, steps[0] % 2] = group(dxr.at[: len(steps), :, here], sems)

    def place(c):
        here, _ = span(c)
        for i in range(2):
            returned[c, i].wait_recv()
        for d in range(4):
            at = rows_at(lax.rem(y + d, 4) * quarter + STARTS[c], CHUNKS[c])
            if d == 0:
                piece = dxs[:elecs, here]
            else:
                piece = dxr[d - 1, :, here]
            out[:, at, :] = (dx_t[:, at, :] + piece.astype(F32)).astype(BF16)

    def summing(n):
        def sems(p, step):
            return ar_send.at[n, p, step], ar_recv.at[n, p, step]

        def spot_of(p, d=0):
            return ar_out.at[n, p, rows_at(core * 1024 + lax.rem(where[orders[p][0]] + d, 4) * 256, 256)]

        waiting, last = [None, None], [None, None]
        for p in range(2):
            push(ar_src.at[n, p, rows_at((1 - core) * 1024, 1024)], recv_c.at[n, p], sems(p, 0), peer(core=1))
            waiting[p] = group(recv_c.at[n, p], sems(p, 0))
        yield
        for p, (a, b) in enumerate(orders):
            waiting[p].wait_recv()
            part_c[n, p] = (
                ar_src[n, p, rows_at(core * 1024, 1024)].astype(F32) + recv_c[n, p].astype(F32)
            ).astype(BF16)
            for d, by in on_axis(a):
                at = rows_at(lax.rem(where[a] + d, 4) * 256, 256)
                push(part_c.at[n, p, at], recv_a.at[n, p, d - 1], sems(p, 1), peer(**by))
            waiting[p] = group(recv_a.at[n, p], sems(p, 1))
        yield
        for p, (a, b) in enumerate(orders):
            waiting[p].wait_recv()
            total = part_c[n, p, rows_at(where[a] * 256, 256)].astype(F32)
            for i in range(3):
                total = total + recv_a[n, p, i].astype(F32)
            part[n, p] = total.astype(BF16)
            for i, by in on_plane(b):
                at = rows_at((lax.rem(where[b] + by[b], 4) * 4 + lax.rem(y + by["y"], 4)) * 16, 16)
                push(part.at[n, p, at], recv_b.at[n, p, i - 1], sems(p, 2), peer(**by))
            waiting[p] = group(recv_b.at[n, p], sems(p, 2))
        yield
        for p, (a, b) in enumerate(orders):
            waiting[p].wait_recv()
            mine = (where[b] * 4 + y) * 16
            total = part[n, p, rows_at(mine, 16)].astype(F32)
            for i in range(15):
                total = total + recv_b[n, p, i].astype(F32)
            at = rows_at(core * 1024 + where[a] * 256 + mine, 16)
            ar_out[n, p, at] = total.astype(BF16)
            for _, by in on_plane(b):
                push(ar_out.at[n, p, at], ar_out.at[n, p, at], sems(p, 3), peer(**by))
            waiting[p] = group(ar_out.at[n, p, :240], sems(p, 3))
        yield
        for p, (a, b) in enumerate(orders):
            waiting[p].wait_recv()
            for _, by in on_axis(a):
                push(spot_of(p), spot_of(p), sems(p, 4), peer(**by))
            waiting[p] = group(ar_out.at[n, p, :768], sems(p, 4))
            push(spot_of(p), spot_of(p), sems(p, 5), peer(core=1))
        yield
        for p in range(2):
            waiting[p].wait_recv()
            for d in range(1, 4):
                push(spot_of(p, d), spot_of(p, d), sems(p, 5), peer(core=1))
            waiting[p] = group(ar_out.at[n, p, :1024], sems(p, 5))
        yield
        for p in range(2):
            waiting[p].wait_recv()
            first = (1 - n) * HALF + p * 128
            for i in range(3):
                w_outs[i][:, first : first + 128] = ar_out[n, p, i * 512 : (i + 1) * 512]
            for i in range(2):
                low, column = (1 - n) * HALF, i * HALF + p * 128
                w_outs[3][low : low + HALF, column : column + 128] = ar_out[
                    n, p, 1536 + i * HALF : 1536 + (i + 1) * HALF
                ]
        yield

    back_copy.wait_recv()
    acc_in_t[...] = jnp.zeros_like(acc_in_t)
    acc_out_t[...] = jnp.zeros_like(acc_out_t)

    def end_time(e, carry):
        def full(own, side):
            tail = own[e, patches - WIN :] + back_in[side, e].astype(F32)
            return jnp.concatenate([own[e, : patches - WIN].astype(BF16), tail.astype(BF16)], axis=0)

        grads = jnp.concatenate([dq_t[e], full(dk_t, 0), full(dv_t, 1)], axis=1)
        dx_t[e] = mm(grads, w_t[...], NT)
        acc_in_t[...] += mm(xv[e], grads, TN)
        acc_out_t[...] += mm(att_t[e], cv[e], NN)
        return carry

    lax.fori_loop(0, elecs, end_time, 0)
    weight_rows(acc_in_t, acc_out_t, ar_src.at[0])
    time_sum, space_sum = summing(0), summing(1)
    next(time_sum)
    spatial_project(0)
    send_raw(2)
    spatial_attend(0)
    next(time_sum)
    spatial_end(0)
    spatial_project(1)
    next(time_sum)
    spatial_attend(1)
    spatial_end(1)
    spatial_project(2)
    next(time_sum)
    send_back(0, (2,))
    send_back(0, (1, 3))
    spatial_attend(2)
    spatial_end(2)
    weight_rows(acc_in_s, acc_out_s, ar_src.at[1])
    next(space_sum)
    next(time_sum)
    next(space_sum)
    next(time_sum)
    next(space_sum)
    next(space_sum)
    send_back(1, (2,))
    send_back(1, (1, 3))
    send_back(2, (2,))
    send_back(2, (1, 3))
    place(0)
    next(space_sum)
    next(time_sum)
    next(space_sum)
    place(1)
    place(2)
    next(space_sum)
    for whole in pending:
        whole.wait_send()


def end_kernel(dx, g0, g1, g2, g3, out, o0, o1, o2, o3):
    out[...] = dx[...]
    for grad, o in zip((g0, g1, g2, g3), (o0, o1, o2, o3)):
        o[...] = grad[...].astype(F32) * (1.0 / math.sqrt(196608))


def sds(shape, dtype):
    return jax.ShapeDtypeStruct(shape, dtype)


def shards(inputs, cotangent, w_query, w_key, w_value, w_out):
    _, elecs, patches, width = inputs.shape
    quarter = patches // 4
    vm, dma = pltpu.VMEM, pltpu.SemaphoreType.DMA
    tokens = (elecs, patches)
    ext = (elecs, patches + WIN)
    everyone = (4 * elecs, quarter)
    scratch = (
        [vm(tokens + (width,), BF16)] * 2
        + [vm((elecs, WIN, width), BF16)]
        + [vm((width, 3 * HALF), BF16)] * 2
        + [vm((width, width), BF16)]
        + [vm(tokens + (HALF,), BF16), vm(ext + (HALF,), BF16), vm(ext + (HALF,), BF16), vm(tokens + (HALF,), BF16)]
        + [vm(tokens + (HALF,), F32)] * 2
        + [vm((elecs, HALF, patches), BF16), vm(tokens + (HALF,), BF16)]
        + [vm((elecs, HALF, patches + WIN), BF16)] * 2
        + [vm((2, elecs, WIN, HALF), BF16)] * 2
        + [vm(tokens + (width,), F32)]
        + [vm(everyone + (width,), BF16)] * 2
        + [vm((4 * elecs, CHUNKS[0], HALF), F32)] * 4
        + [vm(everyone + (width,), BF16), vm((3, elecs, quarter, width), BF16)]
        + [vm((width, 3 * HALF), F32), vm((HALF, width), F32)] * 2
        + [vm((2, 2, 2048, 128), BF16)]
        + [vm((2, 2, 1024, 128), BF16)] * 2
        + [vm((2, 2, 3, 256, 128), BF16), vm((2, 2, 256, 128), BF16), vm((2, 2, 15, 16, 128), BF16)]
        + [vm((2, 2, 2048, 128), BF16)]
        + [vm((WIN, HEADS * WIN), t) for t in (F32, BF16, BF16, F32)]
        + [dma((11,)), dma((2,)), dma((2,))]
        + [dma((3, 2))] * 2
        + [dma((3, 2))] * 2
        + [dma((2, 2, 6))] * 2
    )
    grad_inputs, *grads = pl.pallas_call(
        layer_kernel,
        out_shape=(sds(tokens + (width,), BF16),) + (sds((width, width), BF16),) * 4,
        in_specs=[pl.BlockSpec(memory_space=pl.ANY)] * 6,
        out_specs=(pl.BlockSpec(memory_space=pltpu.VMEM),) * 5,
        scratch_shapes=scratch,
        compiler_params=pltpu.CompilerParams(
            collective_id=0, has_side_effects=True, vmem_limit_bytes=VMEM_LIMIT
        ),
        cost_estimate=pl.CostEstimate(flops=2 * 10**10, bytes_accessed=10**7, transcendentals=2 * 10**6),
    )(inputs[0], cotangent[0], w_query, w_key, w_value, w_out)
    grad_inputs, *grads = pl.pallas_call(
        end_kernel,
        out_shape=(sds(tokens + (width,), BF16),) + (sds((width, width), F32),) * 4,
        in_specs=[pl.BlockSpec(memory_space=pltpu.VMEM)] * 5,
        out_specs=(pl.BlockSpec(memory_space=pltpu.VMEM),) * 5,
        compiler_params=pltpu.CompilerParams(vmem_limit_bytes=VMEM_LIMIT),
    )(grad_inputs, *grads)
    return (grad_inputs[None],) + tuple(grads)


def solution(mesh):
    return jax.shard_map(
        shards,
        mesh=mesh,
        in_specs=(P("dp", "elec", "tm", None), P("dp", "elec", "tm", None), P(), P(), P(), P()),
        out_specs=(P("dp", "elec", "tm", None), P(), P(), P(), P()),
        check_vma=False,
    )
```

```python
import math

import jax
import jax.numpy as jnp
from jax import lax
from jax.experimental import pallas as pl
from jax.experimental.pallas import tpu as pltpu
from jax.sharding import PartitionSpec as P

BF16 = jnp.bfloat16
F32 = jnp.float32
WIN = 128
HALF = 256
HEAD = 64
HEADS = 4
NEG = -1e30
SCALE = 0.125
VMEM_LIMIT = 56 * 1024 * 1024
MESH = pl.DeviceIdType.MESH

NN = (((1,), (0,)), ((), ()))
NT = (((1,), (1,)), ((), ()))
TN = (((0,), (0,)), ((), ()))


def mm(left, right, dims):
    return lax.dot_general(left, right, dims, preferred_element_type=F32)


def stack_heads(rows):
    column = lax.broadcasted_iota(jnp.int32, (1, HALF), 1)
    keeps = [(column >= h * HEAD) & (column < (h + 1) * HEAD) for h in range(HEADS)]
    return jnp.concatenate([rows * keep.astype(F32).astype(BF16) for keep in keeps], axis=0)


def pick_heads(rows):
    r = rows.shape[0] // HEADS
    even = lax.broadcasted_iota(jnp.int32, (r, 128), 1) < HEAD
    return jnp.concatenate(
        [
            jnp.where(even, rows[:r, :128], rows[r : 2 * r, :128]),
            jnp.where(even, rows[2 * r : 3 * r, 128:], rows[3 * r :, 128:]),
        ],
        axis=1,
    )


def soft(scores, grad_probs):
    ex = jnp.exp(scores - jnp.max(scores, axis=0, keepdims=True))
    probs = ex * (1.0 / jnp.sum(ex, axis=0, keepdims=True))
    delta = jnp.sum(probs * grad_probs, axis=0, keepdims=True)
    return probs.astype(BF16), (probs * (grad_probs - delta)).astype(BF16)


def make_masks(older, older_low, newer_low, apart):
    row = lax.broadcasted_iota(jnp.int32, (WIN, WIN), 0)
    column = lax.broadcasted_iota(jnp.int32, (WIN, WIN), 1)
    old = (row > column).astype(F32)
    far = jnp.where(lax.rem(row, 8) == lax.rem(column, 8), 0.0, NEG).astype(F32)
    for h in range(HEADS):
        at = slice(h * WIN, (h + 1) * WIN)
        older[:, at] = old
        older_low[:, at] = old.astype(BF16)
        newer_low[:, at] = (1.0 - old).astype(BF16)
        apart[:, at] = far


def diagonal(cols):
    return jnp.concatenate(
        [cols[h * HEAD : (h + 1) * HEAD, h * WIN : (h + 1) * WIN] for h in range(HEADS)], axis=0
    )


def temporal_block(q, ga, k, v, k_cols, v_cols, bias, older, older_low, newer_low):
    qs, gs = stack_heads(q), stack_heads(ga)
    st = mm(k, qs, NT)
    gt = mm(v, gs, NT)
    old = older[...] > 0.5
    early = st[:WIN] if bias is None else st[:WIN] + bias
    probs, grad = soft(jnp.where(old, early, st[WIN:]), jnp.where(old, gt[:WIN], gt[WIN:]))
    pt = jnp.concatenate([probs * older_low[...], probs * newer_low[...]], axis=0)
    dt = jnp.concatenate([grad * older_low[...], grad * newer_low[...]], axis=0)
    att = diagonal(mm(v_cols, pt, NN)).astype(BF16)
    dq = (diagonal(mm(k_cols, dt, NN)) * SCALE).astype(BF16)
    return att, dq.T, mm(dt, qs, NN), mm(pt, gs, NN)


def spatial_block(q, ga, k, v, apart):
    qs, gs = stack_heads(q), stack_heads(ga)
    pt, dt = soft(mm(k, qs, NT) + apart[...], mm(v, gs, NT))
    att = pick_heads(mm(pt, v, TN))
    dq = pick_heads(mm(dt, k, TN)) * SCALE
    return att, dq, mm(dt, qs, NN), mm(pt, gs, NN)


def coordinates():
    dp, tm, y = lax.axis_index("dp"), lax.axis_index("tm"), lax.axis_index("elec")
    z, rest = lax.div(tm, 4), lax.rem(tm, 4)
    x = lax.div(rest, 2) * 2 + dp
    return x, y, z, lax.rem(rest, 2)


def device_at(x, y, z, core):
    return {"dp": lax.rem(x, 2), "tm": z * 4 + lax.div(x, 2) * 2 + core, "elec": y}


CHUNKS = (48, 32, 16)
STARTS = (0, 48, 80)


def weight_rows(acc_in, acc_out, dst):
    for j in range(2):
        for i in range(3):
            first = i * HALF + j * 128
            dst[j, i * 512 : (i + 1) * 512] = acc_in[:, first : first + 128].astype(BF16)
        for i in range(2):
            first = i * HALF + j * 128
            dst[j, 1536 + i * HALF : 1536 + (i + 1) * HALF] = acc_out[:, first : first + 128].astype(BF16)


def layer_kernel(x_h, cot_h, wq_h, wk_h, wv_h, wo_h, out, *rest):
    w_outs = rest[:4]
    (
        xv, cv, halo, w_t, w_s, wo, q_t, k_t, v_t, g_t, dk_t, dv_t, att_t, dq_t, kc_t, vc_t, back_out, back_in, dx_t,
        xr, cr, q_s, k_s, v_s, g_s, dxs, dxr, acc_in_t, acc_out_t, acc_in_s, acc_out_s,
        ar_src, recv_a, part, recv_b, ar_out, older, older_low, newer_low, apart,
        load_sem, halo_send, halo_recv, go_send, go_recv, ret_send, ret_recv, ar_send, ar_recv,
    ) = rest[4:]
    elecs, patches, width = xv.shape
    quarter = patches // 4
    x, y, z, core = coordinates()
    tm = lax.axis_index("tm")
    right = {"tm": lax.rem(tm + 1, 16)}
    left = {"tm": lax.rem(tm + 15, 16)}
    where = {"x": x, "y": y, "z": z, "core": core}

    def peer(**by):
        at = {n: lax.rem(where[n] + by.get(n, 0), 2 if n == "core" else 4) for n in where}
        return device_at(at["x"], at["y"], at["z"], at["core"])

    orders = ((("x", "core"), ("z", "y")), (("z", "core"), ("x", "y")))

    def others(axes):
        low = 2 if axes[1] == "core" else 4
        return [(i, {axes[0]: i // low, axes[1]: i % low}) for i in range(1, 4 * low)]

    loads = []

    def load(src, dst):
        copy = pltpu.make_async_copy(src, dst, load_sem.at[len(loads)])
        copy.start()
        loads.append(copy)

    load(x_h, xv)
    load(cot_h, cv)
    load(wo_h, wo)
    for i, w in enumerate((wq_h, wk_h, wv_h)):
        load(w.at[:, HALF:], w_t.at[:, i * HALF : (i + 1) * HALF])
    for i, w in enumerate((wq_h, wk_h, wv_h)):
        load(w.at[:, :HALF], w_s.at[:, i * HALF : (i + 1) * HALF])
    at = pl.ds(pl.multiple_of(y * quarter, 16), quarter)
    load(x_h.at[:, at], xr.at[:elecs])
    load(cot_h.at[:, at], cr.at[:elecs])
    near = {tuple(sorted(by.items())) for axes in (orders[0] + orders[1]) for _, by in others(axes)}
    near = sorted({tuple((n, v) for n, v in by if v) for by in near})
    barrier = pltpu.get_barrier_semaphore()
    for device in [right, left] + [peer(**dict(by)) for by in near]:
        pl.semaphore_signal(barrier, inc=1, device_id=device, device_id_type=MESH)
    pl.semaphore_wait(barrier, 2 + len(near))

    pending = []

    def push(src, dst, sems, device):
        pltpu.make_async_remote_copy(
            src_ref=src, dst_ref=dst, send_sem=sems[0], recv_sem=sems[1], device_id=device, device_id_type=MESH
        ).start()

    def group(ref, sems):
        whole = pltpu.make_async_remote_copy(
            src_ref=ref, dst_ref=ref, send_sem=sems[0], recv_sem=sems[1], device_id=right, device_id_type=MESH
        )
        pending.append(whole)
        return whole

    def rows_at(first, size):
        return pl.ds(pl.multiple_of(first, 16), size)

    loads[0].wait()
    loads[1].wait()
    halo_sems = halo_send.at[0], halo_recv.at[0]
    push(xv.at[:, patches - WIN :], halo, halo_sems, right)
    halo_copy = group(halo, halo_sems)
    go = {}

    def send_raw(c):
        here = slice(STARTS[c], STARTS[c] + CHUNKS[c])
        for k, (src, dst) in enumerate(((xv, xr), (cv, cr))):
            sems = go_send.at[c, k], go_recv.at[c, k]
            for d in (2, 1, 3):
                at = rows_at(lax.rem(y + d, 4) * quarter + STARTS[c], CHUNKS[c])
                push(src.at[:, at], dst.at[d * elecs : (d + 1) * elecs, here], sems, peer(y=d))
            go[c, k] = group(dst.at[elecs:, here], sems)

    send_raw(0)
    masks = older, older_low, newer_low
    make_masks(*masks, apart)
    for copy in loads[2:]:
        copy.wait()

    bias0 = jnp.where(tm == 0, NEG, 0.0).astype(F32)

    def project_time(e, carry):
        q_t[e] = (mm(xv[e], w_t[:, :HALF], NN) * SCALE).astype(BF16)
        for own, cols, i in ((k_t, kc_t, 1), (v_t, vc_t, 2)):
            t = mm(xv[e], w_t[:, i * HALF : (i + 1) * HALF], NN).astype(BF16)
            own[e, WIN:] = t
            cols[e, :, WIN:] = t.T
        g_t[e] = mm(cv[e], wo[HALF:, :], NT).astype(BF16)
        return carry

    lax.fori_loop(0, elecs, project_time, 0)

    def time_block(e, c, bias):
        rows, keys = slice(c * WIN, (c + 1) * WIN), slice(c * WIN, (c + 2) * WIN)
        att, dq, dk, dv = temporal_block(
            q_t[e, rows], g_t[e, rows], k_t[e, keys], v_t[e, keys], kc_t[e, :, keys], vc_t[e, :, keys], bias, *masks
        )
        att_t[e, :, rows] = att
        dq_t[e, rows] = dq
        return dk, dv

    def later_blocks(e, first_done):
        ones = time_block(e, 1, None)
        twos = time_block(e, 2, None)
        for ref, one, two in zip((dk_t, dv_t), ones, twos):
            if first_done:
                ref[e, :WIN] += one[:WIN]
            else:
                ref[e, :WIN] = one[:WIN]
            ref[e, WIN : 2 * WIN] = one[WIN:] + two[:WIN]
            ref[e, 2 * WIN :] = two[WIN:]

    def first_block(e, first_done):
        for own, cols, i in ((k_t, kc_t, 1), (v_t, vc_t, 2)):
            t = mm(halo[e], w_t[:, i * HALF : (i + 1) * HALF], NN).astype(BF16)
            own[e, :WIN] = t
            cols[e, :, :WIN] = t.T
        for side, (ref, grad) in enumerate(zip((dk_t, dv_t), time_block(e, 0, bias0))):
            back_out[side, e] = grad[:WIN].astype(BF16)
            if first_done:
                ref[e, :WIN] = grad[WIN:]
            else:
                ref[e, :WIN] += grad[WIN:]

    def first_pair(i, carry):
        first_block(2 + 2 * i, True)
        first_block(3 + 2 * i, True)
        return carry

    def later_one(e, carry):
        later_blocks(e, True)
        return carry

    later_blocks(0, False)
    later_blocks(1, False)
    halo_copy.wait_recv()
    first_block(0, False)
    first_block(1, False)
    lax.fori_loop(0, elecs // 2 - 1, first_pair, 0)
    back_sems = halo_send.at[1], halo_recv.at[1]
    push(back_out, back_in, back_sems, left)
    back_copy = group(back_in, back_sems)
    lax.fori_loop(2, elecs, later_one, 0)
    send_raw(1)

    def span(c):
        return slice(STARTS[c], STARTS[c] + CHUNKS[c]), 4 * elecs * CHUNKS[c]

    def spatial_project(c):
        for k in range(2):
            go[c, k].wait_recv()
        here, rows = span(c)
        xi = xr[:, here].reshape(rows, width)
        shape = (4 * elecs, CHUNKS[c], HALF)
        q_s[:, : CHUNKS[c]] = (mm(xi, w_s[:, :HALF], NN) * SCALE).reshape(shape)
        k_s[:, : CHUNKS[c]] = mm(xi, w_s[:, HALF : 2 * HALF], NN).reshape(shape)
        v_s[:, : CHUNKS[c]] = mm(xi, w_s[:, 2 * HALF :], NN).reshape(shape)
        g_s[:, : CHUNKS[c]] = mm(cr[:, here].reshape(rows, width), wo[:HALF, :], NT).reshape(shape)

    def spatial_attend(c):
        def block(i, carry):
            for j in range(2):
                at = pl.ds(pl.multiple_of(i * 16 + j * 8, 8), 8)
                q, g, k, v = [ref[:, at, :].reshape(WIN, HALF).astype(BF16) for ref in (q_s, g_s, k_s, v_s)]
                for ref, value in zip((g_s, q_s, k_s, v_s), spatial_block(q, g, k, v, apart)):
                    ref[:, at, :] = value.reshape(4 * elecs, 8, HALF)
            return carry

        lax.fori_loop(0, CHUNKS[c] // 16, block, 0)

    def spatial_end(c):
        here, rows = span(c)
        xi = xr[:, here].reshape(rows, width)
        grads = jnp.concatenate(
            [ref[:, : CHUNKS[c]].astype(BF16).reshape(rows, HALF) for ref in (q_s, k_s, v_s)], axis=1
        )
        dxs[:, here] = mm(grads, w_s[...], NT).astype(BF16).reshape(4 * elecs, CHUNKS[c], width)
        add_in = mm(xi, grads, TN)
        att = g_s[:, : CHUNKS[c]].astype(BF16).reshape(rows, HALF)
        add_out = mm(att, cr[:, here].reshape(rows, width), TN)
        if c == 0:
            acc_in_s[...] = add_in
            acc_out_s[...] = add_out
        else:
            acc_in_s[...] += add_in
            acc_out_s[...] += add_out

    returned = {}

    def send_back(c):
        here, _ = span(c)
        sems = ret_send.at[c], ret_recv.at[c]
        for d in (2, 1, 3):
            push(dxs.at[d * elecs : (d + 1) * elecs, here], dxr.at[d - 1, :, here], sems, peer(y=4 - d))
        returned[c] = group(dxr.at[:, :, here], sems)

    def place(c):
        here, _ = span(c)
        returned[c].wait_recv()
        for d in range(4):
            at = rows_at(lax.rem(y + d, 4) * quarter + STARTS[c], CHUNKS[c])
            if d == 0:
                piece = dxs[:elecs, here]
            else:
                piece = dxr[d - 1, :, here]
            out[:, at, :] = (dx_t[:, at, :] + piece.astype(F32)).astype(BF16)

    def summing(n):
        def exchange(p, step, axes, copies, whole):
            sems = ar_send.at[n, p, step], ar_recv.at[n, p, step]
            for i, by in others(axes):
                push(*copies(i, by), sems, peer(**by))
            return group(whole, sems)

        def own(axes, **by):
            at = [lax.rem(where[a] + by.get(a, 0), 2 if a == "core" else 4) for a in axes]
            return at[0] * (2 if axes[1] == "core" else 4) + at[1]

        waiting = [None, None]
        for p in range(2):
            axes = orders[p][0]
            waiting[p] = exchange(
                p,
                0,
                axes,
                lambda i, by: (ar_src.at[n, p, rows_at(own(axes, **by) * 256, 256)], recv_a.at[n, p, i - 1]),
                recv_a.at[n, p],
            )
        yield
        for p in range(2):
            waiting[p].wait_recv()
            total = ar_src[n, p, rows_at(own(orders[p][0]) * 256, 256)].astype(F32)
            for i in range(7):
                total = total + recv_a[n, p, i].astype(F32)
            part[n, p] = total.astype(BF16)
            axes = orders[p][1]
            waiting[p] = exchange(
                p,
                1,
                axes,
                lambda i, by: (part.at[n, p, rows_at(own(axes, **by) * 16, 16)], recv_b.at[n, p, i - 1]),
                recv_b.at[n, p],
            )
        yield
        for p in range(2):
            waiting[p].wait_recv()
            axes = orders[p][1]
            total = part[n, p, rows_at(own(axes) * 16, 16)].astype(F32)
            for i in range(15):
                total = total + recv_b[n, p, i].astype(F32)
            at = rows_at(own(orders[p][0]) * 256 + own(axes) * 16, 16)
            ar_out[n, p, at] = total.astype(BF16)
            spot = ar_out.at[n, p, at]
            waiting[p] = exchange(p, 2, axes, lambda i, by: (spot, spot), ar_out.at[n, p, :240])
        yield
        for p in range(2):
            waiting[p].wait_recv()
            axes = orders[p][0]
            spot = ar_out.at[n, p, rows_at(own(axes) * 256, 256)]
            waiting[p] = exchange(p, 3, axes, lambda i, by: (spot, spot), ar_out.at[n, p, :1792])
        yield
        for p in range(2):
            waiting[p].wait_recv()
            first = (1 - n) * HALF + p * 128
            for i in range(3):
                w_outs[i][:, first : first + 128] = ar_out[n, p, i * 512 : (i + 1) * 512]
            for i in range(2):
                low, column = (1 - n) * HALF, i * HALF + p * 128
                w_outs[3][low : low + HALF, column : column + 128] = ar_out[
                    n, p, 1536 + i * HALF : 1536 + (i + 1) * HALF
                ]
        yield

    back_copy.wait_recv()
    acc_in_t[...] = jnp.zeros_like(acc_in_t)
    acc_out_t[...] = jnp.zeros_like(acc_out_t)

    def end_time(e, carry):
        def full(own, side):
            tail = own[e, patches - WIN :] + back_in[side, e].astype(F32)
            return jnp.concatenate([own[e, : patches - WIN].astype(BF16), tail.astype(BF16)], axis=0)

        grads = jnp.concatenate([dq_t[e], full(dk_t, 0), full(dv_t, 1)], axis=1)
        dx_t[e] = mm(grads, w_t[...], NT)
        acc_in_t[...] += mm(xv[e], grads, TN)
        acc_out_t[...] += mm(att_t[e], cv[e], NN)
        return carry

    lax.fori_loop(0, elecs, end_time, 0)
    weight_rows(acc_in_t, acc_out_t, ar_src.at[0])
    time_sum, space_sum = summing(0), summing(1)
    next(time_sum)
    send_raw(2)
    spatial_project(0)
    spatial_attend(0)
    next(time_sum)
    spatial_end(0)
    spatial_project(1)
    spatial_attend(1)
    spatial_end(1)
    spatial_project(2)
    next(time_sum)
    send_back(0)
    spatial_attend(2)
    spatial_end(2)
    weight_rows(acc_in_s, acc_out_s, ar_src.at[1])
    next(space_sum)
    next(time_sum)
    send_back(2)
    next(space_sum)
    place(0)
    next(space_sum)
    send_back(1)
    next(time_sum)
    place(2)
    next(space_sum)
    place(1)
    next(space_sum)
    for whole in pending:
        whole.wait_send()


def end_kernel(*refs):
    sources, outs = refs[:5], refs[5:10]
    dx_v, grads_v, outs_v, in_sem, out_sem = refs[10:]
    reads = [grads_v.at[i] for i in range(4)] + [dx_v]
    writes = [outs_v.at[i] for i in range(4)] + [dx_v]
    ins = [pltpu.make_async_copy(sources[i], reads[i], in_sem.at[i]) for i in range(5)]
    for copy in ins:
        copy.start()
    back = [pltpu.make_async_copy(writes[i], outs[i], out_sem.at[i]) for i in range(5)]
    for i in range(5):
        ins[i].wait()
        if i < 4:
            outs_v[i] = grads_v[i].astype(F32) * (1.0 / math.sqrt(196608))
        back[i].start()
    for copy in back:
        copy.wait()


def sds(shape, dtype):
    return jax.ShapeDtypeStruct(shape, dtype)


def shards(inputs, cotangent, w_query, w_key, w_value, w_out):
    _, elecs, patches, width = inputs.shape
    quarter = patches // 4
    vm, dma = pltpu.VMEM, pltpu.SemaphoreType.DMA
    tokens = (elecs, patches)
    ext = (elecs, patches + WIN)
    everyone = (4 * elecs, quarter)
    scratch = (
        [vm(tokens + (width,), BF16)] * 2
        + [vm((elecs, WIN, width), BF16)]
        + [vm((width, 3 * HALF), BF16)] * 2
        + [vm((width, width), BF16)]
        + [vm(tokens + (HALF,), BF16), vm(ext + (HALF,), BF16), vm(ext + (HALF,), BF16), vm(tokens + (HALF,), BF16)]
        + [vm(tokens + (HALF,), F32)] * 2
        + [vm((elecs, HALF, patches), BF16), vm(tokens + (HALF,), BF16)]
        + [vm((elecs, HALF, patches + WIN), BF16)] * 2
        + [vm((2, elecs, WIN, HALF), BF16)] * 2
        + [vm(tokens + (width,), F32)]
        + [vm(everyone + (width,), BF16)] * 2
        + [vm((4 * elecs, CHUNKS[0], HALF), F32)] * 4
        + [vm(everyone + (width,), BF16), vm((3, elecs, quarter, width), BF16)]
        + [vm((width, 3 * HALF), F32), vm((HALF, width), F32)] * 2
        + [vm((2, 2, 2048, 128), BF16)]
        + [vm((2, 2, 7, 256, 128), BF16), vm((2, 2, 256, 128), BF16), vm((2, 2, 15, 16, 128), BF16)]
        + [vm((2, 2, 2048, 128), BF16)]
        + [vm((WIN, HEADS * WIN), t) for t in (F32, BF16, BF16, F32)]
        + [dma((11,)), dma((2,)), dma((2,))]
        + [dma((3, 2))] * 2
        + [dma((3,))] * 2
        + [dma((2, 2, 4))] * 2
    )
    grad_inputs, *grads = pl.pallas_call(
        layer_kernel,
        out_shape=(sds(tokens + (width,), BF16),) + (sds((width, width), BF16),) * 4,
        in_specs=[pl.BlockSpec(memory_space=pl.ANY)] * 6,
        out_specs=(pl.BlockSpec(memory_space=pltpu.VMEM),) * 5,
        scratch_shapes=scratch,
        compiler_params=pltpu.CompilerParams(
            collective_id=0, has_side_effects=True, vmem_limit_bytes=VMEM_LIMIT
        ),
        cost_estimate=pl.CostEstimate(flops=2 * 10**10, bytes_accessed=10**7, transcendentals=2 * 10**6),
    )(inputs[0], cotangent[0], w_query, w_key, w_value, w_out)
    hbm = pl.BlockSpec(memory_space=pl.ANY)
    *grads, grad_inputs = pl.pallas_call(
        end_kernel,
        out_shape=(sds((width, width), F32),) * 4 + (sds(tokens + (width,), BF16),),
        in_specs=[hbm] * 5,
        out_specs=(hbm,) * 5,
        scratch_shapes=[
            vm(tokens + (width,), BF16),
            vm((4, width, width), BF16),
            vm((4, width, width), F32),
            dma((5,)),
            dma((5,)),
        ],
        compiler_params=pltpu.CompilerParams(vmem_limit_bytes=VMEM_LIMIT),
    )(*grads, grad_inputs)
    return (grad_inputs[None],) + tuple(grads)


def solution(mesh):
    return jax.shard_map(
        shards,
        mesh=mesh,
        in_specs=(P("dp", "elec", "tm", None), P("dp", "elec", "tm", None), P(), P(), P(), P()),
        out_specs=(P("dp", "elec", "tm", None), P(), P(), P(), P()),
        check_vma=False,
    )
```
